32 devices in a mesh: layer: 4 (over z), row: 4 (over x, core), col: 2 (over y).
Axes of the slice: x: 2, y: 2, z: 4, core: 2. Of those that a mesh axis runs over, the one named last changes fastest.
Arguments:
- c_states: float32 [4, 64, 32, 256], P('layer', None, 'row', 'col'), may hold values from -6 to 6
- c_adjoints: float32 [4, 64, 32, 256], P('layer', None, 'row', 'col'), may hold values from -6 to 6
- weights: bfloat16 [16, 64, 576], P('layer'), may hold values from -0.25 to 0.25
Outputs:
- new_states: float32 [4, 64, 32, 256], P('layer', None, 'row', 'col')
- new_adjoints: float32 [4, 64, 32, 256], P('layer', None, 'row', 'col')
- weight_grads: float32 [16, 64, 576], P('layer')
The draws below stay inside these ranges and needn't reach their ends.
All inputs are finite; a program needn't handle non-finite values.
Results may differ from the reference program's by a relative error of at most 0.006.
Values may be sent and summed in bfloat16 or wider, within the bound.
No kernel may reach another device: no remote copies, remote signals or barrier semaphores. Data moves between devices by JAX's collectives and lax.ppermute only.
A program may use at most 64 MiB of HBM per device.

```python
import jax
import jax.numpy as jnp
from jax import lax

CH = 64
LG = 4
GROUPS = 4
LAYERS = 16
HH = 32
WW = 256


def block_scale(rng, shape, pieces, low, largest):
    def one(dim, parts):
        heights = jax.random.uniform(jax.random.fold_in(jax.random.fold_in(rng, 6), dim), (parts,), jnp.float32, low / len(pieces), largest / len(pieces))
        return jnp.repeat(jnp.exp(heights), shape[dim] // parts).reshape((-1,) + (1,) * (len(shape) - dim - 1))

    gain = one(*pieces[0])
    for cut in pieces[1:]:
        gain = gain * one(*cut)
    return gain


def bell_draw(own_key, shape, spread, bound, pieces=(), kind=jnp.bfloat16):
    values = jax.random.normal(own_key, shape, jnp.float32) * spread
    if len(pieces) > 0:
        values = block_scale(own_key, shape, pieces, -0.22, 0.18) * values
    return jnp.clip(values, min=-bound, max=bound).astype(kind)


def setup_inputs(seed: int = 0) -> dict:
    key_of = jax.random.split(jax.random.key(seed), 4)
    return {
        "c_states": bell_draw(key_of[0], (GROUPS, CH, HH, WW), 1.0, 6.0, ((0, 4), (2, 4), (3, 2)), jnp.float32),
        "c_adjoints": bell_draw(key_of[1], (GROUPS, CH, HH, WW), 1.0, 6.0, ((0, 4), (2, 4), (3, 2)), jnp.float32),
        "weights": bell_draw(key_of[2], (LAYERS, CH, 9 * CH), (9 * CH) ** -0.5, 0.25, ((0, 4),)),
    }


step_size = 0.2


def patches(image):
    padded = jnp.pad(image, ((0, 0), (1, 1), (1, 1)))
    height = image.shape[1]
    width = image.shape[2]
    shifted = [padded[:, row_off:row_off + height, col_off:col_off + width] for row_off in range(3) for col_off in range(3)]
    return jnp.stack(shifted, 0).reshape(9 * image.shape[0], height * width)


def flipped(weight_mat):
    channels = weight_mat.shape[0]
    return jnp.transpose(weight_mat.reshape(channels, 9, channels)[:, ::-1, :], (2, 1, 0)).reshape(channels, 9 * channels)


def exact_dot(left_mat, right_mat):
    return jnp.dot(left_mat, right_mat, precision=lax.Precision.HIGHEST, preferred_element_type=jnp.float32)


def advance(state, weight_mat):
    active = state.astype(jnp.bfloat16)
    preact = jnp.dot(weight_mat, patches(active), preferred_element_type=jnp.float32).reshape(state.shape)
    return state + step_size * jnp.tanh(preact), active, preact


def reference(c_states, c_adjoints, weights):
    group_count = c_states.shape[0]
    channels = c_states.shape[1]
    shape = c_states.shape[1:]
    coarse = []
    group_end = []
    for group in range(group_count):
        state = c_states[group]
        for layer_pos in range(LG):
            state, _, _ = advance(state, weights[group * LG + layer_pos])
        group_end.append(state.reshape(channels, -1))
        summed = jnp.sum(weights[group * LG].astype(jnp.float32).reshape(channels, 9, channels), axis=1)
        coarse.append(jnp.eye(channels, dtype=jnp.float32) + step_size * summed)
    corrected = [c_states[0].reshape(channels, -1), group_end[0]]
    for group in range(1, group_count - 1):
        offset = group_end[group] - exact_dot(coarse[group], c_states[group].reshape(channels, -1))
        corrected.append(exact_dot(coarse[group], corrected[group]) + offset)
    grad_list = [None] * (group_count * LG)
    relaxed = []
    for group in range(group_count):
        state = corrected[group].reshape(shape)
        trail = []
        for layer_pos in range(LG):
            state, active, preact = advance(state, weights[group * LG + layer_pos])
            trail.append((active, preact))
        adjoint = c_adjoints[group]
        for layer_pos in reversed(range(LG)):
            active, preact = trail[layer_pos]
            slope = jnp.tanh(preact)
            source = (adjoint * step_size * (1.0 - slope * slope)).astype(jnp.bfloat16)
            grad_list[group * LG + layer_pos] = lax.dot_general(source.reshape(channels, -1), patches(active), (((1,), (1,)), ((), ())), preferred_element_type=jnp.float32)
            back = jnp.dot(flipped(weights[group * LG + layer_pos]), patches(source), preferred_element_type=jnp.float32)
            adjoint = adjoint + back.reshape(shape)
        relaxed.append(adjoint.reshape(channels, -1))
    lam = [None] * group_count
    lam[group_count - 1] = c_adjoints[group_count - 1].reshape(channels, -1)
    lam[group_count - 2] = relaxed[group_count - 1]
    for group in range(group_count - 2, 0, -1):
        transposed = coarse[group].T
        offset = relaxed[group] - exact_dot(transposed, c_adjoints[group].reshape(channels, -1))
        lam[group - 1] = exact_dot(transposed, lam[group]) + offset
    new_states = jnp.stack([item.reshape(shape) for item in corrected], 0)
    new_adjoints = jnp.stack([item.reshape(shape) for item in lam], 0)
    return new_states, new_adjoints, jnp.stack(grad_list, 0)
```

```python
import functools

import jax
import jax.numpy as jnp
from jax import lax
from jax.experimental import pallas as pl
from jax.experimental.pallas import tpu as pltpu
from jax.sharding import PartitionSpec as P

step_size = 0.2
EDGE = 8
VMEM_BYTES = 40 * 1024 * 1024
f32 = jnp.float32
bf16 = jnp.bfloat16


def call(body, out_shape, scratch=(), flops=0, moved=0):
    return pl.pallas_call(
        body,
        out_shape=out_shape,
        scratch_shapes=list(scratch),
        cost_estimate=pl.CostEstimate(
            flops=int(flops), bytes_accessed=int(moved), transcendentals=0
        ),
        compiler_params=pltpu.CompilerParams(vmem_limit_bytes=VMEM_BYTES),
    )


def row_of(ref, row, channels, rows):
    return ref[pl.ds(row, channels, stride=rows), :]


def lanes_of(shape):
    return lax.broadcasted_iota(jnp.int32, shape, 1)


def fold_edges(rows_list):
    shape = rows_list[0].shape
    slot = lanes_of(shape) // (2 * EDGE)
    total = jnp.zeros(shape, f32)
    for place, row in enumerate(rows_list):
        turned = pltpu.roll(row, (2 * EDGE * place + EDGE) % shape[1], 1)
        total = jnp.where(slot == place, turned, total)
    return total


def join_edges(from_left, from_right, has_left, has_right):
    lanes = lanes_of(from_left.shape)
    return jnp.where(
        lanes % (2 * EDGE) >= EDGE,
        from_right.astype(f32) * has_right,
        from_left.astype(f32) * has_left,
    )


def side_lanes(joined, place):
    cols = joined.shape[1]
    return pltpu.roll(joined, (cols - (2 * EDGE * place + EDGE)) % cols, 1)


def convolved(weights, slab):
    channels = slab.shape[1]
    lanes = slab.shape[2]
    product = jnp.dot(
        weights, slab.reshape(3 * channels, lanes), preferred_element_type=f32
    )
    return (
        pltpu.roll(product[:channels], 1, 1)
        + product[channels : 2 * channels]
        + pltpu.roll(product[2 * channels :], lanes - 1, 1)
    )


def flags():
    row, col = lax.axis_index("row"), lax.axis_index("col")
    up = (row > 0).astype(f32)
    down = (row < lax.axis_size("row") - 1).astype(f32)
    left = (col > 0).astype(f32)
    right = (col < lax.axis_size("col") - 1).astype(f32)
    return up, down, left, right


def lane_mask(cols, left, right):
    lanes = lax.broadcasted_iota(jnp.int32, (1, 2 * cols), 1)
    return jnp.where(lanes < cols, 1.0, jnp.where(lanes < cols + cols // 2, right, left))


def pack_body(c_ref, q_ref, top_ref, bottom_ref, edge_ref, *, channels, rows, depth):
    for which, ref in enumerate((c_ref, q_ref)):
        image = [row_of(ref, row, channels, rows) for row in range(rows)]
        for row in range(depth):
            top_ref[which * depth + row] = image[row].astype(bf16)
            bottom_ref[which * depth + row] = image[rows - depth + row].astype(bf16)
        edge_ref[which] = fold_edges(image).astype(bf16)


def load_halo(dest, first, side_ref, count, halo, joined, offset):
    for row in range(count):
        dest(
            first + row,
            halo[row].astype(f32),
            side_lanes(joined, offset + row),
        )


def layer_rows(low, high, body):
    def two(turn, carry):
        body(low + 2 * turn)
        body(low + 2 * turn + 1)
        return carry

    lax.fori_loop(0, (high - low) // 2, two, 0)


def row_flag(index, halo, rows, up, down):
    return jnp.where(index < halo, up, jnp.where(index >= halo + rows, down, 1.0))


def first_body(
    c_ref, above_ref, below_ref, left_ref, right_ref, w_ref, f_ref, fb_ref, x_ref, a_ref,
    *, channels, rows, depth,
):
    cols = c_ref.shape[1]
    up, down, left, right = flags()
    mask = lane_mask(cols, left, right)
    halo = depth

    def put(index, own, beyond):
        x_ref[index, :, :cols] = own
        x_ref[index, :, cols:] = beyond
        a_ref[0, index, :, :cols] = own.astype(bf16)
        a_ref[0, index, :, cols:] = beyond.astype(bf16)

    joined = [join_edges(left_ref[j], right_ref[j], left, right) for j in range(3)]
    for row in range(rows):
        put(halo + row, row_of(c_ref, row, channels, rows), side_lanes(joined[1], row))
    for row in range(depth):
        put(row, above_ref[row].astype(f32), side_lanes(joined[0], rows - depth + row))
        put(halo + rows + row, below_ref[row].astype(f32), side_lanes(joined[2], row))

    total = rows + 2 * halo
    for layer in range(depth):
        now, later = layer % 2, (layer + 1) % 2

        def step(index, layer=layer, now=now, later=later):
            z = convolved(w_ref[layer], a_ref[now, pl.ds(index - 1, 3)])
            gain = mask * (step_size * row_flag(index, halo, rows, up, down))
            x = x_ref[index] + gain * jnp.tanh(z)
            x_ref[index] = x
            a_ref[later, index] = x.astype(bf16)

        layer_rows(layer + 1, total - layer - 1, step)
    for row in range(rows):
        value = x_ref[halo + row, :, :cols]
        f_ref[row] = value
        fb_ref[row] = value.astype(bf16)


def hop_body(s_ref, c_ref, f_ref, m_ref, out_ref, *, channels, rows):
    for row in range(rows):
        e = s_ref[row].astype(f32) - row_of(c_ref, row, channels, rows)
        high = e.astype(bf16)
        low = (e - high.astype(f32)).astype(bf16)
        stacked = jnp.concatenate([high, high, low], 0)
        moved = jnp.dot(m_ref[...], stacked, preferred_element_type=f32)
        out_ref[row] = (f_ref[row] + e + moved).astype(bf16)


def settle_body(*refs, channels, rows):
    c_ref, arrived, s_ref, edge_ref = refs[0], refs[1:-2], refs[-2], refs[-1]
    first = lax.axis_index("layer") == 0
    image = []
    for row in range(rows):
        value = sum(ref[row].astype(f32) for ref in arrived)
        value = jnp.where(first, row_of(c_ref, row, channels, rows), value)
        s_ref[row] = value.astype(bf16)
        image.append(value)
    edge_ref[0] = fold_edges(image).astype(bf16)


def second_body(
    c_ref, q_ref, s_ref, s_above_ref, s_below_ref, s_left_ref, s_right_ref,
    q_above_ref, q_below_ref, q_left_ref, q_right_ref, w_ref, wt_ref,
    state_ref, g_ref, gb_ref, grad_ref,
    x_ref, a_ref, keep_ref, slope_ref, adj_ref, src_ref,
    *, channels, rows, depth,
):
    cols = c_ref.shape[1]
    up, down, left, right = flags()
    mask = lane_mask(cols, left, right)
    halo = 2 * depth
    total = rows + 2 * halo
    first = lax.axis_index("layer") == 0

    def put(index, own, beyond):
        x_ref[index, :, :cols] = own
        x_ref[index, :, cols:] = beyond
        a_ref[0, index, :, :cols] = own.astype(bf16)
        a_ref[0, index, :, cols:] = beyond.astype(bf16)

    joined = [join_edges(s_left_ref[j], s_right_ref[j], left, right) for j in range(3)]
    for row in range(rows):
        own = jnp.where(first, row_of(c_ref, row, channels, rows), s_ref[row].astype(f32))
        state_ref[pl.ds(row, channels, stride=rows), :] = own
        put(halo + row, own, side_lanes(joined[1], row))
    for row in range(halo):
        put(row, s_above_ref[rows - halo + row].astype(f32), side_lanes(joined[0], rows - halo + row))
        put(halo + rows + row, s_below_ref[row].astype(f32), side_lanes(joined[2], row))

    def put_adj(index, own, beyond):
        adj_ref[index, :, :cols] = own
        adj_ref[index, :, cols:] = beyond

    joined = [join_edges(q_left_ref[j], q_right_ref[j], left, right) for j in range(3)]
    for row in range(rows):
        put_adj(halo + row, row_of(q_ref, row, channels, rows), side_lanes(joined[1], row))
    for row in range(depth):
        put_adj(halo - depth + row, q_above_ref[row].astype(f32), side_lanes(joined[0], rows - depth + row))
        put_adj(halo + rows + row, q_below_ref[row].astype(f32), side_lanes(joined[2], row))

    def keep(layer):
        for row in range(rows):
            x = x_ref[halo + row]
            lanes = 2 * cols
            keep_ref[layer, :, pl.ds(row * cols, cols)] = jnp.concatenate(
                [
                    pltpu.roll(x, 1, 1)[:, :cols],
                    x[:, :cols],
                    pltpu.roll(x, lanes - 1, 1)[:, :cols],
                ],
                0,
            ).astype(bf16)

    for layer in range(depth):
        now, later = layer % 2, (layer + 1) % 2
        keep(layer)

        def step(index, layer=layer, now=now, later=later):
            z = convolved(w_ref[layer], a_ref[now, pl.ds(index - 1, 3)])
            gain = mask * (step_size * row_flag(index, halo, rows, up, down))
            t = jnp.tanh(z)
            slope_ref[layer, index] = gain * (1.0 - t * t)
            if layer < depth - 1:
                x = x_ref[index] + gain * t
                x_ref[index] = x
                a_ref[later, index] = x.astype(bf16)

        layer_rows(layer + 1, total - layer - 1, step)

    for layer in reversed(range(depth)):
        reach = layer + 1

        def source(index, layer=layer):
            src_ref[index] = (adj_ref[index] * slope_ref[layer, index]).astype(bf16)

        layer_rows(halo - reach, halo + rows + reach, source)

        def back(index, layer=layer):
            adj_ref[index] += convolved(wt_ref[layer], src_ref[pl.ds(index - 1, 3)])

        layer_rows(halo - layer, halo + rows + layer, back)
        stacked = jnp.concatenate(
            [
                src_ref[pl.ds(halo + row - 1, 3)].reshape(3 * channels, 2 * cols)[:, :cols]
                for row in range(rows)
            ],
            1,
        )
        grad = lax.dot_general(
            stacked, keep_ref[layer], (((1,), (1,)), ((), ())), preferred_element_type=f32
        )
        for tap in range(3):
            grad_ref[layer, :, pl.ds(tap * 3 * channels, 3 * channels)] = grad[
                (2 - tap) * channels : (3 - tap) * channels
            ]
    for row in range(rows):
        value = adj_ref[halo + row, :, :cols]
        g_ref[row] = value
        gb_ref[row] = value.astype(bf16)


def last_body(*refs, channels, rows):
    q_ref, arrived, out_ref = refs[0], refs[1:-1], refs[-1]
    last = lax.axis_index("layer") == lax.axis_size("layer") - 1
    for row in range(rows):
        value = sum(ref[row].astype(f32) for ref in arrived)
        value = jnp.where(last, row_of(q_ref, row, channels, rows), value)
        out_ref[pl.ds(row, channels, stride=rows), :] = value


def shifted(array, row_by, col_by):
    rows, cols = lax.axis_size("row"), lax.axis_size("col")
    pairs = [
        (r * cols + c, (r + row_by) * cols + c + col_by)
        for r in range(rows)
        for c in range(cols)
        if 0 <= r + row_by < rows and 0 <= c + col_by < cols
    ]
    return lax.ppermute(array, ("row", "col"), pairs)


def swapped(array, row_by):
    rows = lax.axis_size("row")
    pairs = [
        (r * 2 + c, (r + row_by) * 2 + 1 - c)
        for r in range(rows)
        for c in range(2)
        if 0 <= r + row_by < rows
    ]
    return lax.ppermute(array, ("row", "col"), pairs)


def around(edges):
    if lax.axis_size("col") == 2:
        parts = [swapped(edges, by) for by in (1, 0, -1)]
        both = jnp.stack(parts, 0)
        return both, both
    return (
        jnp.stack([shifted(edges, by, 1) for by in (1, 0, -1)], 0),
        jnp.stack([shifted(edges, by, -1) for by in (1, 0, -1)], 0),
    )


def total_over_tiles(grads):
    rows, cols = lax.axis_size("row"), lax.axis_size("col")
    depth = grads.shape[0]
    half = depth // 2
    odd = lax.axis_index("row") % 2 == 1
    sent = jnp.where(odd, grads[:half], grads[half:]).astype(bf16)
    own = jnp.where(odd, grads[half:], grads[:half])
    pair = [(r, r ^ 1) for r in range(rows)]
    value = own + lax.ppermute(sent, "row", pair).astype(f32)

    def add(value, axis, pairs):
        rounded = value.astype(bf16)
        return rounded.astype(f32) + lax.ppermute(rounded, axis, pairs).astype(f32)

    bit = 2
    while bit < rows:
        value = add(value, "row", [(r, r ^ bit) for r in range(rows)])
        bit *= 2
    bit = 1
    while bit < cols:
        value = add(value, "col", [(c, c ^ bit) for c in range(cols)])
        bit *= 2
    rounded = value.astype(bf16)
    other = lax.ppermute(rounded, "row", pair)
    first = jnp.where(odd, other, rounded)
    second = jnp.where(odd, rounded, other)
    return jnp.concatenate([first, second], 0).astype(f32)


def local(c_states, c_adjoints, weights):
    groups = lax.axis_size("layer")
    channels, rows, cols = c_states.shape[1:]
    depth = weights.shape[0]
    flat = (channels * rows, cols)
    c_flat, q_flat = c_states.reshape(flat), c_adjoints.reshape(flat)
    sizes = dict(channels=channels, rows=rows)
    tile_b = jax.ShapeDtypeStruct((rows, channels, cols), bf16)
    tile_f = jax.ShapeDtypeStruct((rows, channels, cols), f32)

    top, bottom, edges = call(
        functools.partial(pack_body, depth=depth, **sizes),
        (
            jax.ShapeDtypeStruct((2 * depth, channels, cols), bf16),
            jax.ShapeDtypeStruct((2 * depth, channels, cols), bf16),
            jax.ShapeDtypeStruct((2, channels, cols), bf16),
        ),
    )(c_flat, q_flat)
    above = shifted(bottom, 1, 0)
    below = shifted(top, -1, 0)
    left, right = around(edges)

    taps = weights.reshape(depth, channels, 3, 3, channels)
    w_fwd = jnp.transpose(taps, (0, 3, 1, 2, 4)).reshape(depth, 3 * channels, 3 * channels)
    w_back = jnp.transpose(taps[:, :, ::-1, ::-1, :], (0, 3, 4, 2, 1)).reshape(
        depth, 3 * channels, 3 * channels
    )
    coarse = step_size * jnp.sum(weights[0].astype(f32).reshape(channels, 9, channels), axis=1)
    high = coarse.astype(bf16)
    low = (coarse - high.astype(f32)).astype(bf16)
    m_fwd = jnp.concatenate([high, low, high], 1)
    m_back = jnp.concatenate([high.T, low.T, high.T], 1)

    lanes = 2 * cols
    mac = 2 * 9 * channels * channels * lanes
    total = rows + 2 * depth
    f, sending = call(
        functools.partial(first_body, depth=depth, **sizes),
        (tile_f, tile_b),
        [
            pltpu.VMEM((total, channels, lanes), f32),
            pltpu.VMEM((2, total, channels, lanes), bf16),
        ],
        flops=mac * 44,
    )(c_flat, above[:depth], below[:depth], left[:, 0], right[:, 0], w_fwd)

    def chain(sending, base, target, matrix, order):
        arrivals = []
        for place, (source, goal) in enumerate(order):
            arrived = lax.ppermute(sending, "layer", [(source, goal)])
            arrivals.append(arrived)
            if place < len(order) - 1:
                sending = call(functools.partial(hop_body, **sizes), tile_b)(
                    arrived, base, target, matrix
                )
        return arrivals

    arrivals = chain(sending, c_flat, f, m_fwd, [(k, k + 1) for k in range(groups - 1)])
    s, s_edges = call(
        functools.partial(settle_body, **sizes),
        (tile_b, jax.ShapeDtypeStruct((1, channels, cols), bf16)),
    )(c_flat, *arrivals)
    s_above = shifted(s, 1, 0)
    s_below = shifted(s, -1, 0)
    s_left, s_right = around(s_edges)

    total = rows + 4 * depth
    state, g, sending, grads = call(
        functools.partial(second_body, depth=depth, **sizes),
        (
            jax.ShapeDtypeStruct(flat, f32),
            tile_f,
            tile_b,
            jax.ShapeDtypeStruct((depth, channels, 9 * channels), f32),
        ),
        [
            pltpu.VMEM((total, channels, lanes), f32),
            pltpu.VMEM((2, total, channels, lanes), bf16),
            pltpu.VMEM((depth, 3 * channels, rows * cols), bf16),
            pltpu.VMEM((depth, total, channels, lanes), f32),
            pltpu.VMEM((total, channels, lanes), f32),
            pltpu.VMEM((total, channels, lanes), bf16),
        ],
        flops=mac * 136,
    )(
        c_flat, q_flat, s, s_above, s_below, s_left[:, 0], s_right[:, 0],
        above[depth:], below[depth:], left[:, 1], right[:, 1], w_fwd, w_back,
    )
    returned = chain(
        sending, q_flat, g, m_back, [(k, k - 1) for k in range(groups - 1, 0, -1)]
    )
    weight_grads = total_over_tiles(grads)
    adjoint = call(
        functools.partial(last_body, **sizes), jax.ShapeDtypeStruct(flat, f32)
    )(q_flat, *returned)
    return state.reshape(c_states.shape), adjoint.reshape(c_states.shape), weight_grads


def solution(mesh):
    placed = (
        P("layer", None, "row", "col"),
        P("layer", None, "row", "col"),
        P("layer", None, None),
    )
    return jax.shard_map(
        local, mesh=mesh, in_specs=placed, out_specs=placed, check_vma=False
    )
```

```python
import functools

import jax
import jax.numpy as jnp
from jax import lax
from jax.experimental import pallas as pl
from jax.experimental.pallas import tpu as pltpu
from jax.sharding import PartitionSpec as P

step_size = 0.2
EDGE = 8
VMEM_BYTES = 40 * 1024 * 1024
f32 = jnp.float32
bf16 = jnp.bfloat16


def call(body, out_shape, scratch=(), flops=0, moved=0):
    return pl.pallas_call(
        body,
        out_shape=out_shape,
        scratch_shapes=list(scratch),
        cost_estimate=pl.CostEstimate(
            flops=int(flops), bytes_accessed=int(moved), transcendentals=0
        ),
        compiler_params=pltpu.CompilerParams(vmem_limit_bytes=VMEM_BYTES),
    )


def row_of(ref, row, channels, rows):
    return ref[pl.ds(row, channels, stride=rows), :]


def lanes_of(shape):
    return lax.broadcasted_iota(jnp.int32, shape, 1)


def fold_edges(rows_list):
    shape = rows_list[0].shape
    slot = lanes_of(shape) // (2 * EDGE)
    total = jnp.zeros(shape, f32)
    for place, row in enumerate(rows_list):
        turned = pltpu.roll(row, (2 * EDGE * place + EDGE) % shape[1], 1)
        total = jnp.where(slot == place, turned, total)
    return total


def join_edges(from_left, from_right, has_left, has_right):
    lanes = lanes_of(from_left.shape)
    return jnp.where(
        lanes % (2 * EDGE) >= EDGE,
        from_right.astype(f32) * has_right,
        from_left.astype(f32) * has_left,
    )


def side_lanes(joined, place):
    cols = joined.shape[1]
    return pltpu.roll(joined, (cols - (2 * EDGE * place + EDGE)) % cols, 1)


def convolved(weights, slab):
    channels = slab.shape[1]
    lanes = slab.shape[2]
    product = jnp.dot(
        weights, slab.reshape(3 * channels, lanes), preferred_element_type=f32
    )
    return (
        pltpu.roll(product[:channels], 1, 1)
        + product[channels : 2 * channels]
        + pltpu.roll(product[2 * channels :], lanes - 1, 1)
    )


def flags():
    row, col = lax.axis_index("row"), lax.axis_index("col")
    up = (row > 0).astype(f32)
    down = (row < lax.axis_size("row") - 1).astype(f32)
    left = (col > 0).astype(f32)
    right = (col < lax.axis_size("col") - 1).astype(f32)
    return up, down, left, right


def lane_mask(cols, left, right):
    lanes = lax.broadcasted_iota(jnp.int32, (1, 2 * cols), 1)
    return jnp.where(lanes < cols, 1.0, jnp.where(lanes < cols + cols // 2, right, left))


def pack_body(c_ref, q_ref, top_ref, bottom_ref, edge_ref, *, channels, rows, depth):
    for which, ref in enumerate((c_ref, q_ref)):
        image = [row_of(ref, row, channels, rows) for row in range(rows)]
        for row in range(depth):
            top_ref[which * depth + row] = image[row].astype(bf16)
            bottom_ref[which * depth + row] = image[rows - depth + row].astype(bf16)
        edge_ref[which] = fold_edges(image).astype(bf16)


def load_halo(dest, first, side_ref, count, halo, joined, offset):
    for row in range(count):
        dest(
            first + row,
            halo[row].astype(f32),
            side_lanes(joined, offset + row),
        )


def row_blocks(low, high, body, size=4):
    turns, rest = divmod(high - low, size)

    def turn(number, carry):
        body(low + size * number, size)
        return carry

    if turns > 0:
        lax.fori_loop(0, turns, turn, 0)
    if rest > 0:
        body(low + size * turns, rest)


def convolved_rows(weights, ref, first, count):
    slab = ref[pl.ds(first - 1, count + 2)]
    return [convolved(weights, slab[place : place + 3]) for place in range(count)]


def row_flag(index, halo, rows, up, down):
    return jnp.where(index < halo, up, jnp.where(index >= halo + rows, down, 1.0))


def first_body(
    c_ref, above_ref, below_ref, left_ref, right_ref, w_ref, f_ref, fb_ref, x_ref, a_ref, a2_ref,
    *, channels, rows, depth,
):
    cols = c_ref.shape[1]
    up, down, left, right = flags()
    mask = lane_mask(cols, left, right)
    halo = depth

    def put(index, own, beyond):
        x_ref[index, :, :cols] = own
        x_ref[index, :, cols:] = beyond
        a_ref[index, :, :cols] = own.astype(bf16)
        a_ref[index, :, cols:] = beyond.astype(bf16)

    joined = [join_edges(left_ref[j], right_ref[j], left, right) for j in range(3)]
    for row in range(rows):
        put(halo + row, row_of(c_ref, row, channels, rows), side_lanes(joined[1], row))
    for row in range(depth):
        put(row, above_ref[row].astype(f32), side_lanes(joined[0], rows - depth + row))
        put(halo + rows + row, below_ref[row].astype(f32), side_lanes(joined[2], row))

    total = rows + 2 * halo
    for layer in range(depth):
        now, later = (a_ref, a2_ref) if layer % 2 == 0 else (a2_ref, a_ref)

        def step(first, count, layer=layer, now=now, later=later):
            states = x_ref[pl.ds(first, count)]
            done = []
            for place, z in enumerate(convolved_rows(w_ref[layer], now, first, count)):
                gain = mask * (step_size * row_flag(first + place, halo, rows, up, down))
                done.append(states[place] + gain * jnp.tanh(z))
            for place, x in enumerate(done):
                x_ref[first + place] = x
                if layer < depth - 1:
                    later[first + place] = x.astype(bf16)

        row_blocks(layer + 1, total - layer - 1, step)
    for row in range(rows):
        value = x_ref[halo + row, :, :cols]
        f_ref[row] = value
        fb_ref[row] = value.astype(bf16)


def hop_body(s_ref, c_ref, f_ref, m_ref, out_ref, *, channels, rows):
    for row in range(rows):
        e = s_ref[row].astype(f32) - row_of(c_ref, row, channels, rows)
        high = e.astype(bf16)
        low = (e - high.astype(f32)).astype(bf16)
        stacked = jnp.concatenate([high, high, low], 0)
        moved = jnp.dot(m_ref[...], stacked, preferred_element_type=f32)
        out_ref[row] = (f_ref[row] + e + moved).astype(bf16)


def settle_body(*refs, channels, rows):
    c_ref, arrived, s_ref, edge_ref = refs[0], refs[1:-2], refs[-2], refs[-1]
    first = lax.axis_index("layer") == 0
    image = []
    for row in range(rows):
        value = sum(ref[row].astype(f32) for ref in arrived)
        value = jnp.where(first, row_of(c_ref, row, channels, rows), value)
        s_ref[row] = value.astype(bf16)
        image.append(value)
    edge_ref[0] = fold_edges(image).astype(bf16)


def second_body(
    c_ref, q_ref, s_ref, s_above_ref, s_below_ref, s_left_ref, s_right_ref,
    q_above_ref, q_below_ref, q_left_ref, q_right_ref, w_ref, wt_ref,
    state_ref, g_ref, gb_ref, grad_ref,
    x_ref, a_ref, a2_ref, keep_ref, slope_ref, adj_ref, src_ref,
    *, channels, rows, depth,
):
    cols = c_ref.shape[1]
    up, down, left, right = flags()
    mask = lane_mask(cols, left, right)
    halo = 2 * depth
    total = rows + 2 * halo
    first = lax.axis_index("layer") == 0

    def put(index, own, beyond):
        x_ref[index, :, :cols] = own
        x_ref[index, :, cols:] = beyond
        a_ref[index, :, :cols] = own.astype(bf16)
        a_ref[index, :, cols:] = beyond.astype(bf16)

    joined = [join_edges(s_left_ref[j], s_right_ref[j], left, right) for j in range(3)]
    for row in range(rows):
        own = jnp.where(first, row_of(c_ref, row, channels, rows), s_ref[row].astype(f32))
        state_ref[pl.ds(row, channels, stride=rows), :] = own
        put(halo + row, own, side_lanes(joined[1], row))
    for row in range(halo):
        put(row, s_above_ref[rows - halo + row].astype(f32), side_lanes(joined[0], rows - halo + row))
        put(halo + rows + row, s_below_ref[row].astype(f32), side_lanes(joined[2], row))

    def put_adj(index, own, beyond):
        adj_ref[index, :, :cols] = own
        adj_ref[index, :, cols:] = beyond

    joined = [join_edges(q_left_ref[j], q_right_ref[j], left, right) for j in range(3)]
    for row in range(rows):
        put_adj(halo + row, row_of(q_ref, row, channels, rows), side_lanes(joined[1], row))
    for row in range(depth):
        put_adj(halo - depth + row, q_above_ref[row].astype(f32), side_lanes(joined[0], rows - depth + row))
        put_adj(halo + rows + row, q_below_ref[row].astype(f32), side_lanes(joined[2], row))

    def keep(layer):
        for row in range(rows):
            x = x_ref[halo + row]
            lanes = 2 * cols
            keep_ref[layer, :, pl.ds(row * cols, cols)] = jnp.concatenate(
                [
                    pltpu.roll(x, 1, 1)[:, :cols],
                    x[:, :cols],
                    pltpu.roll(x, lanes - 1, 1)[:, :cols],
                ],
                0,
            ).astype(bf16)

    for layer in range(depth):
        now, later = (a_ref, a2_ref) if layer % 2 == 0 else (a2_ref, a_ref)
        keep(layer)

        def step(first, count, layer=layer, now=now, later=later):
            states = x_ref[pl.ds(first, count)]
            done = []
            for place, z in enumerate(convolved_rows(w_ref[layer], now, first, count)):
                gain = mask * (step_size * row_flag(first + place, halo, rows, up, down))
                t = jnp.tanh(z)
                done.append((gain * (1.0 - t * t), states[place] + gain * t))
            for place, (slope, x) in enumerate(done):
                slope_ref[layer, first + place] = slope
                if layer < depth - 1:
                    x_ref[first + place] = x
                    later[first + place] = x.astype(bf16)

        row_blocks(layer + 1, total - layer - 1, step)

    for layer in reversed(range(depth)):
        reach = layer + 1

        def source(first, count, layer=layer):
            part = pl.ds(first, count)
            src_ref[part] = (adj_ref[part] * slope_ref[layer, part]).astype(bf16)

        row_blocks(halo - reach, halo + rows + reach, source, 2)

        def back(first, count, layer=layer):
            adjoints = adj_ref[pl.ds(first, count)]
            moved = convolved_rows(wt_ref[layer], src_ref, first, count)
            for place in range(count):
                adj_ref[first + place] = adjoints[place] + moved[place]

        row_blocks(halo - layer, halo + rows + layer, back)
        stacked = jnp.concatenate(
            [
                src_ref[pl.ds(halo + row - 1, 3)].reshape(3 * channels, 2 * cols)[:, :cols]
                for row in range(rows)
            ],
            1,
        )
        grad = lax.dot_general(
            stacked, keep_ref[layer], (((1,), (1,)), ((), ())), preferred_element_type=f32
        )
        for tap in range(3):
            grad_ref[layer, :, pl.ds(tap * 3 * channels, 3 * channels)] = grad[
                (2 - tap) * channels : (3 - tap) * channels
            ]
    for row in range(rows):
        value = adj_ref[halo + row, :, :cols]
        g_ref[row] = value
        gb_ref[row] = value.astype(bf16)


def last_body(*refs, channels, rows):
    q_ref, arrived, out_ref = refs[0], refs[1:-1], refs[-1]
    last = lax.axis_index("layer") == lax.axis_size("layer") - 1
    for row in range(rows):
        value = sum(ref[row].astype(f32) for ref in arrived)
        value = jnp.where(last, row_of(q_ref, row, channels, rows), value)
        out_ref[pl.ds(row, channels, stride=rows), :] = value


def shifted(array, row_by, col_by):
    rows, cols = lax.axis_size("row"), lax.axis_size("col")
    pairs = [
        (r * cols + c, (r + row_by) * cols + c + col_by)
        for r in range(rows)
        for c in range(cols)
        if 0 <= r + row_by < rows and 0 <= c + col_by < cols
    ]
    return lax.ppermute(array, ("row", "col"), pairs)


def swapped(array, row_by):
    rows = lax.axis_size("row")
    pairs = [
        (r * 2 + c, (r + row_by) * 2 + 1 - c)
        for r in range(rows)
        for c in range(2)
        if 0 <= r + row_by < rows
    ]
    return lax.ppermute(array, ("row", "col"), pairs)


def around(edges):
    if lax.axis_size("col") == 2:
        parts = [swapped(edges, by) for by in (1, 0, -1)]
        both = jnp.stack(parts, 0)
        return both, both
    return (
        jnp.stack([shifted(edges, by, 1) for by in (1, 0, -1)], 0),
        jnp.stack([shifted(edges, by, -1) for by in (1, 0, -1)], 0),
    )


def total_over_tiles(grads):
    rows, cols = lax.axis_size("row"), lax.axis_size("col")
    depth = grads.shape[0]
    half = depth // 2
    odd = lax.axis_index("row") % 2 == 1
    sent = jnp.where(odd, grads[:half], grads[half:])
    own = jnp.where(odd, grads[half:], grads[:half])
    pair = [(r, r ^ 1) for r in range(rows)]
    value = own + lax.ppermute(sent, "row", pair)

    def add(value, axis, pairs):
        rounded = value.astype(bf16)
        return rounded.astype(f32) + lax.ppermute(rounded, axis, pairs).astype(f32)

    bit = 2
    while bit < rows:
        value = add(value, "row", [(r, r ^ bit) for r in range(rows)])
        bit *= 2
    bit = 1
    while bit < cols:
        value = add(value, "col", [(c, c ^ bit) for c in range(cols)])
        bit *= 2
    other = lax.ppermute(value, "row", pair)
    first = jnp.where(odd, other, value)
    second = jnp.where(odd, value, other)
    return jnp.concatenate([first, second], 0)


def local(c_states, c_adjoints, weights):
    groups = lax.axis_size("layer")
    channels, rows, cols = c_states.shape[1:]
    depth = weights.shape[0]
    flat = (channels * rows, cols)
    c_flat, q_flat = c_states.reshape(flat), c_adjoints.reshape(flat)
    sizes = dict(channels=channels, rows=rows)
    tile_b = jax.ShapeDtypeStruct((rows, channels, cols), bf16)
    tile_f = jax.ShapeDtypeStruct((rows, channels, cols), f32)

    top, bottom, edges = call(
        functools.partial(pack_body, depth=depth, **sizes),
        (
            jax.ShapeDtypeStruct((2 * depth, channels, cols), bf16),
            jax.ShapeDtypeStruct((2 * depth, channels, cols), bf16),
            jax.ShapeDtypeStruct((2, channels, cols), bf16),
        ),
    )(c_flat, q_flat)
    above = shifted(bottom, 1, 0)
    below = shifted(top, -1, 0)
    left, right = around(edges)

    taps = weights.reshape(depth, channels, 3, 3, channels)
    w_fwd = jnp.transpose(taps, (0, 3, 1, 2, 4)).reshape(depth, 3 * channels, 3 * channels)
    w_back = jnp.transpose(taps[:, :, ::-1, ::-1, :], (0, 3, 4, 2, 1)).reshape(
        depth, 3 * channels, 3 * channels
    )
    coarse = step_size * jnp.sum(weights[0].astype(f32).reshape(channels, 9, channels), axis=1)
    high = coarse.astype(bf16)
    low = (coarse - high.astype(f32)).astype(bf16)
    m_fwd = jnp.concatenate([high, low, high], 1)
    m_back = jnp.concatenate([high.T, low.T, high.T], 1)

    lanes = 2 * cols
    mac = 2 * 9 * channels * channels * lanes
    total = rows + 2 * depth
    f, sending = call(
        functools.partial(first_body, depth=depth, **sizes),
        (tile_f, tile_b),
        [
            pltpu.VMEM((total, channels, lanes), f32),
            pltpu.VMEM((total, channels, lanes), bf16),
            pltpu.VMEM((total, channels, lanes), bf16),
        ],
        flops=mac * 44,
    )(c_flat, above[:depth], below[:depth], left[:, 0], right[:, 0], w_fwd)

    def chain(sending, base, target, matrix, order):
        arrivals = []
        for place, (source, goal) in enumerate(order):
            arrived = lax.ppermute(sending, "layer", [(source, goal)])
            arrivals.append(arrived)
            if place < len(order) - 1:
                sending = call(functools.partial(hop_body, **sizes), tile_b, flops=10**10)(
                    arrived, base, target, matrix
                )
        return arrivals

    arrivals = chain(sending, c_flat, f, m_fwd, [(k, k + 1) for k in range(groups - 1)])
    s, s_edges = call(
        functools.partial(settle_body, **sizes),
        (tile_b, jax.ShapeDtypeStruct((1, channels, cols), bf16)),
    )(c_flat, *arrivals)
    s_above = shifted(s, 1, 0)
    s_below = shifted(s, -1, 0)
    s_left, s_right = around(s_edges)

    total = rows + 4 * depth
    state, g, sending, grads = call(
        functools.partial(second_body, depth=depth, **sizes),
        (
            jax.ShapeDtypeStruct(flat, f32),
            tile_f,
            tile_b,
            jax.ShapeDtypeStruct((depth, channels, 9 * channels), f32),
        ),
        [
            pltpu.VMEM((total, channels, lanes), f32),
            pltpu.VMEM((total, channels, lanes), bf16),
            pltpu.VMEM((total, channels, lanes), bf16),
            pltpu.VMEM((depth, 3 * channels, rows * cols), bf16),
            pltpu.VMEM((depth, total, channels, lanes), f32),
            pltpu.VMEM((total, channels, lanes), f32),
            pltpu.VMEM((total, channels, lanes), bf16),
        ],
        flops=mac * 136,
    )(
        c_flat, q_flat, s, s_above, s_below, s_left[:, 0], s_right[:, 0],
        above[depth:], below[depth:], left[:, 1], right[:, 1], w_fwd, w_back,
    )
    returned = chain(
        sending, q_flat, g, m_back, [(k, k - 1) for k in range(groups - 1, 0, -1)]
    )
    weight_grads = total_over_tiles(grads)
    adjoint = call(
        functools.partial(last_body, **sizes), jax.ShapeDtypeStruct(flat, f32), flops=10**10
    )(q_flat, *returned)
    return state.reshape(c_states.shape), adjoint.reshape(c_states.shape), weight_grads


def solution(mesh):
    placed = (
        P("layer", None, "row", "col"),
        P("layer", None, "row", "col"),
        P("layer", None, None),
    )
    return jax.shard_map(
        local, mesh=mesh, in_specs=placed, out_specs=placed, check_vma=False
    )
```

```python
import functools

import jax
import jax.numpy as jnp
from jax import lax
from jax.experimental import pallas as pl
from jax.experimental.pallas import tpu as pltpu
from jax.sharding import PartitionSpec as P

step_size = 0.2
VMEM_BYTES = 40 * 1024 * 1024
f32 = jnp.float32
bf16 = jnp.bfloat16


def call(body, out_shape, scratch=(), flops=0, moved=0):
    return pl.pallas_call(
        body,
        out_shape=out_shape,
        scratch_shapes=list(scratch),
        cost_estimate=pl.CostEstimate(
            flops=int(flops), bytes_accessed=int(moved), transcendentals=0
        ),
        compiler_params=pltpu.CompilerParams(vmem_limit_bytes=VMEM_BYTES),
    )


def row_of(ref, row, channels, rows):
    return ref[pl.ds(row, channels, stride=rows), :]


def lanes_of(shape):
    return lax.broadcasted_iota(jnp.int32, shape, 1)


def slots(shape, low, width, count):
    return (lanes_of(shape) - low + width * count) // width - count


def fold_edges(rows_list, edge, low, total):
    doubled = total.shape[1] > rows_list[0].shape[1]
    cols = rows_list[0].shape[1]
    slot = slots(total.shape, low, 2 * edge, len(rows_list))
    for place, row in enumerate(rows_list):
        wide = jnp.concatenate([row, row], 1) if doubled else row
        turned = pltpu.roll(wide, (low + 2 * edge * place + edge - cols) % wide.shape[1], 1)
        total = jnp.where(slot == place, turned, total)
    return total


def join_edges(from_left, from_right, left, right, edges):
    lanes = lanes_of(from_left.shape)
    far = jnp.zeros(lanes.shape, jnp.bool_)
    for edge, low, high in edges:
        inside = (lanes >= low) & (lanes < high)
        far = far | (inside & ((lanes - low) % (2 * edge) >= edge))
    return jnp.where(far, from_right.astype(f32) * right, from_left.astype(f32) * left)


def side_lanes(joined, edge, low, place):
    lanes = joined.shape[1]
    turned = pltpu.roll(joined, (2 * lanes - (low + 2 * edge * place + edge)) % lanes, 1)
    if lanes == 128:
        return turned
    front, back = turned[:, :128], turned[:, lanes - 128 :]
    return jnp.where(lanes_of(front.shape) < 64, front, back)


def convolved(weights, slab):
    channels = slab.shape[1]
    lanes = slab.shape[2]
    product = jnp.dot(
        weights, slab.reshape(3 * channels, lanes), preferred_element_type=f32
    )
    return (
        pltpu.roll(product[:channels], 1, 1)
        + product[channels : 2 * channels]
        + pltpu.roll(product[2 * channels :], lanes - 1, 1)
    )


def flags():
    row, col = lax.axis_index("row"), lax.axis_index("col")
    up = (row > 0).astype(f32)
    down = (row < lax.axis_size("row") - 1).astype(f32)
    left = (col > 0).astype(f32)
    right = (col < lax.axis_size("col") - 1).astype(f32)
    return up, down, left, right


def lane_mask(cols, left, right):
    lanes = lax.broadcasted_iota(jnp.int32, (1, 2 * cols), 1)
    return jnp.where(lanes < cols, 1.0, jnp.where(lanes < cols + cols // 2, right, left))


def layout(rows, depth):
    state_edge, adjoint_edge = 3 * depth, depth
    return (state_edge, 0), (adjoint_edge, 2 * state_edge * rows)


def strip_body(c_ref, q_ref, edge_ref, *, channels, rows, depth):
    total = jnp.zeros(edge_ref.shape, f32)
    for ref, (edge, low) in zip((c_ref, q_ref), layout(rows, depth)):
        image = [row_of(ref, row, channels, rows) for row in range(rows)]
        total = fold_edges(image, edge, low, total)
    edge_ref[...] = total.astype(bf16)


def message_body(
    c_ref, q_ref, left_ref, right_ref, top_ref, bottom_ref, side_ref, *, channels, rows, depth
):
    cols = c_ref.shape[1]
    _, _, left, right = flags()
    (c_edge, _), (q_edge, middle) = layout(rows, depth)
    edges = ((c_edge, 0, middle), (q_edge, middle, 2 * cols))
    side = join_edges(left_ref[...], right_ref[...], left, right, edges).astype(bf16)
    side_ref[...] = side
    for which, ref in enumerate((c_ref, q_ref)):
        for row in range(depth):
            place = which * depth + row
            top_ref[place] = row_of(ref, row, channels, rows).astype(bf16)
            bottom_ref[place] = row_of(ref, rows - depth + row, channels, rows).astype(bf16)
    for half in range(2):
        part = side[:, half * cols : (half + 1) * cols]
        top_ref[2 * depth + half] = part
        bottom_ref[2 * depth + half] = part


def strips_of(ref, depth):
    return jnp.concatenate([ref[2 * depth], ref[2 * depth + 1]], 1).astype(f32)


def row_blocks(low, high, body, size=4):
    turns, rest = divmod(high - low, size)

    def turn(number, carry):
        body(low + size * number, size)
        return carry

    if turns > 0:
        lax.fori_loop(0, turns, turn, 0)
    if rest > 0:
        body(low + size * turns, rest)


def convolved_rows(weights, ref, first, count):
    slab = ref[pl.ds(first - 1, count + 2)]
    return [convolved(weights, slab[place : place + 3]) for place in range(count)]


def row_flag(index, halo, rows, up, down):
    return jnp.where(index < halo, up, jnp.where(index >= halo + rows, down, 1.0))


def first_body(
    c_ref, above_ref, below_ref, side_ref, w_ref, f_ref, fb_ref, strip_ref, x_ref, a_ref, a2_ref,
    *, channels, rows, depth,
):
    cols = c_ref.shape[1]
    up, down, left, right = flags()
    mask = lane_mask(cols, left, right)
    halo = depth

    def put(index, own, beyond):
        x_ref[index, :, :cols] = own
        x_ref[index, :, cols:] = beyond
        a_ref[index, :, :cols] = own.astype(bf16)
        a_ref[index, :, cols:] = beyond.astype(bf16)

    (edge, low), _ = layout(rows, depth)
    own_side = side_ref[...].astype(f32)
    image = []
    for row in range(rows):
        beyond = side_lanes(own_side, edge, low, row)
        image.append(beyond)
        put(halo + row, row_of(c_ref, row, channels, rows), beyond)
    strip_ref[...] = fold_edges(image, 2 * depth, 0, jnp.zeros(strip_ref.shape, f32))
    above_side, below_side = strips_of(above_ref, depth), strips_of(below_ref, depth)
    for row in range(depth):
        place = rows - depth + row
        put(row, above_ref[row].astype(f32), side_lanes(above_side, edge, low, place))
        put(halo + rows + row, below_ref[row].astype(f32), side_lanes(below_side, edge, low, row))

    total = rows + 2 * halo
    for layer in range(depth):
        now, later = (a_ref, a2_ref) if layer % 2 == 0 else (a2_ref, a_ref)

        def step(first, count, layer=layer, now=now, later=later):
            states = x_ref[pl.ds(first, count)]
            done = []
            for place, z in enumerate(convolved_rows(w_ref[layer], now, first, count)):
                gain = mask * (step_size * row_flag(first + place, halo, rows, up, down))
                done.append(states[place] + gain * jnp.tanh(z))
            for place, x in enumerate(done):
                x_ref[first + place] = x
                if layer < depth - 1:
                    later[first + place] = x.astype(bf16)

        row_blocks(layer + 1, total - layer - 1, step)
    image = [x_ref[halo + row, :, cols:] for row in range(rows)]
    values = [x_ref[halo + row, :, :cols] for row in range(rows)]
    values.append(fold_edges(image, 2 * depth, 0, jnp.zeros(strip_ref.shape, f32)))
    for row, value in enumerate(values):
        f_ref[row] = value
        fb_ref[row] = value.astype(bf16)


def hop_body(s_ref, c_ref, *refs, channels, rows):
    f_ref, m_ref, out_ref = refs[-3:]
    base = [row_of(c_ref, row, channels, rows) for row in range(rows)]
    base += [ref[...] for ref in refs[:-3]]
    for row in range(len(base)):
        e = s_ref[row].astype(f32) - base[row]
        high = e.astype(bf16)
        low = (e - high.astype(f32)).astype(bf16)
        stacked = jnp.concatenate([high, high, low], 0)
        moved = jnp.dot(m_ref[...], stacked, preferred_element_type=f32)
        out_ref[row] = (f_ref[row] + e + moved).astype(bf16)


def settle_body(c_ref, strip_ref, *refs, channels, rows):
    arrived, s_ref = refs[:-1], refs[-1]
    first = lax.axis_index("layer") == 0
    base = [row_of(c_ref, row, channels, rows) for row in range(rows)] + [strip_ref[...]]
    for row in range(rows + 1):
        value = sum(ref[row].astype(f32) for ref in arrived)
        s_ref[row] = jnp.where(first, base[row], value).astype(bf16)


def second_body(
    c_ref, q_ref, s_ref, s_above_ref, s_below_ref, above_ref, below_ref, side_ref, w_ref, wt_ref,
    state_ref, g_ref, gb_ref, grad_ref,
    x_ref, a_ref, a2_ref, keep_ref, slope_ref, adj_ref, src_ref,
    *, channels, rows, depth,
):
    cols = c_ref.shape[1]
    up, down, left, right = flags()
    mask = lane_mask(cols, left, right)
    halo = 2 * depth
    total = rows + 2 * halo
    first = lax.axis_index("layer") == 0

    def put(index, own, beyond):
        x_ref[index, :, :cols] = own
        x_ref[index, :, cols:] = beyond
        a_ref[index, :, :cols] = own.astype(bf16)
        a_ref[index, :, cols:] = beyond.astype(bf16)

    edge = 2 * depth
    own_side, above_side, below_side = (
        ref[rows].astype(f32) for ref in (s_ref, s_above_ref, s_below_ref)
    )
    for row in range(rows):
        own = jnp.where(first, row_of(c_ref, row, channels, rows), s_ref[row].astype(f32))
        state_ref[pl.ds(row, channels, stride=rows), :] = own
        put(halo + row, own, side_lanes(own_side, edge, 0, row))
    for row in range(halo):
        place = rows - halo + row
        put(row, s_above_ref[place].astype(f32), side_lanes(above_side, edge, 0, place))
        put(halo + rows + row, s_below_ref[row].astype(f32), side_lanes(below_side, edge, 0, row))

    def put_adj(index, own, beyond):
        adj_ref[index, :, :cols] = own
        adj_ref[index, :, cols:] = beyond

    _, (edge, low) = layout(rows, depth)
    own_side = side_ref[...].astype(f32)
    above_side, below_side = strips_of(above_ref, depth), strips_of(below_ref, depth)
    for row in range(rows):
        put_adj(
            halo + row, row_of(q_ref, row, channels, rows), side_lanes(own_side, edge, low, row)
        )
    for row in range(depth):
        place = rows - depth + row
        put_adj(
            halo - depth + row,
            above_ref[depth + row].astype(f32),
            side_lanes(above_side, edge, low, place),
        )
        put_adj(
            halo + rows + row,
            below_ref[depth + row].astype(f32),
            side_lanes(below_side, edge, low, row),
        )

    def keep(layer):
        for row in range(rows):
            x = x_ref[halo + row]
            lanes = 2 * cols
            keep_ref[layer, :, pl.ds(row * cols, cols)] = jnp.concatenate(
                [
                    pltpu.roll(x, 1, 1)[:, :cols],
                    x[:, :cols],
                    pltpu.roll(x, lanes - 1, 1)[:, :cols],
                ],
                0,
            ).astype(bf16)

    for layer in range(depth):
        now, later = (a_ref, a2_ref) if layer % 2 == 0 else (a2_ref, a_ref)
        keep(layer)

        def step(first, count, layer=layer, now=now, later=later):
            states = x_ref[pl.ds(first, count)]
            done = []
            for place, z in enumerate(convolved_rows(w_ref[layer], now, first, count)):
                gain = mask * (step_size * row_flag(first + place, halo, rows, up, down))
                t = jnp.tanh(z)
                done.append((gain * (1.0 - t * t), states[place] + gain * t))
            for place, (slope, x) in enumerate(done):
                slope_ref[layer, first + place] = slope
                if layer < depth - 1:
                    x_ref[first + place] = x
                    later[first + place] = x.astype(bf16)

        row_blocks(layer + 1, total - layer - 1, step)

    for layer in reversed(range(depth)):
        reach = layer + 1

        def source(first, count, layer=layer):
            part = pl.ds(first, count)
            src_ref[part] = (adj_ref[part] * slope_ref[layer, part]).astype(bf16)

        row_blocks(halo - reach, halo + rows + reach, source, 2)

        def back(first, count, layer=layer):
            adjoints = adj_ref[pl.ds(first, count)]
            moved = convolved_rows(wt_ref[layer], src_ref, first, count)
            for place in range(count):
                adj_ref[first + place] = adjoints[place] + moved[place]

        row_blocks(halo - layer, halo + rows + layer, back)
        stacked = jnp.concatenate(
            [
                src_ref[pl.ds(halo + row - 1, 3)].reshape(3 * channels, 2 * cols)[:, :cols]
                for row in range(rows)
            ],
            1,
        )
        grad = lax.dot_general(
            stacked, keep_ref[layer], (((1,), (1,)), ((), ())), preferred_element_type=f32
        )
        for tap in range(3):
            grad_ref[layer, :, pl.ds(tap * 3 * channels, 3 * channels)] = grad[
                (2 - tap) * channels : (3 - tap) * channels
            ]
    for row in range(rows):
        value = adj_ref[halo + row, :, :cols]
        g_ref[row] = value
        gb_ref[row] = value.astype(bf16)


def last_body(*refs, channels, rows):
    q_ref, arrived, out_ref = refs[0], refs[1:-1], refs[-1]
    last = lax.axis_index("layer") == lax.axis_size("layer") - 1
    for row in range(rows):
        value = sum(ref[row].astype(f32) for ref in arrived)
        value = jnp.where(last, row_of(q_ref, row, channels, rows), value)
        out_ref[pl.ds(row, channels, stride=rows), :] = value


def shifted(array, axis, by):
    count = lax.axis_size(axis)
    pairs = [(i, i + by) for i in range(count) if 0 <= i + by < count]
    return lax.ppermute(array, axis, pairs)


def from_sides(array):
    if lax.axis_size("col") == 2:
        other = lax.ppermute(array, "col", [(0, 1), (1, 0)])
        return other, other
    return shifted(array, "col", 1), shifted(array, "col", -1)


def total_over_tiles(grads):
    rows, cols = lax.axis_size("row"), lax.axis_size("col")
    depth = grads.shape[0]
    half = depth // 2
    odd = lax.axis_index("row") % 2 == 1
    sent = jnp.where(odd, grads[:half], grads[half:])
    own = jnp.where(odd, grads[half:], grads[:half])
    pair = [(r, r ^ 1) for r in range(rows)]
    value = own + lax.ppermute(sent, "row", pair)

    def add(value, axis, pairs):
        rounded = value.astype(bf16)
        return rounded.astype(f32) + lax.ppermute(rounded, axis, pairs).astype(f32)

    bit = 2
    while bit < rows:
        value = add(value, "row", [(r, r ^ bit) for r in range(rows)])
        bit *= 2
    bit = 1
    while bit < cols:
        value = add(value, "col", [(c, c ^ bit) for c in range(cols)])
        bit *= 2
    other = lax.ppermute(value, "row", pair)
    first = jnp.where(odd, other, value)
    second = jnp.where(odd, value, other)
    return jnp.concatenate([first, second], 0)


def local(c_states, c_adjoints, weights):
    groups = lax.axis_size("layer")
    channels, rows, cols = c_states.shape[1:]
    depth = weights.shape[0]
    flat = (channels * rows, cols)
    c_flat, q_flat = c_states.reshape(flat), c_adjoints.reshape(flat)
    sizes = dict(channels=channels, rows=rows)
    tile_b = jax.ShapeDtypeStruct((rows, channels, cols), bf16)
    tile_f = jax.ShapeDtypeStruct((rows, channels, cols), f32)

    strip_f = jax.ShapeDtypeStruct((channels, cols), f32)
    wide_b = jax.ShapeDtypeStruct((channels, 2 * cols), bf16)
    more_f, more_b, message_b = (
        jax.ShapeDtypeStruct((count, channels, cols), kind)
        for count, kind in ((rows + 1, f32), (rows + 1, bf16), (2 * depth + 2, bf16))
    )

    edges = call(functools.partial(strip_body, depth=depth, **sizes), wide_b)(c_flat, q_flat)
    left, right = from_sides(edges)
    top, bottom, side = call(
        functools.partial(message_body, depth=depth, **sizes), (message_b, message_b, wide_b)
    )(c_flat, q_flat, left, right)
    above = shifted(bottom, "row", 1)
    below = shifted(top, "row", -1)

    taps = weights.reshape(depth, channels, 3, 3, channels)
    w_fwd = jnp.transpose(taps, (0, 3, 1, 2, 4)).reshape(depth, 3 * channels, 3 * channels)
    w_back = jnp.transpose(taps[:, :, ::-1, ::-1, :], (0, 3, 4, 2, 1)).reshape(
        depth, 3 * channels, 3 * channels
    )
    coarse = step_size * jnp.sum(weights[0].astype(f32).reshape(channels, 9, channels), axis=1)
    high = coarse.astype(bf16)
    low = (coarse - high.astype(f32)).astype(bf16)
    m_fwd = jnp.concatenate([high, low, high], 1)
    m_back = jnp.concatenate([high.T, low.T, high.T], 1)

    lanes = 2 * cols
    mac = 2 * 9 * channels * channels * lanes
    total = rows + 2 * depth
    f, sending, strip = call(
        functools.partial(first_body, depth=depth, **sizes),
        (more_f, more_b, strip_f),
        [
            pltpu.VMEM((total, channels, lanes), f32),
            pltpu.VMEM((total, channels, lanes), bf16),
            pltpu.VMEM((total, channels, lanes), bf16),
        ],
        flops=mac * 44,
    )(c_flat, above, below, side, w_fwd)

    def chain(sending, base, target, matrix, order):
        arrivals = []
        for place, (source, goal) in enumerate(order):
            arrived = lax.ppermute(sending, "layer", [(source, goal)])
            arrivals.append(arrived)
            if place < len(order) - 1:
                sending = call(
                    functools.partial(hop_body, **sizes),
                    jax.ShapeDtypeStruct(sending.shape, bf16),
                    flops=10**10,
                )(arrived, *base, target, matrix)
        return arrivals

    arrivals = chain(
        sending, (c_flat, strip), f, m_fwd, [(k, k + 1) for k in range(groups - 1)]
    )
    s = call(functools.partial(settle_body, **sizes), more_b)(c_flat, strip, *arrivals)
    s_above = shifted(s, "row", 1)
    s_below = shifted(s, "row", -1)

    total = rows + 4 * depth
    state, g, sending, grads = call(
        functools.partial(second_body, depth=depth, **sizes),
        (
            jax.ShapeDtypeStruct(flat, f32),
            tile_f,
            tile_b,
            jax.ShapeDtypeStruct((depth, channels, 9 * channels), f32),
        ),
        [
            pltpu.VMEM((total, channels, lanes), f32),
            pltpu.VMEM((total, channels, lanes), bf16),
            pltpu.VMEM((total, channels, lanes), bf16),
            pltpu.VMEM((depth, 3 * channels, rows * cols), bf16),
            pltpu.VMEM((depth, total, channels, lanes), f32),
            pltpu.VMEM((total, channels, lanes), f32),
            pltpu.VMEM((total, channels, lanes), bf16),
        ],
        flops=mac * 136,
    )(
        c_flat, q_flat, s, s_above, s_below, above, below, side, w_fwd, w_back
    )
    returned = chain(
        sending, (q_flat,), g, m_back, [(k, k - 1) for k in range(groups - 1, 0, -1)]
    )
    weight_grads = total_over_tiles(grads)
    adjoint = call(
        functools.partial(last_body, **sizes), jax.ShapeDtypeStruct(flat, f32), flops=10**10
    )(q_flat, *returned)
    return state.reshape(c_states.shape), adjoint.reshape(c_states.shape), weight_grads


def solution(mesh):
    placed = (
        P("layer", None, "row", "col"),
        P("layer", None, "row", "col"),
        P("layer", None, None),
    )
    return jax.shard_map(
        local, mesh=mesh, in_specs=placed, out_specs=placed, check_vma=False
    )
```

```python
import functools

import jax
import jax.numpy as jnp
from jax import lax
from jax.experimental import pallas as pl
from jax.experimental.pallas import tpu as pltpu
from jax.sharding import PartitionSpec as P

step_size = 0.2
VMEM_BYTES = 40 * 1024 * 1024
f32 = jnp.float32
bf16 = jnp.bfloat16


def call(body, out_shape, scratch=(), flops=0, moved=0):
    return pl.pallas_call(
        body,
        out_shape=out_shape,
        scratch_shapes=list(scratch),
        cost_estimate=pl.CostEstimate(
            flops=int(flops), bytes_accessed=int(moved), transcendentals=0
        ),
        compiler_params=pltpu.CompilerParams(vmem_limit_bytes=VMEM_BYTES),
    )


def piece_of(upper, lower, row, rows):
    half = rows // 2
    if row < half:
        return upper, row
    return (lower, row - half) if row < rows else (upper, half)


def row_of(ref, row, channels, rows):
    return ref[pl.ds(row, channels, stride=rows), :]


def lanes_of(shape):
    return lax.broadcasted_iota(jnp.int32, shape, 1)


def slots(shape, low, width, count):
    return (lanes_of(shape) - low + width * count) // width - count


def fold_edges(rows_list, edge, low, total):
    doubled = total.shape[1] > rows_list[0].shape[1]
    cols = rows_list[0].shape[1]
    slot = slots(total.shape, low, 2 * edge, len(rows_list))
    for place, row in enumerate(rows_list):
        wide = jnp.concatenate([row, row], 1) if doubled else row
        turned = pltpu.roll(wide, (low + 2 * edge * place + edge - cols) % wide.shape[1], 1)
        total = jnp.where(slot == place, turned, total)
    return total


def join_edges(from_left, from_right, left, right, edges):
    lanes = lanes_of(from_left.shape)
    far = jnp.zeros(lanes.shape, jnp.bool_)
    for edge, low, high in edges:
        inside = (lanes >= low) & (lanes < high)
        far = far | (inside & ((lanes - low) % (2 * edge) >= edge))
    return jnp.where(far, from_right.astype(f32) * right, from_left.astype(f32) * left)


def side_lanes(joined, edge, low, place):
    lanes = joined.shape[1]
    turned = pltpu.roll(joined, (2 * lanes - (low + 2 * edge * place + edge)) % lanes, 1)
    if lanes == 128:
        return turned
    front, back = turned[:, :128], turned[:, lanes - 128 :]
    return jnp.where(lanes_of(front.shape) < 64, front, back)


def convolved(weights, slab):
    channels = slab.shape[1]
    lanes = slab.shape[2]
    product = jnp.dot(
        weights, slab.reshape(3 * channels, lanes), preferred_element_type=f32
    )
    return (
        pltpu.roll(product[:channels], 1, 1)
        + product[channels : 2 * channels]
        + pltpu.roll(product[2 * channels :], lanes - 1, 1)
    )


def flags():
    row, col = lax.axis_index("row"), lax.axis_index("col")
    up = (row > 0).astype(f32)
    down = (row < lax.axis_size("row") - 1).astype(f32)
    left = (col > 0).astype(f32)
    right = (col < lax.axis_size("col") - 1).astype(f32)
    return up, down, left, right


def lane_mask(cols, left, right):
    lanes = lax.broadcasted_iota(jnp.int32, (1, 2 * cols), 1)
    return jnp.where(lanes < cols, 1.0, jnp.where(lanes < cols + cols // 2, right, left))


def layout(rows, depth):
    state_edge, adjoint_edge = 3 * depth, depth
    return (state_edge, 0), (adjoint_edge, 2 * state_edge * rows)


def strip_body(c_ref, q_ref, edge_ref, *, channels, rows, depth):
    total = jnp.zeros(edge_ref.shape, f32)
    for ref, (edge, low) in zip((c_ref, q_ref), layout(rows, depth)):
        image = [row_of(ref, row, channels, rows) for row in range(rows)]
        total = fold_edges(image, edge, low, total)
    edge_ref[...] = total.astype(bf16)


def message_body(
    c_ref, q_ref, left_ref, right_ref, top_ref, bottom_ref, side_ref, *, channels, rows, depth
):
    cols = c_ref.shape[1]
    _, _, left, right = flags()
    (c_edge, _), (q_edge, middle) = layout(rows, depth)
    edges = ((c_edge, 0, middle), (q_edge, middle, 2 * cols))
    side = join_edges(left_ref[...], right_ref[...], left, right, edges).astype(bf16)
    side_ref[...] = side
    for which, ref in enumerate((c_ref, q_ref)):
        for row in range(depth):
            place = which * depth + row
            top_ref[place] = row_of(ref, row, channels, rows).astype(bf16)
            bottom_ref[place] = row_of(ref, rows - depth + row, channels, rows).astype(bf16)
    for half in range(2):
        part = side[:, half * cols : (half + 1) * cols]
        top_ref[2 * depth + half] = part
        bottom_ref[2 * depth + half] = part


def strips_of(ref, depth):
    return jnp.concatenate([ref[2 * depth], ref[2 * depth + 1]], 1).astype(f32)


def row_blocks(low, high, body, size=4):
    turns, rest = divmod(high - low, size)

    def turn(number, carry):
        body(low + size * number, size)
        return carry

    if turns > 0:
        lax.fori_loop(0, turns, turn, 0)
    if rest > 0:
        body(low + size * turns, rest)


def convolved_rows(weights, ref, first, count):
    slab = ref[pl.ds(first - 1, count + 2)]
    return [convolved(weights, slab[place : place + 3]) for place in range(count)]


def row_flag(index, halo, rows, up, down):
    return jnp.where(index < halo, up, jnp.where(index >= halo + rows, down, 1.0))


def first_body(
    c_ref, above_ref, below_ref, side_ref, w_ref, f_ref, upper_ref, lower_ref, strip_ref, x_ref, a_ref, a2_ref,
    *, channels, rows, depth,
):
    cols = c_ref.shape[1]
    up, down, left, right = flags()
    mask = lane_mask(cols, left, right)
    halo = depth

    def put(index, own, beyond):
        x_ref[index, :, :cols] = own
        x_ref[index, :, cols:] = beyond
        a_ref[index, :, :cols] = own.astype(bf16)
        a_ref[index, :, cols:] = beyond.astype(bf16)

    (edge, low), _ = layout(rows, depth)
    own_side = side_ref[...].astype(f32)
    image = []
    for row in range(rows):
        beyond = side_lanes(own_side, edge, low, row)
        image.append(beyond)
        put(halo + row, row_of(c_ref, row, channels, rows), beyond)
    strip_ref[...] = fold_edges(image, 2 * depth, 0, jnp.zeros(strip_ref.shape, f32))
    above_side, below_side = strips_of(above_ref, depth), strips_of(below_ref, depth)
    for row in range(depth):
        place = rows - depth + row
        put(row, above_ref[row].astype(f32), side_lanes(above_side, edge, low, place))
        put(halo + rows + row, below_ref[row].astype(f32), side_lanes(below_side, edge, low, row))

    total = rows + 2 * halo
    for layer in range(depth):
        now, later = (a_ref, a2_ref) if layer % 2 == 0 else (a2_ref, a_ref)

        def step(first, count, layer=layer, now=now, later=later):
            states = x_ref[pl.ds(first, count)]
            done = []
            for place, z in enumerate(convolved_rows(w_ref[layer], now, first, count)):
                gain = mask * (step_size * row_flag(first + place, halo, rows, up, down))
                done.append(states[place] + gain * jnp.tanh(z))
            for place, x in enumerate(done):
                x_ref[first + place] = x
                if layer < depth - 1:
                    later[first + place] = x.astype(bf16)

        row_blocks(layer + 1, total - layer - 1, step)
    image = [x_ref[halo + row, :, cols:] for row in range(rows)]
    values = [x_ref[halo + row, :, :cols] for row in range(rows)]
    values.append(fold_edges(image, 2 * depth, 0, jnp.zeros(strip_ref.shape, f32)))
    for row, value in enumerate(values):
        f_ref[row] = value
        ref, place = piece_of(upper_ref, lower_ref, row, rows)
        ref[place] = value.astype(bf16)


def hop_body(s_ref, c_ref, *refs, start, channels, rows):
    f_ref, m_ref, out_ref = refs[-3:]
    count = rows // 2
    work = [(start + row, row_of(c_ref, start + row, channels, rows)) for row in range(count)]
    work += [(rows, ref[...]) for ref in refs[:-3]]
    for place, (row, base) in enumerate(work):
        e = s_ref[place].astype(f32) - base
        high = e.astype(bf16)
        low = (e - high.astype(f32)).astype(bf16)
        stacked = jnp.concatenate([high, high, low], 0)
        moved = jnp.dot(m_ref[...], stacked, preferred_element_type=f32)
        out_ref[place] = (f_ref[row] + e + moved).astype(bf16)


def settle_body(c_ref, *refs, start, strips, channels, rows):
    arrived, s_ref = refs[strips:-1], refs[-1]
    first = lax.axis_index("layer") == 0
    base = [row_of(c_ref, start + row, channels, rows) for row in range(rows // 2)]
    base += [ref[...] for ref in refs[:strips]]
    for place in range(len(base)):
        value = sum(ref[place].astype(f32) for ref in arrived)
        s_ref[place] = jnp.where(first, base[place], value).astype(bf16)


def second_body(
    c_ref, q_ref, s_up_ref, s_lo_ref, above_up_ref, above_lo_ref, below_up_ref, below_lo_ref,
    above_ref, below_ref, side_ref, w_ref, wt_ref,
    state_ref, g_ref, g_up_ref, g_lo_ref, kept_ref, sent_ref,
    x_ref, a_ref, a2_ref, slope_ref, adj_ref, src_ref,
    *, channels, rows, depth,
):
    cols = c_ref.shape[1]
    up, down, left, right = flags()
    mask = lane_mask(cols, left, right)
    halo = 2 * depth
    total = rows + 2 * halo
    first = lax.axis_index("layer") == 0

    def put(index, own, beyond):
        x_ref[index, :, :cols] = own
        x_ref[index, :, cols:] = beyond
        a_ref[index, :, :cols] = own.astype(bf16)
        a_ref[index, :, cols:] = beyond.astype(bf16)

    edge = 2 * depth

    def piece(upper, lower, row):
        ref, place = piece_of(upper, lower, row, rows)
        return ref[place].astype(f32)

    own_side = piece(s_up_ref, s_lo_ref, rows)
    above_side = piece(above_up_ref, above_lo_ref, rows)
    below_side = piece(below_up_ref, below_lo_ref, rows)
    for row in range(rows):
        own = jnp.where(
            first, row_of(c_ref, row, channels, rows), piece(s_up_ref, s_lo_ref, row)
        )
        state_ref[pl.ds(row, channels, stride=rows), :] = own
        put(halo + row, own, side_lanes(own_side, edge, 0, row))
    for row in range(halo):
        place = rows - halo + row
        put(
            row,
            piece(above_up_ref, above_lo_ref, place),
            side_lanes(above_side, edge, 0, place),
        )
        put(
            halo + rows + row,
            piece(below_up_ref, below_lo_ref, row),
            side_lanes(below_side, edge, 0, row),
        )

    def put_adj(index, own, beyond):
        adj_ref[index, :, :cols] = own
        adj_ref[index, :, cols:] = beyond

    _, (edge, low) = layout(rows, depth)
    own_side = side_ref[...].astype(f32)
    above_side, below_side = strips_of(above_ref, depth), strips_of(below_ref, depth)
    for row in range(rows):
        put_adj(
            halo + row, row_of(q_ref, row, channels, rows), side_lanes(own_side, edge, low, row)
        )
    for row in range(depth):
        place = rows - depth + row
        put_adj(
            halo - depth + row,
            above_ref[depth + row].astype(f32),
            side_lanes(above_side, edge, low, place),
        )
        put_adj(
            halo + rows + row,
            below_ref[depth + row].astype(f32),
            side_lanes(below_side, edge, low, row),
        )

    for layer in range(depth):
        now, later = (a_ref, a2_ref) if layer % 2 == 0 else (a2_ref, a_ref)
        kept_ref[layer] = now[pl.ds(halo, rows)]

        def step(first, count, layer=layer, now=now, later=later):
            states = x_ref[pl.ds(first, count)]
            done = []
            for place, z in enumerate(convolved_rows(w_ref[layer], now, first, count)):
                gain = mask * (step_size * row_flag(first + place, halo, rows, up, down))
                t = jnp.tanh(z)
                done.append((gain * (1.0 - t * t), states[place] + gain * t))
            for place, (slope, x) in enumerate(done):
                slope_ref[layer, first + place] = slope
                if layer < depth - 1:
                    x_ref[first + place] = x
                    later[first + place] = x.astype(bf16)

        row_blocks(layer + 1, total - layer - 1, step)

    for layer in reversed(range(depth)):
        reach = layer + 1

        def source(first, count, layer=layer):
            part = pl.ds(first, count)
            src_ref[part] = (adj_ref[part] * slope_ref[layer, part]).astype(bf16)

        row_blocks(halo - reach, halo + rows + reach, source, 2)

        def back(first, count, layer=layer):
            adjoints = adj_ref[pl.ds(first, count)]
            moved = convolved_rows(wt_ref[layer], src_ref, first, count)
            for place in range(count):
                adj_ref[first + place] = adjoints[place] + moved[place]

        row_blocks(halo - layer, halo + rows + layer, back)
        sent_ref[layer] = src_ref[pl.ds(halo - 1, rows + 2), :, :cols]
    for row in range(rows):
        value = adj_ref[halo + row, :, :cols]
        g_ref[row] = value
        ref, place = piece_of(g_up_ref, g_lo_ref, row, rows)
        ref[place] = value.astype(bf16)


def grad_body(kept_ref, sent_ref, grad_ref, *, channels, rows, depth):
    lanes = kept_ref.shape[3]
    cols = lanes // 2
    for layer in range(depth):
        columns = []
        for row in range(rows):
            a = kept_ref[layer, row].astype(f32)
            columns.append(
                jnp.concatenate(
                    [
                        pltpu.roll(a, 1, 1)[:, :cols],
                        a[:, :cols],
                        pltpu.roll(a, lanes - 1, 1)[:, :cols],
                    ],
                    0,
                ).astype(bf16)
            )
        sources = [
            sent_ref[layer, pl.ds(row, 3)].reshape(3 * channels, cols) for row in range(rows)
        ]
        grad = lax.dot_general(
            jnp.concatenate(sources, 1),
            jnp.concatenate(columns, 1),
            (((1,), (1,)), ((), ())),
            preferred_element_type=f32,
        )
        for tap in range(3):
            grad_ref[layer, :, pl.ds(tap * 3 * channels, 3 * channels)] = grad[
                (2 - tap) * channels : (3 - tap) * channels
            ]


def last_body(q_ref, *refs, channels, rows):
    out_ref = refs[-1]
    uppers, lowers = refs[: len(refs) // 2], refs[len(refs) // 2 : -1]
    last = lax.axis_index("layer") == lax.axis_size("layer") - 1
    half = rows // 2
    for row in range(rows):
        arrived, place = (uppers, row) if row < half else (lowers, row - half)
        value = sum(ref[place].astype(f32) for ref in arrived)
        value = jnp.where(last, row_of(q_ref, row, channels, rows), value)
        out_ref[pl.ds(row, channels, stride=rows), :] = value


def shifted(array, axis, by):
    count = lax.axis_size(axis)
    pairs = [(i, i + by) for i in range(count) if 0 <= i + by < count]
    return lax.ppermute(array, axis, pairs)


def from_sides(array):
    if lax.axis_size("col") == 2:
        other = lax.ppermute(array, "col", [(0, 1), (1, 0)])
        return other, other
    return shifted(array, "col", 1), shifted(array, "col", -1)


def total_over_tiles(grads):
    rows, cols = lax.axis_size("row"), lax.axis_size("col")
    depth = grads.shape[0]
    half = depth // 2
    odd = lax.axis_index("row") % 2 == 1
    sent = jnp.where(odd, grads[:half], grads[half:])
    own = jnp.where(odd, grads[half:], grads[:half])
    pair = [(r, r ^ 1) for r in range(rows)]
    value = own + lax.ppermute(sent, "row", pair)

    flips = [(1 << bit, 0) for bit in range(1, rows.bit_length() - 1)]
    flips += [(0, 1 << bit) for bit in range(cols.bit_length() - 1)]
    for even, uneven in zip(flips, flips[::-1]):
        pairs = []
        for r in range(rows):
            row_by, col_by = uneven if r % 2 else even
            pairs += [
                (r * cols + c, (r ^ row_by) * cols + (c ^ col_by)) for c in range(cols)
            ]
        rounded = value.astype(bf16)
        arrived = lax.ppermute(rounded, ("row", "col"), pairs)
        value = rounded.astype(f32) + arrived.astype(f32)
    other = lax.ppermute(value, "row", pair)
    first = jnp.where(odd, other, value)
    second = jnp.where(odd, value, other)
    return jnp.concatenate([first, second], 0)


def local(c_states, c_adjoints, weights):
    groups = lax.axis_size("layer")
    channels, rows, cols = c_states.shape[1:]
    depth = weights.shape[0]
    flat = (channels * rows, cols)
    c_flat, q_flat = c_states.reshape(flat), c_adjoints.reshape(flat)
    sizes = dict(channels=channels, rows=rows)
    tile_f = jax.ShapeDtypeStruct((rows, channels, cols), f32)

    strip_f = jax.ShapeDtypeStruct((channels, cols), f32)
    wide_b = jax.ShapeDtypeStruct((channels, 2 * cols), bf16)
    half = rows // 2
    more_f, upper_b, lower_b, message_b = (
        jax.ShapeDtypeStruct((count, channels, cols), kind)
        for count, kind in (
            (rows + 1, f32), (half + 1, bf16), (half, bf16), (2 * depth + 2, bf16)
        )
    )

    edges = call(functools.partial(strip_body, depth=depth, **sizes), wide_b)(c_flat, q_flat)
    left, right = from_sides(edges)
    top, bottom, side = call(
        functools.partial(message_body, depth=depth, **sizes), (message_b, message_b, wide_b)
    )(c_flat, q_flat, left, right)
    above = shifted(bottom, "row", 1)
    below = shifted(top, "row", -1)

    taps = weights.reshape(depth, channels, 3, 3, channels)
    w_fwd = jnp.transpose(taps, (0, 3, 1, 2, 4)).reshape(depth, 3 * channels, 3 * channels)
    later_taps, _ = lax.optimization_barrier((taps, top))
    w_back = jnp.transpose(later_taps[:, :, ::-1, ::-1, :], (0, 3, 4, 2, 1)).reshape(
        depth, 3 * channels, 3 * channels
    )
    w_fwd, w_back = lax.optimization_barrier((w_fwd, w_back))
    coarse = step_size * jnp.sum(weights[0].astype(f32).reshape(channels, 9, channels), axis=1)
    high = coarse.astype(bf16)
    low = (coarse - high.astype(f32)).astype(bf16)
    m_fwd = jnp.concatenate([high, low, high], 1)
    m_back = jnp.concatenate([high.T, low.T, high.T], 1)

    lanes = 2 * cols
    mac = 2 * 9 * channels * channels * lanes
    total = rows + 2 * depth
    f, f_upper, f_lower, strip = call(
        functools.partial(first_body, depth=depth, **sizes),
        (more_f, upper_b, lower_b, strip_f),
        [
            pltpu.VMEM((total, channels, lanes), f32),
            pltpu.VMEM((total, channels, lanes), bf16),
            pltpu.VMEM((total, channels, lanes), bf16),
        ],
        flops=mac * 44,
    )(c_flat, above, below, side, w_fwd)

    def chain(pieces, target, matrix, order):
        sendings = [piece[0] for piece in pieces]
        arrivals = []
        for turn, hop in enumerate(order):
            arrived = [lax.ppermute(sending, "layer", [hop]) for sending in sendings]
            arrivals.append(arrived)
            if turn < len(order) - 1:
                sendings = [
                    call(
                        functools.partial(hop_body, start=start, **sizes),
                        jax.ShapeDtypeStruct(value.shape, bf16),
                        flops=10**10,
                    )(value, *base, target, matrix)
                    for value, (_, start, base) in zip(arrived, pieces)
                ]
        return [list(piece) for piece in zip(*arrivals)]

    uppers, lowers = chain(
        ((f_upper, 0, (c_flat, strip)), (f_lower, half, (c_flat,))),
        f,
        m_fwd,
        [(k, k + 1) for k in range(groups - 1)],
    )
    tiles = []
    for start, kind, strips, arrived in (
        (0, upper_b, (strip,), uppers),
        (half, lower_b, (), lowers),
    ):
        s = call(
            functools.partial(settle_body, start=start, strips=len(strips), **sizes), kind
        )(c_flat, *strips, *arrived)
        tiles.append((s, shifted(s, "row", 1), shifted(s, "row", -1)))
    pieces = [part for parts in zip(*tiles) for part in parts]

    total = rows + 4 * depth
    state, g, g_upper, g_lower, kept, sources = call(
        functools.partial(second_body, depth=depth, **sizes),
        (
            jax.ShapeDtypeStruct(flat, f32),
            tile_f,
            lower_b,
            lower_b,
            jax.ShapeDtypeStruct((depth, rows, channels, lanes), bf16),
            jax.ShapeDtypeStruct((depth, rows + 2, channels, cols), bf16),
        ),
        [
            pltpu.VMEM((total, channels, lanes), f32),
            pltpu.VMEM((total, channels, lanes), bf16),
            pltpu.VMEM((total, channels, lanes), bf16),
            pltpu.VMEM((depth, total, channels, lanes), f32),
            pltpu.VMEM((total, channels, lanes), f32),
            pltpu.VMEM((total, channels, lanes), bf16),
        ],
        flops=mac * 120,
    )(c_flat, q_flat, *pieces, above, below, side, w_fwd, w_back)
    uppers, lowers = chain(
        ((g_upper, 0, (q_flat,)), (g_lower, half, (q_flat,))),
        g,
        m_back,
        [(k, k - 1) for k in range(groups - 1, 0, -1)],
    )
    grads = call(
        functools.partial(grad_body, depth=depth, **sizes),
        jax.ShapeDtypeStruct((depth, channels, 9 * channels), f32),
        flops=10**9,
    )(kept, sources)
    weight_grads = total_over_tiles(grads)
    adjoint = call(
        functools.partial(last_body, **sizes), jax.ShapeDtypeStruct(flat, f32), flops=10**10
    )(q_flat, *uppers, *lowers)
    return state.reshape(c_states.shape), adjoint.reshape(c_states.shape), weight_grads


def solution(mesh):
    placed = (
        P("layer", None, "row", "col"),
        P("layer", None, "row", "col"),
        P("layer", None, None),
    )
    return jax.shard_map(
        local, mesh=mesh, in_specs=placed, out_specs=placed, check_vma=False
    )
```

```python
import functools

import jax
import jax.numpy as jnp
from jax import lax
from jax.experimental import pallas as pl
from jax.experimental.pallas import tpu as pltpu
from jax.sharding import PartitionSpec as P

step_size = 0.2
VMEM_BYTES = 40 * 1024 * 1024
f32 = jnp.float32
bf16 = jnp.bfloat16


def call(body, out_shape, scratch=(), flops=0, moved=0, **more):
    return pl.pallas_call(
        body,
        out_shape=out_shape,
        scratch_shapes=list(scratch),
        cost_estimate=pl.CostEstimate(
            flops=int(flops), bytes_accessed=int(moved), transcendentals=0
        ),
        compiler_params=pltpu.CompilerParams(vmem_limit_bytes=VMEM_BYTES),
        **more,
    )


def piece_of(upper, lower, row, rows):
    half = rows // 2
    if row < half:
        return upper, row
    return (lower, row - half) if row < rows else (upper, half)


def row_of(ref, row, channels, rows):
    return ref[pl.ds(row, channels, stride=rows), :]


def lanes_of(shape):
    return lax.broadcasted_iota(jnp.int32, shape, 1)


def slots(shape, low, width, count):
    return (lanes_of(shape) - low + width * count) // width - count


def fold_edges(rows_list, edge, low, total):
    doubled = total.shape[1] > rows_list[0].shape[1]
    cols = rows_list[0].shape[1]
    slot = slots(total.shape, low, 2 * edge, len(rows_list))
    for place, row in enumerate(rows_list):
        wide = jnp.concatenate([row, row], 1) if doubled else row
        turned = pltpu.roll(wide, (low + 2 * edge * place + edge - cols) % wide.shape[1], 1)
        total = jnp.where(slot == place, turned, total)
    return total


def join_edges(from_left, from_right, left, right, edges):
    lanes = lanes_of(from_left.shape)
    far = jnp.zeros(lanes.shape, jnp.bool_)
    for edge, low, high in edges:
        inside = (lanes >= low) & (lanes < high)
        far = far | (inside & ((lanes - low) % (2 * edge) >= edge))
    return jnp.where(far, from_right.astype(f32) * right, from_left.astype(f32) * left)


def side_lanes(joined, edge, low, place):
    lanes = joined.shape[1]
    turned = pltpu.roll(joined, (2 * lanes - (low + 2 * edge * place + edge)) % lanes, 1)
    if lanes == 128:
        return turned
    front, back = turned[:, :128], turned[:, lanes - 128 :]
    return jnp.where(lanes_of(front.shape) < 64, front, back)


def convolved(weights, slab):
    channels = slab.shape[1]
    lanes = slab.shape[2]
    product = jnp.dot(
        weights, slab.reshape(3 * channels, lanes), preferred_element_type=f32
    )
    return (
        pltpu.roll(product[:channels], 1, 1)
        + product[channels : 2 * channels]
        + pltpu.roll(product[2 * channels :], lanes - 1, 1)
    )


def flags():
    row, col = lax.axis_index("row"), lax.axis_index("col")
    up = (row > 0).astype(f32)
    down = (row < lax.axis_size("row") - 1).astype(f32)
    left = (col > 0).astype(f32)
    right = (col < lax.axis_size("col") - 1).astype(f32)
    return up, down, left, right


def even_row():
    return lax.axis_index("row") % 2 == 0


def lane_mask(cols, left, right):
    lanes = lax.broadcasted_iota(jnp.int32, (1, 2 * cols), 1)
    return jnp.where(lanes < cols, 1.0, jnp.where(lanes < cols + cols // 2, right, left))


def layout(rows, depth):
    state_edge, adjoint_edge = 3 * depth, depth
    return (state_edge, 0), (adjoint_edge, 2 * state_edge * rows)


def strip_body(
    c_hbm, q_hbm, edge_ref, c_ref, q_ref, arrived, *, channels, rows, depth
):
    copies = [
        pltpu.make_async_copy(source, target, arrived.at[place])
        for place, (source, target) in enumerate(((c_hbm, c_ref), (q_hbm, q_ref)))
    ]
    for copy in copies:
        copy.start()
    for copy in copies:
        copy.wait()
    total = jnp.zeros(edge_ref.shape, f32)
    for ref, (edge, low) in zip((c_ref, q_ref), layout(rows, depth)):
        image = [row_of(ref, row, channels, rows) for row in range(rows)]
        total = fold_edges(image, edge, low, total)
    edge_ref[...] = total.astype(bf16)


def message_body(
    c_ref, q_ref, left_ref, right_ref, pair_ref, cross_ref, side_ref, *, channels, rows, depth
):
    cols = c_ref.shape[1]
    _, _, left, right = flags()
    (c_edge, _), (q_edge, middle) = layout(rows, depth)
    edges = ((c_edge, 0, middle), (q_edge, middle, 2 * cols))
    side = join_edges(left_ref[...], right_ref[...], left, right, edges).astype(bf16)
    side_ref[...] = side
    even = even_row()
    for which, ref in enumerate((c_ref, q_ref)):
        for row in range(depth):
            place = which * depth + row
            top = row_of(ref, row, channels, rows)
            bottom = row_of(ref, rows - depth + row, channels, rows)
            pair_ref[place] = jnp.where(even, bottom, top).astype(bf16)
            cross_ref[place] = jnp.where(even, top, bottom).astype(bf16)
    for half in range(2):
        part = side[:, half * cols : (half + 1) * cols]
        pair_ref[2 * depth + half] = part
        cross_ref[2 * depth + half] = part


class Beside:
    def __init__(self, pair_ref, cross_ref):
        self.pair, self.cross, self.even = pair_ref, cross_ref, even_row()

    def above(self, place):
        return jnp.where(
            self.even, self.cross[place].astype(f32), self.pair[place].astype(f32)
        )

    def below(self, place):
        return jnp.where(
            self.even, self.pair[place].astype(f32), self.cross[place].astype(f32)
        )


def strips_of(get, depth):
    return jnp.concatenate([get(2 * depth), get(2 * depth + 1)], 1)


def row_blocks(low, high, body, size=6):
    turns, rest = divmod(high - low, size)

    def turn(number, carry):
        body(low + size * number, size)
        return carry

    if turns > 0:
        lax.fori_loop(0, turns, turn, 0)
    if rest > 0:
        body(low + size * turns, rest)


def convolved_rows(weights, ref, first, count):
    slab = ref[pl.ds(first - 1, count + 2)]
    return [convolved(weights, slab[place : place + 3]) for place in range(count)]


def row_flag(index, halo, rows, up, down):
    return jnp.where(index < halo, up, jnp.where(index >= halo + rows, down, 1.0))


def first_body(
    c_ref, pair_ref, cross_ref, side_ref, w_ref, f_ref, upper_ref, lower_ref, strip_ref, x_ref, a_ref, a2_ref,
    *, channels, rows, depth,
):
    cols = c_ref.shape[1]
    up, down, left, right = flags()
    mask = lane_mask(cols, left, right)
    halo = depth

    def put(index, own, beyond):
        x_ref[index, :, :cols] = own
        x_ref[index, :, cols:] = beyond
        a_ref[index, :, :cols] = own.astype(bf16)
        a_ref[index, :, cols:] = beyond.astype(bf16)

    (edge, low), _ = layout(rows, depth)
    own_side = side_ref[...].astype(f32)
    image = []
    for row in range(rows):
        beyond = side_lanes(own_side, edge, low, row)
        image.append(beyond)
        put(halo + row, row_of(c_ref, row, channels, rows), beyond)
    strip_ref[...] = fold_edges(image, 2 * depth, 0, jnp.zeros(strip_ref.shape, f32))
    beside = Beside(pair_ref, cross_ref)
    above_side, below_side = strips_of(beside.above, depth), strips_of(beside.below, depth)
    for row in range(depth):
        place = rows - depth + row
        put(row, beside.above(row), side_lanes(above_side, edge, low, place))
        put(halo + rows + row, beside.below(row), side_lanes(below_side, edge, low, row))

    total = rows + 2 * halo
    for layer in range(depth):
        now, later = (a_ref, a2_ref) if layer % 2 == 0 else (a2_ref, a_ref)

        def step(first, count, layer=layer, now=now, later=later):
            states = x_ref[pl.ds(first, count)]
            done = []
            for place, z in enumerate(convolved_rows(w_ref[layer], now, first, count)):
                gain = mask * (step_size * row_flag(first + place, halo, rows, up, down))
                done.append(states[place] + gain * jnp.tanh(z))
            for place, x in enumerate(done):
                x_ref[first + place] = x
                if layer < depth - 1:
                    later[first + place] = x.astype(bf16)

        row_blocks(layer + 1, total - layer - 1, step)
    image = [x_ref[halo + row, :, cols:] for row in range(rows)]
    values = [x_ref[halo + row, :, :cols] for row in range(rows)]
    values.append(fold_edges(image, 2 * depth, 0, jnp.zeros(strip_ref.shape, f32)))
    for row, value in enumerate(values):
        f_ref[row] = value
        ref, place = piece_of(upper_ref, lower_ref, row, rows)
        ref[place] = value.astype(bf16)


def hop_body(s_ref, c_ref, *refs, start, channels, rows):
    f_ref, m_ref, out_ref = refs[-3:]
    count = rows // 2
    work = [(start + row, row_of(c_ref, start + row, channels, rows)) for row in range(count)]
    work += [(rows, ref[...]) for ref in refs[:-3]]
    for place, (row, base) in enumerate(work):
        e = s_ref[place].astype(f32) - base
        high = e.astype(bf16)
        low = (e - high.astype(f32)).astype(bf16)
        stacked = jnp.concatenate([high, high, low], 0)
        moved = jnp.dot(m_ref[...], stacked, preferred_element_type=f32)
        out_ref[place] = (f_ref[row] + e + moved).astype(bf16)


def settle_body(c_ref, strip_ref, *refs, channels, rows):
    s_ref = refs[-1]
    uppers, lowers = refs[: len(refs) // 2], refs[len(refs) // 2 : -1]
    first = lax.axis_index("layer") == 0
    base = [row_of(c_ref, row, channels, rows) for row in range(rows)] + [strip_ref[...]]
    for row in range(rows + 1):
        value = 0.0
        for upper, lower in zip(uppers, lowers):
            ref, place = piece_of(upper, lower, row, rows)
            value = value + ref[place].astype(f32)
        s_ref[row] = jnp.where(first, base[row], value).astype(bf16)


def second_body(
    c_ref, q_ref, s_ref, s_pair_ref, s_cross_ref, pair_ref, cross_ref, side_ref, w_ref, wt_ref,
    state_ref, g_ref, g_up_ref, g_lo_ref, kept_ref, sent_ref,
    x_ref, a_ref, a2_ref, slope_ref, adj_ref, src_ref,
    *, channels, rows, depth,
):
    cols = c_ref.shape[1]
    up, down, left, right = flags()
    mask = lane_mask(cols, left, right)
    halo = 2 * depth
    total = rows + 2 * halo
    first = lax.axis_index("layer") == 0

    def put(index, own, beyond):
        x_ref[index, :, :cols] = own
        x_ref[index, :, cols:] = beyond
        a_ref[index, :, :cols] = own.astype(bf16)
        a_ref[index, :, cols:] = beyond.astype(bf16)

    edge = 2 * depth

    beside = Beside(s_pair_ref, s_cross_ref)
    own_side = s_ref[rows].astype(f32)
    above_side, below_side = beside.above(rows), beside.below(rows)
    for row in range(rows):
        own = jnp.where(first, row_of(c_ref, row, channels, rows), s_ref[row].astype(f32))
        state_ref[pl.ds(row, channels, stride=rows), :] = own
        put(halo + row, own, side_lanes(own_side, edge, 0, row))
    for row in range(halo):
        place = rows - halo + row
        put(
            row,
            beside.above(place),
            side_lanes(above_side, edge, 0, place),
        )
        put(
            halo + rows + row,
            beside.below(row),
            side_lanes(below_side, edge, 0, row),
        )

    def put_adj(index, own, beyond):
        adj_ref[index, :, :cols] = own
        adj_ref[index, :, cols:] = beyond

    _, (edge, low) = layout(rows, depth)
    own_side = side_ref[...].astype(f32)
    beside = Beside(pair_ref, cross_ref)
    above_side, below_side = strips_of(beside.above, depth), strips_of(beside.below, depth)
    for row in range(rows):
        put_adj(
            halo + row, row_of(q_ref, row, channels, rows), side_lanes(own_side, edge, low, row)
        )
    for row in range(depth):
        place = rows - depth + row
        put_adj(
            halo - depth + row,
            beside.above(depth + row),
            side_lanes(above_side, edge, low, place),
        )
        put_adj(
            halo + rows + row,
            beside.below(depth + row),
            side_lanes(below_side, edge, low, row),
        )

    for layer in range(depth):
        now, later = (a_ref, a2_ref) if layer % 2 == 0 else (a2_ref, a_ref)
        kept_ref[layer] = now[pl.ds(halo, rows)]

        def step(first, count, layer=layer, now=now, later=later):
            states = x_ref[pl.ds(first, count)]
            done = []
            for place, z in enumerate(convolved_rows(w_ref[layer], now, first, count)):
                gain = mask * (step_size * row_flag(first + place, halo, rows, up, down))
                t = jnp.tanh(z)
                done.append((gain * (1.0 - t * t), states[place] + gain * t))
            for place, (slope, x) in enumerate(done):
                slope_ref[layer, first + place] = slope
                if layer < depth - 1:
                    x_ref[first + place] = x
                    later[first + place] = x.astype(bf16)

        row_blocks(layer + 1, total - layer - 1, step)

    for layer in reversed(range(depth)):
        reach = layer + 1

        def source(first, count, layer=layer):
            part = pl.ds(first, count)
            src_ref[part] = (adj_ref[part] * slope_ref[layer, part]).astype(bf16)

        row_blocks(halo - reach, halo + rows + reach, source, 2)

        def back(first, count, layer=layer):
            adjoints = adj_ref[pl.ds(first, count)]
            moved = convolved_rows(wt_ref[layer], src_ref, first, count)
            for place in range(count):
                adj_ref[first + place] = adjoints[place] + moved[place]

        row_blocks(halo - layer, halo + rows + layer, back)
        sent_ref[layer] = src_ref[pl.ds(halo - 1, rows + 2), :, :cols]
    for row in range(rows):
        value = adj_ref[halo + row, :, :cols]
        g_ref[row] = value
        ref, place = piece_of(g_up_ref, g_lo_ref, row, rows)
        ref[place] = value.astype(bf16)


def grad_body(kept_ref, sent_ref, grad_ref, *, channels, rows, depth):
    lanes = kept_ref.shape[3]
    cols = lanes // 2
    for layer in range(depth):
        columns = []
        for row in range(rows):
            a = kept_ref[layer, row].astype(f32)
            columns.append(
                jnp.concatenate(
                    [
                        pltpu.roll(a, 1, 1)[:, :cols],
                        a[:, :cols],
                        pltpu.roll(a, lanes - 1, 1)[:, :cols],
                    ],
                    0,
                ).astype(bf16)
            )
        sources = [
            sent_ref[layer, pl.ds(row, 3)].reshape(3 * channels, cols) for row in range(rows)
        ]
        grad = lax.dot_general(
            jnp.concatenate(sources, 1),
            jnp.concatenate(columns, 1),
            (((1,), (1,)), ((), ())),
            preferred_element_type=f32,
        )
        for tap in range(3):
            grad_ref[layer, :, pl.ds(tap * 3 * channels, 3 * channels)] = grad[
                (2 - tap) * channels : (3 - tap) * channels
            ]


def last_body(q_ref, *refs, channels, rows):
    out_ref = refs[-1]
    uppers, lowers = refs[: len(refs) // 2], refs[len(refs) // 2 : -1]
    last = lax.axis_index("layer") == lax.axis_size("layer") - 1
    half = rows // 2
    for row in range(rows):
        arrived, place = (uppers, row) if row < half else (lowers, row - half)
        value = sum(ref[place].astype(f32) for ref in arrived)
        value = jnp.where(last, row_of(q_ref, row, channels, rows), value)
        out_ref[pl.ds(row, channels, stride=rows), :] = value


def shifted(array, axis, by):
    count = lax.axis_size(axis)
    pairs = [(i, i + by) for i in range(count) if 0 <= i + by < count]
    return lax.ppermute(array, axis, pairs)


def exchanged(to_pair, to_cross):
    rows = lax.axis_size("row")
    pairs = [(r, r ^ 1) for r in range(rows)]
    crossing = [(r, r + 1 if r % 2 else r - 1) for r in range(1, rows - 1)]
    return lax.ppermute(to_pair, "row", pairs), lax.ppermute(to_cross, "row", crossing)


def from_sides(array):
    if lax.axis_size("col") == 2:
        other = lax.ppermute(array, "col", [(0, 1), (1, 0)])
        return other, other
    return shifted(array, "col", 1), shifted(array, "col", -1)


def total_over_tiles(grads):
    rows, cols = lax.axis_size("row"), lax.axis_size("col")
    depth = grads.shape[0]
    half = depth // 2
    odd = lax.axis_index("row") % 2 == 1
    sent = jnp.where(odd, grads[:half], grads[half:])
    own = jnp.where(odd, grads[half:], grads[:half])
    pair = [(r, r ^ 1) for r in range(rows)]
    value = own + lax.ppermute(sent, "row", pair)

    flips = [(1 << bit, 0) for bit in range(1, rows.bit_length() - 1)]
    flips += [(0, 1 << bit) for bit in range(cols.bit_length() - 1)]
    for even, uneven in zip(flips, flips[::-1]):
        pairs = []
        for r in range(rows):
            row_by, col_by = uneven if r % 2 else even
            pairs += [
                (r * cols + c, (r ^ row_by) * cols + (c ^ col_by)) for c in range(cols)
            ]
        rounded = value.astype(bf16)
        arrived = lax.ppermute(rounded, ("row", "col"), pairs)
        value = rounded.astype(f32) + arrived.astype(f32)
    other = lax.ppermute(value, "row", pair)
    first = jnp.where(odd, other, value)
    second = jnp.where(odd, value, other)
    return jnp.concatenate([first, second], 0)


def local(c_states, c_adjoints, weights):
    groups = lax.axis_size("layer")
    channels, rows, cols = c_states.shape[1:]
    depth = weights.shape[0]
    flat = (channels * rows, cols)
    c_flat, q_flat = c_states.reshape(flat), c_adjoints.reshape(flat)
    sizes = dict(channels=channels, rows=rows)
    tile_f = jax.ShapeDtypeStruct((rows, channels, cols), f32)

    strip_f = jax.ShapeDtypeStruct((channels, cols), f32)
    wide_b = jax.ShapeDtypeStruct((channels, 2 * cols), bf16)
    half = rows // 2
    more_f, more_b, upper_b, lower_b, message_b = (
        jax.ShapeDtypeStruct((count, channels, cols), kind)
        for count, kind in (
            (rows + 1, f32), (rows + 1, bf16), (half + 1, bf16), (half, bf16),
            (2 * depth + 2, bf16),
        )
    )

    edges = call(
        functools.partial(strip_body, depth=depth, **sizes),
        wide_b,
        [pltpu.VMEM(flat, f32), pltpu.VMEM(flat, f32), pltpu.SemaphoreType.DMA((2,))],
        in_specs=[pl.BlockSpec(memory_space=pltpu.HBM)] * 2,
    )(c_flat, q_flat)
    left, right = from_sides(edges)
    to_pair, to_cross, side = call(
        functools.partial(message_body, depth=depth, **sizes), (message_b, message_b, wide_b)
    )(c_flat, q_flat, left, right)
    pair, cross = exchanged(to_pair, to_cross)

    taps = weights.reshape(depth, channels, 3, 3, channels)
    w_fwd = jnp.transpose(taps, (0, 3, 1, 2, 4)).reshape(depth, 3 * channels, 3 * channels)
    later_taps, _ = lax.optimization_barrier((taps, to_pair))
    w_back = jnp.transpose(later_taps[:, :, ::-1, ::-1, :], (0, 3, 4, 2, 1)).reshape(
        depth, 3 * channels, 3 * channels
    )
    w_fwd, w_back = lax.optimization_barrier((w_fwd, w_back))
    coarse = step_size * jnp.sum(weights[0].astype(f32).reshape(channels, 9, channels), axis=1)
    high = coarse.astype(bf16)
    low = (coarse - high.astype(f32)).astype(bf16)
    m_fwd = jnp.concatenate([high, low, high], 1)
    m_back = jnp.concatenate([high.T, low.T, high.T], 1)

    lanes = 2 * cols
    mac = 2 * 9 * channels * channels * lanes
    total = rows + 2 * depth
    f, f_upper, f_lower, strip = call(
        functools.partial(first_body, depth=depth, **sizes),
        (more_f, upper_b, lower_b, strip_f),
        [
            pltpu.VMEM((total, channels, lanes), f32),
            pltpu.VMEM((total, channels, lanes), bf16),
            pltpu.VMEM((total, channels, lanes), bf16),
        ],
        flops=mac * 44,
    )(c_flat, pair, cross, side, w_fwd)

    def chain(pieces, target, matrix, order):
        sendings = [piece[0] for piece in pieces]
        arrivals = []
        for turn, hop in enumerate(order):
            arrived = [lax.ppermute(sending, "layer", [hop]) for sending in sendings]
            arrivals.append(arrived)
            if turn < len(order) - 1:
                sendings = [
                    call(
                        functools.partial(hop_body, start=start, **sizes),
                        jax.ShapeDtypeStruct(value.shape, bf16),
                        flops=10**10,
                    )(value, *base, target, matrix)
                    for value, (_, start, base) in zip(arrived, pieces)
                ]
        return [list(piece) for piece in zip(*arrivals)]

    uppers, lowers = chain(
        ((f_upper, 0, (c_flat, strip)), (f_lower, half, (c_flat,))),
        f,
        m_fwd,
        [(k, k + 1) for k in range(groups - 1)],
    )
    s = call(functools.partial(settle_body, **sizes), more_b)(
        c_flat, strip, *uppers, *lowers
    )
    s_pair, s_cross = exchanged(s, s)

    total = rows + 4 * depth
    state, g, g_upper, g_lower, kept, sources = call(
        functools.partial(second_body, depth=depth, **sizes),
        (
            jax.ShapeDtypeStruct(flat, f32),
            tile_f,
            lower_b,
            lower_b,
            jax.ShapeDtypeStruct((depth, rows, channels, lanes), bf16),
            jax.ShapeDtypeStruct((depth, rows + 2, channels, cols), bf16),
        ),
        [
            pltpu.VMEM((total, channels, lanes), f32),
            pltpu.VMEM((total, channels, lanes), bf16),
            pltpu.VMEM((total, channels, lanes), bf16),
            pltpu.VMEM((depth, total, channels, lanes), f32),
            pltpu.VMEM((total, channels, lanes), f32),
            pltpu.VMEM((total, channels, lanes), bf16),
        ],
        flops=mac * 120,
    )(c_flat, q_flat, s, s_pair, s_cross, pair, cross, side, w_fwd, w_back)
    uppers, lowers = chain(
        ((g_upper, 0, (q_flat,)), (g_lower, half, (q_flat,))),
        g,
        m_back,
        [(k, k - 1) for k in range(groups - 1, 0, -1)],
    )
    grads = call(
        functools.partial(grad_body, depth=depth, **sizes),
        jax.ShapeDtypeStruct((depth, channels, 9 * channels), f32),
        flops=10**9,
    )(kept, sources)
    weight_grads = total_over_tiles(grads)
    adjoint = call(
        functools.partial(last_body, **sizes), jax.ShapeDtypeStruct(flat, f32), flops=10**10
    )(q_flat, *uppers, *lowers)
    return state.reshape(c_states.shape), adjoint.reshape(c_states.shape), weight_grads


def solution(mesh):
    placed = (
        P("layer", None, "row", "col"),
        P("layer", None, "row", "col"),
        P("layer", None, None),
    )
    return jax.shard_map(
        local, mesh=mesh, in_specs=placed, out_specs=placed, check_vma=False
    )
```

```python
import functools

import jax
import jax.numpy as jnp
from jax import lax
from jax.experimental import pallas as pl
from jax.experimental.pallas import tpu as pltpu
from jax.sharding import PartitionSpec as P

step_size = 0.2
VMEM_BYTES = 40 * 1024 * 1024
f32 = jnp.float32
bf16 = jnp.bfloat16


def call(body, out_shape, scratch=(), flops=0, moved=0):
    return pl.pallas_call(
        body,
        out_shape=out_shape,
        scratch_shapes=list(scratch),
        cost_estimate=pl.CostEstimate(
            flops=int(flops), bytes_accessed=int(moved), transcendentals=0
        ),
        compiler_params=pltpu.CompilerParams(vmem_limit_bytes=VMEM_BYTES),
    )


def row_of(ref, row, channels, rows):
    return ref[pl.ds(row, channels, stride=rows), :]


def lanes_of(shape):
    return lax.broadcasted_iota(jnp.int32, shape, 1)


def slots(shape, low, width, count):
    return (lanes_of(shape) - low + width * count) // width - count


def fold_edges(rows_list, edge, low, total):
    doubled = total.shape[1] > rows_list[0].shape[1]
    cols = rows_list[0].shape[1]
    slot = slots(total.shape, low, 2 * edge, len(rows_list))
    for place, row in enumerate(rows_list):
        wide = jnp.concatenate([row, row], 1) if doubled else row
        turned = pltpu.roll(wide, (low + 2 * edge * place + edge - cols) % wide.shape[1], 1)
        total = jnp.where(slot == place, turned, total)
    return total


def join_edges(from_left, from_right, left, right, edges):
    lanes = lanes_of(from_left.shape)
    far = jnp.zeros(lanes.shape, jnp.bool_)
    for edge, low, high in edges:
        inside = (lanes >= low) & (lanes < high)
        far = far | (inside & ((lanes - low) % (2 * edge) >= edge))
    return jnp.where(far, from_right.astype(f32) * right, from_left.astype(f32) * left)


def side_lanes(joined, edge, low, place):
    lanes = joined.shape[1]
    turned = pltpu.roll(joined, (2 * lanes - (low + 2 * edge * place + edge)) % lanes, 1)
    if lanes == 128:
        return turned
    front, back = turned[:, :128], turned[:, lanes - 128 :]
    return jnp.where(lanes_of(front.shape) < 64, front, back)


def convolved(weights, slab):
    channels = slab.shape[1]
    lanes = slab.shape[2]
    product = jnp.dot(
        weights, slab.reshape(3 * channels, lanes), preferred_element_type=f32
    )
    return (
        pltpu.roll(product[:channels], 1, 1)
        + product[channels : 2 * channels]
        + pltpu.roll(product[2 * channels :], lanes - 1, 1)
    )


def flags():
    row, col = lax.axis_index("row"), lax.axis_index("col")
    up = (row > 0).astype(f32)
    down = (row < lax.axis_size("row") - 1).astype(f32)
    left = (col > 0).astype(f32)
    right = (col < lax.axis_size("col") - 1).astype(f32)
    return up, down, left, right


def even_row():
    return lax.axis_index("row") % 2 == 0


def lane_mask(cols, left, right):
    lanes = lax.broadcasted_iota(jnp.int32, (1, 2 * cols), 1)
    return jnp.where(lanes < cols, 1.0, jnp.where(lanes < cols + cols // 2, right, left))


def layout(rows, depth):
    state_edge, adjoint_edge = 3 * depth, depth
    return (state_edge, 0), (adjoint_edge, 2 * state_edge * rows)


def strip_body(c_ref, q_ref, edge_ref, *, channels, rows, depth):
    total = jnp.zeros(edge_ref.shape, f32)
    for ref, (edge, low) in zip((c_ref, q_ref), layout(rows, depth)):
        image = [row_of(ref, row, channels, rows) for row in range(rows)]
        total = fold_edges(image, edge, low, total)
    edge_ref[...] = total.astype(bf16)


def message_body(
    c_ref, q_ref, left_ref, right_ref, pair_ref, cross_ref, side_ref, strip_ref,
    *, channels, rows, depth,
):
    cols = c_ref.shape[1]
    _, _, left, right = flags()
    (c_edge, _), (q_edge, middle) = layout(rows, depth)
    edges = ((c_edge, 0, middle), (q_edge, middle, 2 * cols))
    side = join_edges(left_ref[...], right_ref[...], left, right, edges).astype(bf16)
    side_ref[...] = side
    wide = side.astype(f32)
    image = [side_lanes(wide, c_edge, 0, row) for row in range(rows)]
    strip_ref[...] = fold_edges(image, 2 * depth, 0, jnp.zeros(strip_ref.shape, f32))
    even = even_row()
    for which, ref in enumerate((c_ref, q_ref)):
        for row in range(depth):
            place = which * depth + row
            top = row_of(ref, row, channels, rows)
            bottom = row_of(ref, rows - depth + row, channels, rows)
            pair_ref[place] = jnp.where(even, bottom, top).astype(bf16)
            cross_ref[place] = jnp.where(even, top, bottom).astype(bf16)
    for half in range(2):
        part = side[:, half * cols : (half + 1) * cols]
        pair_ref[2 * depth + half] = part
        cross_ref[2 * depth + half] = part


class Beside:
    def __init__(self, pair_ref, cross_ref):
        self.pair, self.cross, self.even = pair_ref, cross_ref, even_row()

    def above(self, place):
        return jnp.where(
            self.even, self.cross[place].astype(f32), self.pair[place].astype(f32)
        )

    def below(self, place):
        return jnp.where(
            self.even, self.pair[place].astype(f32), self.cross[place].astype(f32)
        )


def strips_of(get, depth):
    return jnp.concatenate([get(2 * depth), get(2 * depth + 1)], 1)


def row_blocks(low, high, body, turns=2):
    size, rest = divmod(high - low, turns)

    def turn(number, carry):
        body(low + size * number, size)
        return carry

    if size > 0:
        lax.fori_loop(0, turns, turn, 0)
    if rest > 0:
        body(low + size * turns, rest)


def convolved_rows(weights, ref, first, count):
    slab = ref[pl.ds(first - 1, count + 2)]
    return [convolved(weights, slab[place : place + 3]) for place in range(count)]


def row_flag(index, halo, rows, up, down):
    return jnp.where(index < halo, up, jnp.where(index >= halo + rows, down, 1.0))


def first_body(
    c_ref, pair_ref, cross_ref, side_ref, w_ref, out_ref, x_ref, a_ref, a2_ref,
    *, channels, rows, depth, sender,
):
    active = (lax.axis_index("layer") == 0) == sender

    @pl.when(jnp.logical_not(active))
    def nothing():
        out_ref[...] = jnp.zeros(out_ref.shape, out_ref.dtype)

    @pl.when(active)
    def run():
        first_pass(
            c_ref, pair_ref, cross_ref, side_ref, w_ref, out_ref, x_ref, a_ref, a2_ref,
            channels, rows, depth,
        )


def first_pass(
    c_ref, pair_ref, cross_ref, side_ref, w_ref, out_ref, x_ref, a_ref, a2_ref,
    channels, rows, depth,
):
    cols = c_ref.shape[1]
    up, down, left, right = flags()
    mask = lane_mask(cols, left, right)
    halo = depth

    def put(index, own, beyond):
        x_ref[index, :, :cols] = own
        x_ref[index, :, cols:] = beyond
        a_ref[index, :, :cols] = own.astype(bf16)
        a_ref[index, :, cols:] = beyond.astype(bf16)

    (edge, low), _ = layout(rows, depth)
    own_side = side_ref[...].astype(f32)
    for row in range(rows):
        own = row_of(c_ref, row, channels, rows)
        put(halo + row, own, side_lanes(own_side, edge, low, row))
    beside = Beside(pair_ref, cross_ref)
    above_side, below_side = strips_of(beside.above, depth), strips_of(beside.below, depth)
    for row in range(depth):
        place = rows - depth + row
        put(row, beside.above(row), side_lanes(above_side, edge, low, place))
        put(halo + rows + row, beside.below(row), side_lanes(below_side, edge, low, row))

    total = rows + 2 * halo
    for layer in range(depth):
        now, later = (a_ref, a2_ref) if layer % 2 == 0 else (a2_ref, a_ref)

        def step(first, count, layer=layer, now=now, later=later):
            states = x_ref[pl.ds(first, count)]
            done = []
            for place, z in enumerate(convolved_rows(w_ref[layer], now, first, count)):
                gain = mask * (step_size * row_flag(first + place, halo, rows, up, down))
                done.append(states[place] + gain * jnp.tanh(z))
            for place, x in enumerate(done):
                x_ref[first + place] = x
                if layer < depth - 1:
                    later[first + place] = x.astype(bf16)

        row_blocks(layer + 1, total - layer - 1, step)
    image = [x_ref[halo + row, :, cols:] for row in range(rows)]
    values = [x_ref[halo + row, :, :cols] for row in range(rows)]
    values.append(fold_edges(image, 2 * depth, 0, jnp.zeros((channels, cols), f32)))
    for row, value in enumerate(values):
        out_ref[row] = value.astype(out_ref.dtype)


def hop_body(s_ref, c_ref, *refs, channels, rows):
    f_ref, m_ref, out_ref = refs[-3:]
    base = [row_of(c_ref, row, channels, rows) for row in range(rows)]
    base += [ref[...] for ref in refs[:-3]]
    for row in range(len(base)):
        e = s_ref[row].astype(f32) - base[row]
        high = e.astype(bf16)
        low = (e - high.astype(f32)).astype(bf16)
        stacked = jnp.concatenate([high, high, low], 0)
        moved = jnp.dot(m_ref[...], stacked, preferred_element_type=f32)
        out_ref[row] = (f_ref[row] + e + moved).astype(bf16)


def settle_body(c_ref, strip_ref, *refs, channels, rows):
    arrived, s_ref = refs[:-1], refs[-1]
    first = lax.axis_index("layer") == 0
    base = [row_of(c_ref, row, channels, rows) for row in range(rows)] + [strip_ref[...]]
    for row in range(rows + 1):
        value = sum(ref[row].astype(f32) for ref in arrived)
        s_ref[row] = jnp.where(first, base[row], value).astype(bf16)


def second_body(
    c_ref, q_ref, s_ref, s_pair_ref, s_cross_ref, pair_ref, cross_ref, side_ref, w_ref, wt_ref,
    state_ref, g_ref, sending_ref, kept_ref, sent_ref,
    x_ref, a_ref, a2_ref, slope_ref, adj_ref, src_ref,
    *, channels, rows, depth,
):
    cols = c_ref.shape[1]
    up, down, left, right = flags()
    mask = lane_mask(cols, left, right)
    halo = 2 * depth
    total = rows + 2 * halo
    first = lax.axis_index("layer") == 0

    def put(index, own, beyond):
        x_ref[index, :, :cols] = own
        x_ref[index, :, cols:] = beyond
        a_ref[index, :, :cols] = own.astype(bf16)
        a_ref[index, :, cols:] = beyond.astype(bf16)

    edge = 2 * depth

    beside = Beside(s_pair_ref, s_cross_ref)
    own_side = s_ref[rows].astype(f32)
    above_side, below_side = beside.above(rows), beside.below(rows)
    for row in range(rows):
        own = jnp.where(first, row_of(c_ref, row, channels, rows), s_ref[row].astype(f32))
        state_ref[pl.ds(row, channels, stride=rows), :] = own
        put(halo + row, own, side_lanes(own_side, edge, 0, row))
    for row in range(halo):
        place = rows - halo + row
        put(
            row,
            beside.above(place),
            side_lanes(above_side, edge, 0, place),
        )
        put(
            halo + rows + row,
            beside.below(row),
            side_lanes(below_side, edge, 0, row),
        )

    def put_adj(index, own, beyond):
        adj_ref[index, :, :cols] = own
        adj_ref[index, :, cols:] = beyond

    _, (edge, low) = layout(rows, depth)
    own_side = side_ref[...].astype(f32)
    beside = Beside(pair_ref, cross_ref)
    above_side, below_side = strips_of(beside.above, depth), strips_of(beside.below, depth)
    for row in range(rows):
        put_adj(
            halo + row, row_of(q_ref, row, channels, rows), side_lanes(own_side, edge, low, row)
        )
    for row in range(depth):
        place = rows - depth + row
        put_adj(
            halo - depth + row,
            beside.above(depth + row),
            side_lanes(above_side, edge, low, place),
        )
        put_adj(
            halo + rows + row,
            beside.below(depth + row),
            side_lanes(below_side, edge, low, row),
        )

    for layer in range(depth):
        now, later = (a_ref, a2_ref) if layer % 2 == 0 else (a2_ref, a_ref)
        kept_ref[layer] = now[pl.ds(halo, rows)]

        def step(first, count, layer=layer, now=now, later=later):
            states = x_ref[pl.ds(first, count)]
            done = []
            for place, z in enumerate(convolved_rows(w_ref[layer], now, first, count)):
                gain = mask * (step_size * row_flag(first + place, halo, rows, up, down))
                t = jnp.tanh(z)
                done.append((gain * (1.0 - t * t), states[place] + gain * t))
            for place, (slope, x) in enumerate(done):
                slope_ref[layer, first + place] = slope
                if layer < depth - 1:
                    x_ref[first + place] = x
                    later[first + place] = x.astype(bf16)

        row_blocks(layer + 1, total - layer - 1, step)

    for layer in reversed(range(depth)):
        reach = layer + 1

        def source(first, count, layer=layer):
            part = pl.ds(first, count)
            src_ref[part] = (adj_ref[part] * slope_ref[layer, part]).astype(bf16)

        row_blocks(halo - reach, halo + rows + reach, source)

        def back(first, count, layer=layer):
            adjoints = adj_ref[pl.ds(first, count)]
            moved = convolved_rows(wt_ref[layer], src_ref, first, count)
            for place in range(count):
                adj_ref[first + place] = adjoints[place] + moved[place]

        row_blocks(halo - layer, halo + rows + layer, back)
        sent_ref[layer] = src_ref[pl.ds(halo - 1, rows + 2), :, :cols]
    for row in range(rows):
        value = adj_ref[halo + row, :, :cols]
        g_ref[row] = value
        sending_ref[row] = value.astype(bf16)


def grad_body(kept_ref, sent_ref, grad_ref, *, channels, rows, depth):
    lanes = kept_ref.shape[3]
    cols = lanes // 2
    for layer in range(depth):
        columns = []
        for row in range(rows):
            a = kept_ref[layer, row].astype(f32)
            columns.append(
                jnp.concatenate(
                    [
                        pltpu.roll(a, 1, 1)[:, :cols],
                        a[:, :cols],
                        pltpu.roll(a, lanes - 1, 1)[:, :cols],
                    ],
                    0,
                ).astype(bf16)
            )
        sources = [
            sent_ref[layer, pl.ds(row, 3)].reshape(3 * channels, cols) for row in range(rows)
        ]
        grad = lax.dot_general(
            jnp.concatenate(sources, 1),
            jnp.concatenate(columns, 1),
            (((1,), (1,)), ((), ())),
            preferred_element_type=f32,
        )
        for tap in range(3):
            grad_ref[layer, :, pl.ds(tap * 3 * channels, 3 * channels)] = grad[
                (2 - tap) * channels : (3 - tap) * channels
            ]


def last_body(q_ref, *refs, channels, rows):
    arrived, out_ref = refs[:-1], refs[-1]
    last = lax.axis_index("layer") == lax.axis_size("layer") - 1
    for row in range(rows):
        value = sum(ref[row].astype(f32) for ref in arrived)
        value = jnp.where(last, row_of(q_ref, row, channels, rows), value)
        out_ref[pl.ds(row, channels, stride=rows), :] = value


def shifted(array, axis, by):
    count = lax.axis_size(axis)
    pairs = [(i, i + by) for i in range(count) if 0 <= i + by < count]
    return lax.ppermute(array, axis, pairs)


def exchanged(to_pair, to_cross):
    rows = lax.axis_size("row")
    pairs = [(r, r ^ 1) for r in range(rows)]
    crossing = [(r, r + 1 if r % 2 else r - 1) for r in range(1, rows - 1)]
    return lax.ppermute(to_pair, "row", pairs), lax.ppermute(to_cross, "row", crossing)


def from_sides(array):
    if lax.axis_size("col") == 2:
        other = lax.ppermute(array, "col", [(0, 1), (1, 0)])
        return other, other
    return shifted(array, "col", 1), shifted(array, "col", -1)


def total_over_tiles(grads):
    rows, cols = lax.axis_size("row"), lax.axis_size("col")
    depth = grads.shape[0]
    half = depth // 2
    odd = lax.axis_index("row") % 2 == 1
    sent = jnp.where(odd, grads[:half], grads[half:])
    own = jnp.where(odd, grads[half:], grads[:half])
    pair = [(r, r ^ 1) for r in range(rows)]
    value = own + lax.ppermute(sent, "row", pair)

    flips = [(1 << bit, 0) for bit in range(1, rows.bit_length() - 1)]
    flips += [(0, 1 << bit) for bit in range(cols.bit_length() - 1)]
    for even, uneven in zip(flips, flips[::-1]):
        pairs = []
        for r in range(rows):
            row_by, col_by = uneven if r % 2 else even
            pairs += [
                (r * cols + c, (r ^ row_by) * cols + (c ^ col_by)) for c in range(cols)
            ]
        rounded = value.astype(bf16)
        arrived = lax.ppermute(rounded, ("row", "col"), pairs)
        value = rounded.astype(f32) + arrived.astype(f32)
    other = lax.ppermute(value, "row", pair)
    first = jnp.where(odd, other, value)
    second = jnp.where(odd, value, other)
    return jnp.concatenate([first, second], 0)


def local(c_states, c_adjoints, weights):
    groups = lax.axis_size("layer")
    channels, rows, cols = c_states.shape[1:]
    depth = weights.shape[0]
    flat = (channels * rows, cols)
    c_flat, q_flat = c_states.reshape(flat), c_adjoints.reshape(flat)
    sizes = dict(channels=channels, rows=rows)
    tile_f = jax.ShapeDtypeStruct((rows, channels, cols), f32)

    strip_f = jax.ShapeDtypeStruct((channels, cols), f32)
    wide_b = jax.ShapeDtypeStruct((channels, 2 * cols), bf16)
    more_f, more_b, message_b = (
        jax.ShapeDtypeStruct((count, channels, cols), kind)
        for count, kind in ((rows + 1, f32), (rows + 1, bf16), (2 * depth + 2, bf16))
    )
    flat_f = jax.ShapeDtypeStruct(flat, f32)
    edges = call(functools.partial(strip_body, depth=depth, **sizes), wide_b)(c_flat, q_flat)
    left, right = from_sides(edges)
    to_pair, to_cross, side, strip = call(
        functools.partial(message_body, depth=depth, **sizes),
        (message_b, message_b, wide_b, strip_f),
    )(c_flat, q_flat, left, right)
    pair, cross = exchanged(to_pair, to_cross)

    taps = weights.reshape(depth, channels, 3, 3, channels)
    w_fwd = jnp.transpose(taps, (0, 3, 1, 2, 4)).reshape(depth, 3 * channels, 3 * channels)
    later_taps, _ = lax.optimization_barrier((taps, to_pair))
    w_back = jnp.transpose(later_taps[:, :, ::-1, ::-1, :], (0, 3, 4, 2, 1)).reshape(
        depth, 3 * channels, 3 * channels
    )
    w_fwd, w_back = lax.optimization_barrier((w_fwd, w_back))
    coarse = step_size * jnp.sum(weights[0].astype(f32).reshape(channels, 9, channels), axis=1)
    high = coarse.astype(bf16)
    low = (coarse - high.astype(f32)).astype(bf16)
    m_fwd = jnp.concatenate([high, low, high], 1)
    m_back = jnp.concatenate([high.T, low.T, high.T], 1)

    lanes = 2 * cols
    mac = 2 * 9 * channels * channels * lanes
    total = rows + 2 * depth

    def first(kind, sender, *inputs):
        return call(
            functools.partial(first_body, depth=depth, sender=sender, **sizes),
            kind,
            [
                pltpu.VMEM((total, channels, lanes), f32),
                pltpu.VMEM((total, channels, lanes), bf16),
                pltpu.VMEM((total, channels, lanes), bf16),
            ],
            flops=mac * 44,
        )(*inputs)

    def hop(arrived, base, target, matrix):
        return call(
            functools.partial(hop_body, **sizes),
            jax.ShapeDtypeStruct(arrived.shape, bf16),
            flops=10**10,
        )(arrived, *base, target, matrix)

    inputs = (c_flat, pair, cross, side, w_fwd)
    sending = first(more_b, True, *inputs)
    inputs = lax.optimization_barrier((inputs, sending))[0]
    f = first(more_f, False, *inputs)
    arrivals = []
    for k in range(groups - 1):
        arrivals.append(lax.ppermute(sending, "layer", [(k, k + 1)]))
        if k < groups - 2:
            sending = hop(arrivals[-1], (c_flat, strip), f, m_fwd)
    s = call(functools.partial(settle_body, **sizes), more_b)(c_flat, strip, *arrivals)
    s_pair, s_cross = exchanged(s, s)

    total = rows + 4 * depth
    state, g, sending, kept, sources = call(
        functools.partial(second_body, depth=depth, **sizes),
        (
            flat_f,
            tile_f,
            jax.ShapeDtypeStruct(tile_f.shape, bf16),
            jax.ShapeDtypeStruct((depth, rows, channels, lanes), bf16),
            jax.ShapeDtypeStruct((depth, rows + 2, channels, cols), bf16),
        ),
        [
            pltpu.VMEM((total, channels, lanes), f32),
            pltpu.VMEM((total, channels, lanes), bf16),
            pltpu.VMEM((total, channels, lanes), bf16),
            pltpu.VMEM((depth, total, channels, lanes), f32),
            pltpu.VMEM((total, channels, lanes), f32),
            pltpu.VMEM((total, channels, lanes), bf16),
        ],
        flops=mac * 120,
    )(c_flat, q_flat, s, s_pair, s_cross, pair, cross, side, w_fwd, w_back)
    returned = []
    for k in range(groups - 1, 0, -1):
        returned.append(lax.ppermute(sending, "layer", [(k, k - 1)]))
        if k > 1:
            sending = hop(returned[-1], (q_flat,), g, m_back)
    grads = call(
        functools.partial(grad_body, depth=depth, **sizes),
        jax.ShapeDtypeStruct((depth, channels, 9 * channels), f32),
        flops=10**9,
    )(kept, sources)
    weight_grads = total_over_tiles(grads)
    adjoint = call(
        functools.partial(last_body, **sizes), jax.ShapeDtypeStruct(flat, f32), flops=10**10
    )(q_flat, *returned)
    return state.reshape(c_states.shape), adjoint.reshape(c_states.shape), weight_grads


def solution(mesh):
    placed = (
        P("layer", None, "row", "col"),
        P("layer", None, "row", "col"),
        P("layer", None, None),
    )
    return jax.shard_map(
        local, mesh=mesh, in_specs=placed, out_specs=placed, check_vma=False
    )
```

```python
import functools

import jax
import jax.numpy as jnp
from jax import lax
from jax.experimental import pallas as pl
from jax.experimental.pallas import tpu as pltpu
from jax.sharding import PartitionSpec as P

step_size = 0.2
VMEM_BYTES = 40 * 1024 * 1024
f32 = jnp.float32
bf16 = jnp.bfloat16


def call(body, out_shape, scratch=(), flops=0, moved=0):
    return pl.pallas_call(
        body,
        out_shape=out_shape,
        scratch_shapes=list(scratch),
        cost_estimate=pl.CostEstimate(
            flops=int(flops), bytes_accessed=int(moved), transcendentals=0
        ),
        compiler_params=pltpu.CompilerParams(vmem_limit_bytes=VMEM_BYTES),
    )


def row_of(ref, row, channels, rows):
    return ref[pl.ds(row, channels, stride=rows), :]


def lanes_of(shape):
    return lax.broadcasted_iota(jnp.int32, shape, 1)


def slots(shape, low, width, count):
    return (lanes_of(shape) - low + width * count) // width - count


def fold_edges(rows_list, edge, low, total):
    doubled = total.shape[1] > rows_list[0].shape[1]
    cols = rows_list[0].shape[1]
    slot = slots(total.shape, low, 2 * edge, len(rows_list))
    for place, row in enumerate(rows_list):
        wide = jnp.concatenate([row, row], 1) if doubled else row
        turned = pltpu.roll(wide, (low + 2 * edge * place + edge - cols) % wide.shape[1], 1)
        total = jnp.where(slot == place, turned, total)
    return total


def join_edges(from_left, from_right, left, right, edges):
    lanes = lanes_of(from_left.shape)
    far = jnp.zeros(lanes.shape, jnp.bool_)
    for edge, low, high in edges:
        inside = (lanes >= low) & (lanes < high)
        far = far | (inside & ((lanes - low) % (2 * edge) >= edge))
    return jnp.where(far, from_right.astype(f32) * right, from_left.astype(f32) * left)


def side_lanes(joined, edge, low, place):
    lanes = joined.shape[1]
    turned = pltpu.roll(joined, (2 * lanes - (low + 2 * edge * place + edge)) % lanes, 1)
    if lanes == 128:
        return turned
    front, back = turned[:, :128], turned[:, lanes - 128 :]
    return jnp.where(lanes_of(front.shape) < 64, front, back)


def convolved(weights, slab):
    channels = slab.shape[1]
    lanes = slab.shape[2]
    product = jnp.dot(
        weights, slab.reshape(3 * channels, lanes), preferred_element_type=f32
    )
    return (
        pltpu.roll(product[:channels], 1, 1)
        + product[channels : 2 * channels]
        + pltpu.roll(product[2 * channels :], lanes - 1, 1)
    )


def flags():
    row, col = lax.axis_index("row"), lax.axis_index("col")
    up = (row > 0).astype(f32)
    down = (row < lax.axis_size("row") - 1).astype(f32)
    left = (col > 0).astype(f32)
    right = (col < lax.axis_size("col") - 1).astype(f32)
    return up, down, left, right


def even_row():
    return lax.axis_index("row") % 2 == 0


def lane_mask(cols, left, right):
    lanes = lax.broadcasted_iota(jnp.int32, (1, 2 * cols), 1)
    return jnp.where(lanes < cols, 1.0, jnp.where(lanes < cols + cols // 2, right, left))


def layout(rows, depth):
    state_edge, adjoint_edge = 3 * depth, depth
    return (state_edge, 0), (adjoint_edge, 2 * state_edge * rows)


def strip_body(c_ref, q_ref, edge_ref, *, channels, rows, depth):
    total = jnp.zeros(edge_ref.shape, f32)
    for ref, (edge, low) in zip((c_ref, q_ref), layout(rows, depth)):
        image = [row_of(ref, row, channels, rows) for row in range(rows)]
        total = fold_edges(image, edge, low, total)
    edge_ref[...] = total.astype(bf16)


def message_body(
    c_ref, q_ref, left_ref, right_ref, pair_ref, cross_ref, side_ref, strip_ref,
    *, channels, rows, depth,
):
    cols = c_ref.shape[1]
    _, _, left, right = flags()
    (c_edge, _), (q_edge, middle) = layout(rows, depth)
    edges = ((c_edge, 0, middle), (q_edge, middle, 2 * cols))
    side = join_edges(left_ref[...], right_ref[...], left, right, edges).astype(bf16)
    side_ref[...] = side
    wide = side.astype(f32)
    image = [side_lanes(wide, c_edge, 0, row) for row in range(rows)]
    strip_ref[...] = fold_edges(image, 2 * depth, 0, jnp.zeros(strip_ref.shape, f32))
    even = even_row()
    for which, ref in enumerate((c_ref, q_ref)):
        for row in range(depth):
            place = which * depth + row
            top = row_of(ref, row, channels, rows)
            bottom = row_of(ref, rows - depth + row, channels, rows)
            pair_ref[place] = jnp.where(even, bottom, top).astype(bf16)
            cross_ref[place] = jnp.where(even, top, bottom).astype(bf16)
    for half in range(2):
        part = side[:, half * cols : (half + 1) * cols]
        pair_ref[2 * depth + half] = part
        cross_ref[2 * depth + half] = part


class Beside:
    def __init__(self, pair_ref, cross_ref):
        self.pair, self.cross, self.even = pair_ref, cross_ref, even_row()

    def above(self, place):
        return jnp.where(
            self.even, self.cross[place].astype(f32), self.pair[place].astype(f32)
        )

    def below(self, place):
        return jnp.where(
            self.even, self.pair[place].astype(f32), self.cross[place].astype(f32)
        )


def strips_of(get, depth):
    return jnp.concatenate([get(2 * depth), get(2 * depth + 1)], 1)


def row_blocks(low, high, body):
    turns = 1 if high - low <= 10 else 2
    size, rest = divmod(high - low, turns)

    def turn(number, carry):
        body(low + size * number, size)
        return carry

    if size > 0:
        lax.fori_loop(0, turns, turn, 0)
    if rest > 0:
        body(low + size * turns, rest)


def convolved_rows(weights, ref, first, count):
    slab = ref[pl.ds(first - 1, count + 2)]
    return [convolved(weights, slab[place : place + 3]) for place in range(count)]


def row_flag(index, halo, rows, up, down):
    return jnp.where(index < halo, up, jnp.where(index >= halo + rows, down, 1.0))


def first_body(
    c_ref, pair_ref, cross_ref, side_ref, w_ref, out_ref, x_ref, a_ref, a2_ref,
    *, channels, rows, depth, sender,
):
    active = (lax.axis_index("layer") == 0) == sender

    @pl.when(jnp.logical_not(active))
    def nothing():
        out_ref[...] = jnp.zeros(out_ref.shape, out_ref.dtype)

    @pl.when(active)
    def run():
        first_pass(
            c_ref, pair_ref, cross_ref, side_ref, w_ref, out_ref, x_ref, a_ref, a2_ref,
            channels, rows, depth,
        )


def first_pass(
    c_ref, pair_ref, cross_ref, side_ref, w_ref, out_ref, x_ref, a_ref, a2_ref,
    channels, rows, depth,
):
    cols = c_ref.shape[1]
    up, down, left, right = flags()
    mask = lane_mask(cols, left, right)
    halo = depth

    def put(index, own, beyond):
        x_ref[index, :, :cols] = own
        x_ref[index, :, cols:] = beyond
        a_ref[index, :, :cols] = own.astype(bf16)
        a_ref[index, :, cols:] = beyond.astype(bf16)

    (edge, low), _ = layout(rows, depth)
    own_side = side_ref[...].astype(f32)
    for row in range(rows):
        own = row_of(c_ref, row, channels, rows)
        put(halo + row, own, side_lanes(own_side, edge, low, row))
    beside = Beside(pair_ref, cross_ref)
    above_side, below_side = strips_of(beside.above, depth), strips_of(beside.below, depth)
    for row in range(depth):
        place = rows - depth + row
        put(row, beside.above(row), side_lanes(above_side, edge, low, place))
        put(halo + rows + row, beside.below(row), side_lanes(below_side, edge, low, row))

    total = rows + 2 * halo
    for layer in range(depth):
        now, later = (a_ref, a2_ref) if layer % 2 == 0 else (a2_ref, a_ref)

        def step(first, count, layer=layer, now=now, later=later):
            states = x_ref[pl.ds(first, count)]
            done = []
            for place, z in enumerate(convolved_rows(w_ref[layer], now, first, count)):
                gain = mask * (step_size * row_flag(first + place, halo, rows, up, down))
                done.append(states[place] + gain * jnp.tanh(z))
            for place, x in enumerate(done):
                x_ref[first + place] = x
                if layer < depth - 1:
                    later[first + place] = x.astype(bf16)

        row_blocks(layer + 1, total - layer - 1, step)
    image = [x_ref[halo + row, :, cols:] for row in range(rows)]
    values = [x_ref[halo + row, :, :cols] for row in range(rows)]
    values.append(fold_edges(image, 2 * depth, 0, jnp.zeros((channels, cols), f32)))
    for row, value in enumerate(values):
        out_ref[row] = value.astype(out_ref.dtype)


def hop_body(s_ref, c_ref, *refs, channels, rows):
    f_ref, m_ref, out_ref = refs[-3:]
    base = [row_of(c_ref, row, channels, rows) for row in range(rows)]
    base += [ref[...] for ref in refs[:-3]]
    for row in range(len(base)):
        e = s_ref[row].astype(f32) - base[row]
        high = e.astype(bf16)
        low = (e - high.astype(f32)).astype(bf16)
        stacked = jnp.concatenate([high, high, low], 0)
        moved = jnp.dot(m_ref[...], stacked, preferred_element_type=f32)
        out_ref[row] = (f_ref[row] + e + moved).astype(bf16)


def settle_body(c_ref, strip_ref, *refs, channels, rows):
    arrived, s_ref = refs[:-1], refs[-1]
    first = lax.axis_index("layer") == 0
    base = [row_of(c_ref, row, channels, rows) for row in range(rows)] + [strip_ref[...]]
    for row in range(rows + 1):
        value = sum(ref[row].astype(f32) for ref in arrived)
        s_ref[row] = jnp.where(first, base[row], value).astype(bf16)


def second_body(
    c_ref, q_ref, s_ref, s_pair_ref, s_cross_ref, pair_ref, cross_ref, side_ref, w_ref, wt_ref,
    state_ref, g_ref, sending_ref, kept_ref, sent_ref,
    x_ref, a_ref, a2_ref, slope_ref, adj_ref, src_ref,
    *, channels, rows, depth,
):
    cols = c_ref.shape[1]
    up, down, left, right = flags()
    mask = lane_mask(cols, left, right)
    halo = 2 * depth
    total = rows + 2 * halo
    first = lax.axis_index("layer") == 0

    def put(index, own, beyond):
        x_ref[index, :, :cols] = own
        x_ref[index, :, cols:] = beyond
        a_ref[index, :, :cols] = own.astype(bf16)
        a_ref[index, :, cols:] = beyond.astype(bf16)

    edge = 2 * depth

    beside = Beside(s_pair_ref, s_cross_ref)
    own_side = s_ref[rows].astype(f32)
    above_side, below_side = beside.above(rows), beside.below(rows)
    for row in range(rows):
        own = jnp.where(first, row_of(c_ref, row, channels, rows), s_ref[row].astype(f32))
        state_ref[pl.ds(row, channels, stride=rows), :] = own
        put(halo + row, own, side_lanes(own_side, edge, 0, row))
    for row in range(halo):
        place = rows - halo + row
        put(
            row,
            beside.above(place),
            side_lanes(above_side, edge, 0, place),
        )
        put(
            halo + rows + row,
            beside.below(row),
            side_lanes(below_side, edge, 0, row),
        )

    def put_adj(index, own, beyond):
        adj_ref[index, :, :cols] = own
        adj_ref[index, :, cols:] = beyond

    _, (edge, low) = layout(rows, depth)
    own_side = side_ref[...].astype(f32)
    beside = Beside(pair_ref, cross_ref)
    above_side, below_side = strips_of(beside.above, depth), strips_of(beside.below, depth)
    for row in range(rows):
        put_adj(
            halo + row, row_of(q_ref, row, channels, rows), side_lanes(own_side, edge, low, row)
        )
    for row in range(depth):
        place = rows - depth + row
        put_adj(
            halo - depth + row,
            beside.above(depth + row),
            side_lanes(above_side, edge, low, place),
        )
        put_adj(
            halo + rows + row,
            beside.below(depth + row),
            side_lanes(below_side, edge, low, row),
        )

    for layer in range(depth):
        now, later = (a_ref, a2_ref) if layer % 2 == 0 else (a2_ref, a_ref)
        kept_ref[layer] = now[pl.ds(halo, rows)]

        def step(first, count, layer=layer, now=now, later=later):
            states = x_ref[pl.ds(first, count)]
            done = []
            for place, z in enumerate(convolved_rows(w_ref[layer], now, first, count)):
                gain = mask * (step_size * row_flag(first + place, halo, rows, up, down))
                t = jnp.tanh(z)
                done.append((gain * (1.0 - t * t), states[place] + gain * t))
            for place, (slope, x) in enumerate(done):
                slope_ref[layer, first + place] = slope
                if layer < depth - 1:
                    x_ref[first + place] = x
                    later[first + place] = x.astype(bf16)

        row_blocks(layer + 1, total - layer - 1, step)

    for layer in reversed(range(depth)):
        reach = layer + 1

        def source(first, count, layer=layer):
            part = pl.ds(first, count)
            src_ref[part] = (adj_ref[part] * slope_ref[layer, part]).astype(bf16)

        row_blocks(halo - reach, halo + rows + reach, source)

        def back(first, count, layer=layer):
            adjoints = adj_ref[pl.ds(first, count)]
            moved = convolved_rows(wt_ref[layer], src_ref, first, count)
            for place in range(count):
                adj_ref[first + place] = adjoints[place] + moved[place]

        row_blocks(halo - layer, halo + rows + layer, back)
        sent_ref[layer] = src_ref[pl.ds(halo - 1, rows + 2), :, :cols]
    for row in range(rows):
        value = adj_ref[halo + row, :, :cols]
        g_ref[row] = value
        sending_ref[row] = value.astype(bf16)


def grad_body(kept_ref, sent_ref, grad_ref, *, channels, rows, depth):
    lanes = kept_ref.shape[3]
    cols = lanes // 2
    for layer in range(depth):
        columns = []
        for row in range(rows):
            a = kept_ref[layer, row].astype(f32)
            columns.append(
                jnp.concatenate(
                    [
                        pltpu.roll(a, 1, 1)[:, :cols],
                        a[:, :cols],
                        pltpu.roll(a, lanes - 1, 1)[:, :cols],
                    ],
                    0,
                ).astype(bf16)
            )
        sources = [
            sent_ref[layer, pl.ds(row, 3)].reshape(3 * channels, cols) for row in range(rows)
        ]
        grad = lax.dot_general(
            jnp.concatenate(sources, 1),
            jnp.concatenate(columns, 1),
            (((1,), (1,)), ((), ())),
            preferred_element_type=f32,
        )
        for tap in range(3):
            grad_ref[layer, :, pl.ds(tap * 3 * channels, 3 * channels)] = grad[
                (2 - tap) * channels : (3 - tap) * channels
            ]


def last_body(q_ref, *refs, channels, rows):
    arrived, out_ref = refs[:-1], refs[-1]
    last = lax.axis_index("layer") == lax.axis_size("layer") - 1
    for row in range(rows):
        value = sum(ref[row].astype(f32) for ref in arrived)
        value = jnp.where(last, row_of(q_ref, row, channels, rows), value)
        out_ref[pl.ds(row, channels, stride=rows), :] = value


def shifted(array, axis, by):
    count = lax.axis_size(axis)
    pairs = [(i, i + by) for i in range(count) if 0 <= i + by < count]
    return lax.ppermute(array, axis, pairs)


def exchanged(to_pair, to_cross):
    rows = lax.axis_size("row")
    pairs = [(r, r ^ 1) for r in range(rows)]
    crossing = [(r, r + 1 if r % 2 else r - 1) for r in range(1, rows - 1)]
    return lax.ppermute(to_pair, "row", pairs), lax.ppermute(to_cross, "row", crossing)


def from_sides(array):
    if lax.axis_size("col") == 2:
        other = lax.ppermute(array, "col", [(0, 1), (1, 0)])
        return other, other
    return shifted(array, "col", 1), shifted(array, "col", -1)


def total_over_tiles(grads):
    rows, cols = lax.axis_size("row"), lax.axis_size("col")
    depth = grads.shape[0]
    half = depth // 2
    odd = lax.axis_index("row") % 2 == 1
    sent = jnp.where(odd, grads[:half], grads[half:])
    own = jnp.where(odd, grads[half:], grads[:half])
    pair = [(r, r ^ 1) for r in range(rows)]
    value = own + lax.ppermute(sent, "row", pair)

    flips = [(1 << bit, 0) for bit in range(1, rows.bit_length() - 1)]
    flips += [(0, 1 << bit) for bit in range(cols.bit_length() - 1)]
    for even, uneven in zip(flips, flips[::-1]):
        pairs = []
        for r in range(rows):
            row_by, col_by = uneven if r % 2 else even
            pairs += [
                (r * cols + c, (r ^ row_by) * cols + (c ^ col_by)) for c in range(cols)
            ]
        rounded = value.astype(bf16)
        arrived = lax.ppermute(rounded, ("row", "col"), pairs)
        value = rounded.astype(f32) + arrived.astype(f32)
    other = lax.ppermute(value, "row", pair)
    first = jnp.where(odd, other, value)
    second = jnp.where(odd, value, other)
    return jnp.concatenate([first, second], 0)


def local(c_states, c_adjoints, weights):
    groups = lax.axis_size("layer")
    channels, rows, cols = c_states.shape[1:]
    depth = weights.shape[0]
    flat = (channels * rows, cols)
    c_flat, q_flat = c_states.reshape(flat), c_adjoints.reshape(flat)
    sizes = dict(channels=channels, rows=rows)
    tile_f = jax.ShapeDtypeStruct((rows, channels, cols), f32)

    strip_f = jax.ShapeDtypeStruct((channels, cols), f32)
    wide_b = jax.ShapeDtypeStruct((channels, 2 * cols), bf16)
    more_f, more_b, message_b = (
        jax.ShapeDtypeStruct((count, channels, cols), kind)
        for count, kind in ((rows + 1, f32), (rows + 1, bf16), (2 * depth + 2, bf16))
    )
    flat_f = jax.ShapeDtypeStruct(flat, f32)
    edges = call(functools.partial(strip_body, depth=depth, **sizes), wide_b)(c_flat, q_flat)
    left, right = from_sides(edges)
    to_pair, to_cross, side, strip = call(
        functools.partial(message_body, depth=depth, **sizes),
        (message_b, message_b, wide_b, strip_f),
    )(c_flat, q_flat, left, right)
    pair, cross = exchanged(to_pair, to_cross)

    taps = weights.reshape(depth, channels, 3, 3, channels)
    w_fwd = jnp.transpose(taps, (0, 3, 1, 2, 4)).reshape(depth, 3 * channels, 3 * channels)
    later_taps, _ = lax.optimization_barrier((taps, to_pair))
    w_back = jnp.transpose(later_taps[:, :, ::-1, ::-1, :], (0, 3, 4, 2, 1)).reshape(
        depth, 3 * channels, 3 * channels
    )
    w_fwd, w_back = lax.optimization_barrier((w_fwd, w_back))
    coarse = step_size * jnp.sum(weights[0].astype(f32).reshape(channels, 9, channels), axis=1)
    high = coarse.astype(bf16)
    low = (coarse - high.astype(f32)).astype(bf16)
    m_fwd = jnp.concatenate([high, low, high], 1)
    m_back = jnp.concatenate([high.T, low.T, high.T], 1)

    lanes = 2 * cols
    mac = 2 * 9 * channels * channels * lanes
    total = rows + 2 * depth

    def first(kind, sender, *inputs):
        return call(
            functools.partial(first_body, depth=depth, sender=sender, **sizes),
            kind,
            [
                pltpu.VMEM((total, channels, lanes), f32),
                pltpu.VMEM((total, channels, lanes), bf16),
                pltpu.VMEM((total, channels, lanes), bf16),
            ],
            flops=mac * 44,
        )(*inputs)

    def hop(arrived, base, target, matrix):
        return call(
            functools.partial(hop_body, **sizes),
            jax.ShapeDtypeStruct(arrived.shape, bf16),
            flops=10**10,
        )(arrived, *base, target, matrix)

    inputs = (c_flat, pair, cross, side, w_fwd)
    sending = first(more_b, True, *inputs)
    inputs = lax.optimization_barrier((inputs, sending))[0]
    f = first(more_f, False, *inputs)
    arrivals = []
    for k in range(groups - 1):
        arrivals.append(lax.ppermute(sending, "layer", [(k, k + 1)]))
        if k < groups - 2:
            sending = hop(arrivals[-1], (c_flat, strip), f, m_fwd)
    s = call(functools.partial(settle_body, **sizes), more_b)(c_flat, strip, *arrivals)
    s_pair, s_cross = exchanged(s, s)

    total = rows + 4 * depth
    state, g, sending, kept, sources = call(
        functools.partial(second_body, depth=depth, **sizes),
        (
            flat_f,
            tile_f,
            jax.ShapeDtypeStruct(tile_f.shape, bf16),
            jax.ShapeDtypeStruct((depth, rows, channels, lanes), bf16),
            jax.ShapeDtypeStruct((depth, rows + 2, channels, cols), bf16),
        ),
        [
            pltpu.VMEM((total, channels, lanes), f32),
            pltpu.VMEM((total, channels, lanes), bf16),
            pltpu.VMEM((total, channels, lanes), bf16),
            pltpu.VMEM((depth, total, channels, lanes), f32),
            pltpu.VMEM((total, channels, lanes), f32),
            pltpu.VMEM((total, channels, lanes), bf16),
        ],
        flops=mac * 120,
    )(c_flat, q_flat, s, s_pair, s_cross, pair, cross, side, w_fwd, w_back)
    returned = [lax.ppermute(sending, "layer", [(groups - 1, groups - 2)])]
    grads = call(
        functools.partial(grad_body, depth=depth, **sizes),
        jax.ShapeDtypeStruct((depth, channels, 9 * channels), f32),
        flops=10**9,
    )(kept, sources)
    sending = hop(returned[0], (q_flat,), g, m_back)
    grads, sending = lax.optimization_barrier((grads, sending))
    for k in range(groups - 2, 0, -1):
        returned.append(lax.ppermute(sending, "layer", [(k, k - 1)]))
        if k > 1:
            sending = hop(returned[-1], (q_flat,), g, m_back)
    weight_grads = total_over_tiles(grads)
    returned[-1], weight_grads = lax.optimization_barrier((returned[-1], weight_grads))
    adjoint = call(
        functools.partial(last_body, **sizes), jax.ShapeDtypeStruct(flat, f32), flops=10**10
    )(q_flat, *returned)
    return state.reshape(c_states.shape), adjoint.reshape(c_states.shape), weight_grads


def solution(mesh):
    placed = (
        P("layer", None, "row", "col"),
        P("layer", None, "row", "col"),
        P("layer", None, None),
    )
    return jax.shard_map(
        local, mesh=mesh, in_specs=placed, out_specs=placed, check_vma=False
    )
```

```python
import functools

import jax
import jax.numpy as jnp
from jax import lax
from jax.experimental import pallas as pl
from jax.experimental.pallas import tpu as pltpu
from jax.sharding import PartitionSpec as P

step_size = 0.2
VMEM_BYTES = 40 * 1024 * 1024
f32 = jnp.float32
bf16 = jnp.bfloat16


def call(body, out_shape, scratch=(), flops=0, moved=0):
    return pl.pallas_call(
        body,
        out_shape=out_shape,
        scratch_shapes=list(scratch),
        cost_estimate=pl.CostEstimate(
            flops=int(flops), bytes_accessed=int(moved), transcendentals=0
        ),
        compiler_params=pltpu.CompilerParams(vmem_limit_bytes=VMEM_BYTES),
    )


def piece_of(parts, row, rows):
    half = rows // 2
    if len(parts) == 1 or row < half:
        return parts[0], row
    return (parts[1], row - half) if row < rows else (parts[0], half)


def row_of(ref, row, channels, rows):
    return ref[pl.ds(row, channels, stride=rows), :]


def lanes_of(shape):
    return lax.broadcasted_iota(jnp.int32, shape, 1)


def slots(shape, low, width, count):
    return (lanes_of(shape) - low + width * count) // width - count


def fold_edges(rows_list, edge, low, total):
    doubled = total.shape[1] > rows_list[0].shape[1]
    cols = rows_list[0].shape[1]
    slot = slots(total.shape, low, 2 * edge, len(rows_list))
    for place, row in enumerate(rows_list):
        wide = jnp.concatenate([row, row], 1) if doubled else row
        turned = pltpu.roll(wide, (low + 2 * edge * place + edge - cols) % wide.shape[1], 1)
        total = jnp.where(slot == place, turned, total)
    return total


def join_edges(from_left, from_right, left, right, edges):
    lanes = lanes_of(from_left.shape)
    far = jnp.zeros(lanes.shape, jnp.bool_)
    for edge, low, high in edges:
        inside = (lanes >= low) & (lanes < high)
        far = far | (inside & ((lanes - low) % (2 * edge) >= edge))
    return jnp.where(far, from_right.astype(f32) * right, from_left.astype(f32) * left)


def side_lanes(joined, edge, low, place):
    lanes = joined.shape[1]
    turned = pltpu.roll(joined, (2 * lanes - (low + 2 * edge * place + edge)) % lanes, 1)
    if lanes == 128:
        return turned
    front, back = turned[:, :128], turned[:, lanes - 128 :]
    return jnp.where(lanes_of(front.shape) < 64, front, back)


def convolved(weights, slab):
    channels = slab.shape[1]
    lanes = slab.shape[2]
    product = jnp.dot(
        weights, slab.reshape(3 * channels, lanes), preferred_element_type=f32
    )
    return (
        pltpu.roll(product[:channels], 1, 1)
        + product[channels : 2 * channels]
        + pltpu.roll(product[2 * channels :], lanes - 1, 1)
    )


def flags():
    row, col = lax.axis_index("row"), lax.axis_index("col")
    up = (row > 0).astype(f32)
    down = (row < lax.axis_size("row") - 1).astype(f32)
    left = (col > 0).astype(f32)
    right = (col < lax.axis_size("col") - 1).astype(f32)
    return up, down, left, right


def even_row():
    return lax.axis_index("row") % 2 == 0


def lane_mask(cols, left, right):
    lanes = lax.broadcasted_iota(jnp.int32, (1, 2 * cols), 1)
    return jnp.where(lanes < cols, 1.0, jnp.where(lanes < cols + cols // 2, right, left))


def layout(rows, depth):
    state_edge, adjoint_edge = 3 * depth, depth
    return (state_edge, 0), (adjoint_edge, 2 * state_edge * rows)


def strip_body(c_ref, q_ref, edge_ref, *, channels, rows, depth):
    total = jnp.zeros(edge_ref.shape, f32)
    for ref, (edge, low) in zip((c_ref, q_ref), layout(rows, depth)):
        image = [row_of(ref, row, channels, rows) for row in range(rows)]
        total = fold_edges(image, edge, low, total)
    edge_ref[...] = total.astype(bf16)


def message_body(
    c_ref, q_ref, left_ref, right_ref, pair_ref, cross_ref, side_ref, strip_ref,
    *, channels, rows, depth,
):
    cols = c_ref.shape[1]
    _, _, left, right = flags()
    (c_edge, _), (q_edge, middle) = layout(rows, depth)
    edges = ((c_edge, 0, middle), (q_edge, middle, 2 * cols))
    side = join_edges(left_ref[...], right_ref[...], left, right, edges).astype(bf16)
    side_ref[...] = side
    wide = side.astype(f32)
    image = [side_lanes(wide, c_edge, 0, row) for row in range(rows)]
    strip_ref[...] = fold_edges(image, 2 * depth, 0, jnp.zeros(strip_ref.shape, f32))
    even = even_row()
    for which, ref in enumerate((c_ref, q_ref)):
        for row in range(depth):
            place = which * depth + row
            top = row_of(ref, row, channels, rows)
            bottom = row_of(ref, rows - depth + row, channels, rows)
            pair_ref[place] = jnp.where(even, bottom, top).astype(bf16)
            cross_ref[place] = jnp.where(even, top, bottom).astype(bf16)
    for half in range(2):
        part = side[:, half * cols : (half + 1) * cols]
        pair_ref[2 * depth + half] = part
        cross_ref[2 * depth + half] = part


class Beside:
    def __init__(self, pair_ref, cross_ref):
        self.pair, self.cross, self.even = pair_ref, cross_ref, even_row()

    def above(self, place):
        return jnp.where(
            self.even, self.cross[place].astype(f32), self.pair[place].astype(f32)
        )

    def below(self, place):
        return jnp.where(
            self.even, self.pair[place].astype(f32), self.cross[place].astype(f32)
        )


def strips_of(get, depth):
    return jnp.concatenate([get(2 * depth), get(2 * depth + 1)], 1)


def row_blocks(low, high, body):
    turns = 1 if high - low <= 10 else 2
    size, rest = divmod(high - low, turns)

    def turn(number, carry):
        body(low + size * number, size)
        return carry

    if size > 0:
        lax.fori_loop(0, turns, turn, 0)
    if rest > 0:
        body(low + size * turns, rest)


def convolved_rows(weights, ref, first, count):
    slab = ref[pl.ds(first - 1, count + 2)]
    return [convolved(weights, slab[place : place + 3]) for place in range(count)]


def row_flag(index, halo, rows, up, down):
    return jnp.where(index < halo, up, jnp.where(index >= halo + rows, down, 1.0))


def first_body(
    c_ref, pair_ref, cross_ref, side_ref, w_ref, *refs, channels, rows, depth, sender
):
    outs = refs[:-3]
    active = (lax.axis_index("layer") == 0) == sender

    @pl.when(jnp.logical_not(active))
    def nothing():
        for out_ref in outs:
            out_ref[...] = jnp.zeros(out_ref.shape, out_ref.dtype)

    @pl.when(active)
    def run():
        first_pass(
            c_ref, pair_ref, cross_ref, side_ref, w_ref, outs, *refs[-3:],
            channels, rows, depth,
        )


def first_pass(
    c_ref, pair_ref, cross_ref, side_ref, w_ref, outs, x_ref, a_ref, a2_ref,
    channels, rows, depth,
):
    cols = c_ref.shape[1]
    up, down, left, right = flags()
    mask = lane_mask(cols, left, right)
    halo = depth

    def put(index, own, beyond):
        x_ref[index, :, :cols] = own
        x_ref[index, :, cols:] = beyond
        a_ref[index, :, :cols] = own.astype(bf16)
        a_ref[index, :, cols:] = beyond.astype(bf16)

    (edge, low), _ = layout(rows, depth)
    own_side = side_ref[...].astype(f32)
    for row in range(rows):
        own = row_of(c_ref, row, channels, rows)
        put(halo + row, own, side_lanes(own_side, edge, low, row))
    beside = Beside(pair_ref, cross_ref)
    above_side, below_side = strips_of(beside.above, depth), strips_of(beside.below, depth)
    for row in range(depth):
        place = rows - depth + row
        put(row, beside.above(row), side_lanes(above_side, edge, low, place))
        put(halo + rows + row, beside.below(row), side_lanes(below_side, edge, low, row))

    total = rows + 2 * halo
    for layer in range(depth):
        now, later = (a_ref, a2_ref) if layer % 2 == 0 else (a2_ref, a_ref)

        def step(first, count, layer=layer, now=now, later=later):
            states = x_ref[pl.ds(first, count)]
            done = []
            for place, z in enumerate(convolved_rows(w_ref[layer], now, first, count)):
                gain = mask * (step_size * row_flag(first + place, halo, rows, up, down))
                done.append(states[place] + gain * jnp.tanh(z))
            for place, x in enumerate(done):
                x_ref[first + place] = x
                if layer < depth - 1:
                    later[first + place] = x.astype(bf16)

        row_blocks(layer + 1, total - layer - 1, step)
    image = [x_ref[halo + row, :, cols:] for row in range(rows)]
    values = [x_ref[halo + row, :, :cols] for row in range(rows)]
    values.append(fold_edges(image, 2 * depth, 0, jnp.zeros((channels, cols), f32)))
    for row, value in enumerate(values):
        out_ref, place = piece_of(outs, row, rows)
        out_ref[place] = value.astype(out_ref.dtype)


def hop_body(s_ref, c_ref, *refs, start, channels, rows):
    f_ref, m_ref, out_ref = refs[-3:]
    work = [
        (row, row_of(c_ref, row, channels, rows)) for row in range(start, start + rows // 2)
    ]
    work += [(rows, ref[...]) for ref in refs[:-3]]
    for place, (row, base) in enumerate(work):
        e = s_ref[place].astype(f32) - base
        high = e.astype(bf16)
        low = (e - high.astype(f32)).astype(bf16)
        stacked = jnp.concatenate([high, high, low], 0)
        moved = jnp.dot(m_ref[...], stacked, preferred_element_type=f32)
        out_ref[place] = (f_ref[row] + e + moved).astype(bf16)


def arrived_row(refs, row, rows):
    value = 0.0
    for pieces in zip(refs[::2], refs[1::2]):
        ref, place = piece_of(pieces, row, rows)
        value = value + ref[place].astype(f32)
    return value


def settle_body(c_ref, strip_ref, *refs, channels, rows):
    arrived, s_ref = refs[:-1], refs[-1]
    first = lax.axis_index("layer") == 0
    base = [row_of(c_ref, row, channels, rows) for row in range(rows)] + [strip_ref[...]]
    for row in range(rows + 1):
        value = arrived_row(arrived, row, rows)
        s_ref[row] = jnp.where(first, base[row], value).astype(bf16)


def second_body(
    c_ref, q_ref, s_ref, s_pair_ref, s_cross_ref, pair_ref, cross_ref, side_ref, w_ref, wt_ref,
    state_ref, g_ref, g_upper_ref, g_lower_ref, kept_ref, sent_ref,
    x_ref, a_ref, a2_ref, slope_ref, adj_ref, src_ref,
    *, channels, rows, depth,
):
    cols = c_ref.shape[1]
    up, down, left, right = flags()
    mask = lane_mask(cols, left, right)
    halo = 2 * depth
    total = rows + 2 * halo
    first = lax.axis_index("layer") == 0

    def put(index, own, beyond):
        x_ref[index, :, :cols] = own
        x_ref[index, :, cols:] = beyond
        a_ref[index, :, :cols] = own.astype(bf16)
        a_ref[index, :, cols:] = beyond.astype(bf16)

    edge = 2 * depth

    beside = Beside(s_pair_ref, s_cross_ref)
    own_side = s_ref[rows].astype(f32)
    above_side, below_side = beside.above(rows), beside.below(rows)
    for row in range(rows):
        own = jnp.where(first, row_of(c_ref, row, channels, rows), s_ref[row].astype(f32))
        state_ref[pl.ds(row, channels, stride=rows), :] = own
        put(halo + row, own, side_lanes(own_side, edge, 0, row))
    for row in range(halo):
        place = rows - halo + row
        put(
            row,
            beside.above(place),
            side_lanes(above_side, edge, 0, place),
        )
        put(
            halo + rows + row,
            beside.below(row),
            side_lanes(below_side, edge, 0, row),
        )

    def put_adj(index, own, beyond):
        adj_ref[index, :, :cols] = own
        adj_ref[index, :, cols:] = beyond

    _, (edge, low) = layout(rows, depth)
    own_side = side_ref[...].astype(f32)
    beside = Beside(pair_ref, cross_ref)
    above_side, below_side = strips_of(beside.above, depth), strips_of(beside.below, depth)
    for row in range(rows):
        put_adj(
            halo + row, row_of(q_ref, row, channels, rows), side_lanes(own_side, edge, low, row)
        )
    for row in range(depth):
        place = rows - depth + row
        put_adj(
            halo - depth + row,
            beside.above(depth + row),
            side_lanes(above_side, edge, low, place),
        )
        put_adj(
            halo + rows + row,
            beside.below(depth + row),
            side_lanes(below_side, edge, low, row),
        )

    for layer in range(depth):
        now, later = (a_ref, a2_ref) if layer % 2 == 0 else (a2_ref, a_ref)
        kept_ref[layer] = now[pl.ds(halo, rows)]

        def step(first, count, layer=layer, now=now, later=later):
            states = x_ref[pl.ds(first, count)]
            done = []
            for place, z in enumerate(convolved_rows(w_ref[layer], now, first, count)):
                gain = mask * (step_size * row_flag(first + place, halo, rows, up, down))
                t = jnp.tanh(z)
                done.append((gain * (1.0 - t * t), states[place] + gain * t))
            for place, (slope, x) in enumerate(done):
                slope_ref[layer, first + place] = slope
                if layer < depth - 1:
                    x_ref[first + place] = x
                    later[first + place] = x.astype(bf16)

        row_blocks(layer + 1, total - layer - 1, step)

    for layer in reversed(range(depth)):
        reach = layer + 1

        def source(first, count, layer=layer):
            part = pl.ds(first, count)
            src_ref[part] = (adj_ref[part] * slope_ref[layer, part]).astype(bf16)

        row_blocks(halo - reach, halo + rows + reach, source)

        def back(first, count, layer=layer):
            adjoints = adj_ref[pl.ds(first, count)]
            moved = convolved_rows(wt_ref[layer], src_ref, first, count)
            for place in range(count):
                adj_ref[first + place] = adjoints[place] + moved[place]

        row_blocks(halo - layer, halo + rows + layer, back)
        sent_ref[layer] = src_ref[pl.ds(halo - 1, rows + 2), :, :cols]
    for row in range(rows):
        value = adj_ref[halo + row, :, :cols]
        g_ref[row] = value
        ref, place = piece_of((g_upper_ref, g_lower_ref), row, rows)
        ref[place] = value.astype(bf16)


def grad_body(kept_ref, sent_ref, grad_ref, *, channels, rows, depth):
    lanes = kept_ref.shape[3]
    cols = lanes // 2
    for layer in range(depth):
        columns = []
        for row in range(rows):
            a = kept_ref[layer, row].astype(f32)
            columns.append(
                jnp.concatenate(
                    [
                        pltpu.roll(a, 1, 1)[:, :cols],
                        a[:, :cols],
                        pltpu.roll(a, lanes - 1, 1)[:, :cols],
                    ],
                    0,
                ).astype(bf16)
            )
        sources = [
            sent_ref[layer, pl.ds(row, 3)].reshape(3 * channels, cols) for row in range(rows)
        ]
        grad = lax.dot_general(
            jnp.concatenate(sources, 1),
            jnp.concatenate(columns, 1),
            (((1,), (1,)), ((), ())),
            preferred_element_type=f32,
        )
        for tap in range(3):
            grad_ref[layer, :, pl.ds(tap * 3 * channels, 3 * channels)] = grad[
                (2 - tap) * channels : (3 - tap) * channels
            ]


def last_body(q_ref, *refs, channels, rows):
    arrived, out_ref = refs[:-1], refs[-1]
    last = lax.axis_index("layer") == lax.axis_size("layer") - 1
    for row in range(rows):
        value = arrived_row(arrived, row, rows)
        value = jnp.where(last, row_of(q_ref, row, channels, rows), value)
        out_ref[pl.ds(row, channels, stride=rows), :] = value


def shifted(array, axis, by):
    count = lax.axis_size(axis)
    pairs = [(i, i + by) for i in range(count) if 0 <= i + by < count]
    return lax.ppermute(array, axis, pairs)


def exchanged(to_pair, to_cross):
    rows = lax.axis_size("row")
    pairs = [(r, r ^ 1) for r in range(rows)]
    crossing = [(r, r + 1 if r % 2 else r - 1) for r in range(1, rows - 1)]
    return lax.ppermute(to_pair, "row", pairs), lax.ppermute(to_cross, "row", crossing)


def from_sides(array):
    if lax.axis_size("col") == 2:
        other = lax.ppermute(array, "col", [(0, 1), (1, 0)])
        return other, other
    return shifted(array, "col", 1), shifted(array, "col", -1)


def total_over_tiles(grads):
    rows, cols = lax.axis_size("row"), lax.axis_size("col")
    depth = grads.shape[0]
    half = depth // 2
    odd = lax.axis_index("row") % 2 == 1
    sent = jnp.where(odd, grads[:half], grads[half:])
    own = jnp.where(odd, grads[half:], grads[:half])
    pair = [(r, r ^ 1) for r in range(rows)]
    value = own + lax.ppermute(sent, "row", pair)

    flips = [(1 << bit, 0) for bit in range(1, rows.bit_length() - 1)]
    flips += [(0, 1 << bit) for bit in range(cols.bit_length() - 1)]
    for even, uneven in zip(flips, flips[::-1]):
        pairs = []
        for r in range(rows):
            row_by, col_by = uneven if r % 2 else even
            pairs += [
                (r * cols + c, (r ^ row_by) * cols + (c ^ col_by)) for c in range(cols)
            ]
        rounded = value.astype(bf16)
        arrived = lax.ppermute(rounded, ("row", "col"), pairs)
        value = rounded.astype(f32) + arrived.astype(f32)
    other = lax.ppermute(value, "row", pair)
    first = jnp.where(odd, other, value)
    second = jnp.where(odd, value, other)
    return jnp.concatenate([first, second], 0)


def local(c_states, c_adjoints, weights):
    groups = lax.axis_size("layer")
    channels, rows, cols = c_states.shape[1:]
    depth = weights.shape[0]
    flat = (channels * rows, cols)
    c_flat, q_flat = c_states.reshape(flat), c_adjoints.reshape(flat)
    sizes = dict(channels=channels, rows=rows)
    tile_f = jax.ShapeDtypeStruct((rows, channels, cols), f32)

    strip_f = jax.ShapeDtypeStruct((channels, cols), f32)
    wide_b = jax.ShapeDtypeStruct((channels, 2 * cols), bf16)
    half = rows // 2
    more_f, more_b, upper_b, lower_b, message_b = (
        jax.ShapeDtypeStruct((count, channels, cols), kind)
        for count, kind in (
            (rows + 1, f32), (rows + 1, bf16), (half + 1, bf16), (half, bf16),
            (2 * depth + 2, bf16),
        )
    )
    flat_f = jax.ShapeDtypeStruct(flat, f32)
    edges = call(functools.partial(strip_body, depth=depth, **sizes), wide_b)(c_flat, q_flat)
    left, right = from_sides(edges)
    to_pair, to_cross, side, strip = call(
        functools.partial(message_body, depth=depth, **sizes),
        (message_b, message_b, wide_b, strip_f),
    )(c_flat, q_flat, left, right)
    pair, cross = exchanged(to_pair, to_cross)

    taps = weights.reshape(depth, channels, 3, 3, channels)
    w_fwd = jnp.transpose(taps, (0, 3, 1, 2, 4)).reshape(depth, 3 * channels, 3 * channels)
    later_taps, _ = lax.optimization_barrier((taps, to_pair))
    w_back = jnp.transpose(later_taps[:, :, ::-1, ::-1, :], (0, 3, 4, 2, 1)).reshape(
        depth, 3 * channels, 3 * channels
    )
    w_fwd, w_back = lax.optimization_barrier((w_fwd, w_back))
    coarse = step_size * jnp.sum(weights[0].astype(f32).reshape(channels, 9, channels), axis=1)
    high = coarse.astype(bf16)
    low = (coarse - high.astype(f32)).astype(bf16)
    m_fwd = jnp.concatenate([high, low, high], 1)
    m_back = jnp.concatenate([high.T, low.T, high.T], 1)

    lanes = 2 * cols
    mac = 2 * 9 * channels * channels * lanes
    total = rows + 2 * depth

    def first(kind, sender, *inputs):
        return call(
            functools.partial(first_body, depth=depth, sender=sender, **sizes),
            kind,
            [
                pltpu.VMEM((total, channels, lanes), f32),
                pltpu.VMEM((total, channels, lanes), bf16),
                pltpu.VMEM((total, channels, lanes), bf16),
            ],
            flops=mac * 44,
        )(*inputs)

    def chain(pieces, target, matrix, order):
        sendings = [piece[0] for piece in pieces]
        arrivals = []
        for turn, step in enumerate(order):
            arrived = [lax.ppermute(sending, "layer", [step]) for sending in sendings]
            arrivals += arrived
            if turn < len(order) - 1:
                sendings = [
                    call(
                        functools.partial(hop_body, start=start, **sizes),
                        jax.ShapeDtypeStruct(value.shape, bf16),
                        flops=10**10,
                    )(value, *base, target, matrix)
                    for value, (_, start, base) in zip(arrived, pieces)
                ]
        return arrivals

    inputs = (c_flat, pair, cross, side, w_fwd)
    upper, lower = first((upper_b, lower_b), True, *inputs)
    inputs = lax.optimization_barrier((inputs, upper))[0]
    (f,) = first((more_f,), False, *inputs)
    arrivals = chain(
        ((upper, 0, (c_flat, strip)), (lower, half, (c_flat,))),
        f,
        m_fwd,
        [(k, k + 1) for k in range(groups - 1)],
    )
    s = call(functools.partial(settle_body, **sizes), more_b)(c_flat, strip, *arrivals)
    s_pair, s_cross = exchanged(s, s)

    total = rows + 4 * depth
    state, g, upper, lower, kept, sources = call(
        functools.partial(second_body, depth=depth, **sizes),
        (
            flat_f,
            tile_f,
            lower_b,
            lower_b,
            jax.ShapeDtypeStruct((depth, rows, channels, lanes), bf16),
            jax.ShapeDtypeStruct((depth, rows + 2, channels, cols), bf16),
        ),
        [
            pltpu.VMEM((total, channels, lanes), f32),
            pltpu.VMEM((total, channels, lanes), bf16),
            pltpu.VMEM((total, channels, lanes), bf16),
            pltpu.VMEM((depth, total, channels, lanes), f32),
            pltpu.VMEM((total, channels, lanes), f32),
            pltpu.VMEM((total, channels, lanes), bf16),
        ],
        flops=mac * 120,
    )(c_flat, q_flat, s, s_pair, s_cross, pair, cross, side, w_fwd, w_back)
    returned = chain(
        ((upper, 0, (q_flat,)), (lower, half, (q_flat,))),
        g,
        m_back,
        [(k, k - 1) for k in range(groups - 1, 0, -1)],
    )
    grads = call(
        functools.partial(grad_body, depth=depth, **sizes),
        jax.ShapeDtypeStruct((depth, channels, 9 * channels), f32),
        flops=10**9,
    )(kept, sources)
    weight_grads = total_over_tiles(grads)
    adjoint = call(
        functools.partial(last_body, **sizes), jax.ShapeDtypeStruct(flat, f32), flops=10**10
    )(q_flat, *returned)
    return state.reshape(c_states.shape), adjoint.reshape(c_states.shape), weight_grads


def solution(mesh):
    placed = (
        P("layer", None, "row", "col"),
        P("layer", None, "row", "col"),
        P("layer", None, None),
    )
    return jax.shard_map(
        local, mesh=mesh, in_specs=placed, out_specs=placed, check_vma=False
    )
```

```python
import functools

import jax
import jax.numpy as jnp
from jax import lax
from jax.experimental import pallas as pl
from jax.experimental.pallas import tpu as pltpu
from jax.sharding import PartitionSpec as P

step_size = 0.2
VMEM_BYTES = 40 * 1024 * 1024
STRIP_VMEM_BYTES = 63 * 1024 * 1024
f32 = jnp.float32
bf16 = jnp.bfloat16


def call(body, out_shape, scratch=(), flops=0, vmem=VMEM_BYTES):
    return pl.pallas_call(
        body,
        out_shape=out_shape,
        scratch_shapes=list(scratch),
        cost_estimate=pl.CostEstimate(
            flops=int(flops), bytes_accessed=0, transcendentals=0
        ),
        compiler_params=pltpu.CompilerParams(vmem_limit_bytes=vmem),
    )


def piece_of(parts, row, rows):
    half = rows // 2
    if len(parts) == 1 or row < half:
        return parts[0], row
    return (parts[1], row - half) if row < rows else (parts[0], half)


def row_of(ref, row, channels, rows):
    return ref[pl.ds(row, channels, stride=rows), :]


def lanes_of(shape):
    return lax.broadcasted_iota(jnp.int32, shape, 1)


def slots(shape, low, width, count):
    return (lanes_of(shape) - low + width * count) // width - count


def fold_edges(rows_list, edge, low, total):
    doubled = total.shape[1] > rows_list[0].shape[1]
    cols = rows_list[0].shape[1]
    slot = slots(total.shape, low, 2 * edge, len(rows_list))
    for place, row in enumerate(rows_list):
        wide = jnp.concatenate([row, row], 1) if doubled else row
        turned = pltpu.roll(wide, (low + 2 * edge * place + edge - cols) % wide.shape[1], 1)
        total = jnp.where(slot == place, turned, total)
    return total


def join_edges(from_left, from_right, left, right, edges):
    lanes = lanes_of(from_left.shape)
    far = jnp.zeros(lanes.shape, jnp.bool_)
    for edge, low, high in edges:
        inside = (lanes >= low) & (lanes < high)
        far = far | (inside & ((lanes - low) % (2 * edge) >= edge))
    return jnp.where(far, from_right.astype(f32) * right, from_left.astype(f32) * left)


def side_lanes(joined, edge, low, place):
    lanes = joined.shape[1]
    turned = pltpu.roll(joined, (2 * lanes - (low + 2 * edge * place + edge)) % lanes, 1)
    if lanes == 128:
        return turned
    front, back = turned[:, :128], turned[:, lanes - 128 :]
    return jnp.where(lanes_of(front.shape) < 64, front, back)


def convolved(weights, slab):
    channels = slab.shape[1]
    lanes = slab.shape[2]
    product = jnp.dot(
        weights, slab.reshape(3 * channels, lanes), preferred_element_type=f32
    )
    return (
        pltpu.roll(product[:channels], 1, 1)
        + product[channels : 2 * channels]
        + pltpu.roll(product[2 * channels :], lanes - 1, 1)
    )


def flags():
    row, col = lax.axis_index("row"), lax.axis_index("col")
    up = (row > 0).astype(f32)
    down = (row < lax.axis_size("row") - 1).astype(f32)
    left = (col > 0).astype(f32)
    right = (col < lax.axis_size("col") - 1).astype(f32)
    return up, down, left, right


def even_row():
    return lax.axis_index("row") % 2 == 0


def lane_mask(cols, left, right):
    lanes = lax.broadcasted_iota(jnp.int32, (1, 2 * cols), 1)
    return jnp.where(lanes < cols, 1.0, jnp.where(lanes < cols + cols // 2, right, left))


def layout(rows, depth):
    state_edge, adjoint_edge = 3 * depth, depth
    return (state_edge, 0), (adjoint_edge, 2 * state_edge * rows)


def strip_body(c_ref, q_ref, edge_ref, *, channels, rows, depth):
    total = jnp.zeros(edge_ref.shape, f32)
    for ref, (edge, low) in zip((c_ref, q_ref), layout(rows, depth)):
        image = [row_of(ref, row, channels, rows) for row in range(rows)]
        total = fold_edges(image, edge, low, total)
    edge_ref[...] = total.astype(bf16)


def message_body(
    c_ref, q_ref, left_ref, right_ref, pair_ref, cross_ref, side_ref, strip_ref,
    *, channels, rows, depth,
):
    cols = c_ref.shape[1]
    _, _, left, right = flags()
    (c_edge, _), (q_edge, middle) = layout(rows, depth)
    edges = ((c_edge, 0, middle), (q_edge, middle, 2 * cols))
    side = join_edges(left_ref[...], right_ref[...], left, right, edges).astype(bf16)
    side_ref[...] = side
    wide = side.astype(f32)
    image = [side_lanes(wide, c_edge, 0, row) for row in range(rows)]
    strip_ref[...] = fold_edges(image, 2 * depth, 0, jnp.zeros(strip_ref.shape, f32))
    even = even_row()
    for which, ref in enumerate((c_ref, q_ref)):
        for row in range(depth):
            place = which * depth + row
            top = row_of(ref, row, channels, rows)
            bottom = row_of(ref, rows - depth + row, channels, rows)
            pair_ref[place] = jnp.where(even, bottom, top).astype(bf16)
            cross_ref[place] = jnp.where(even, top, bottom).astype(bf16)
    for half in range(2):
        part = side[:, half * cols : (half + 1) * cols]
        pair_ref[2 * depth + half] = part
        cross_ref[2 * depth + half] = part


class Beside:
    def __init__(self, pair_ref, cross_ref):
        self.pair, self.cross, self.even = pair_ref, cross_ref, even_row()

    def above(self, place):
        return jnp.where(
            self.even, self.cross[place].astype(f32), self.pair[place].astype(f32)
        )

    def below(self, place):
        return jnp.where(
            self.even, self.pair[place].astype(f32), self.cross[place].astype(f32)
        )


def strips_of(get, depth):
    return jnp.concatenate([get(2 * depth), get(2 * depth + 1)], 1)


def row_blocks(low, high, body):
    turns = 1 if high - low <= 10 else 2
    size, rest = divmod(high - low, turns)

    def turn(number, carry):
        body(low + size * number, size)
        return carry

    if size > 0:
        lax.fori_loop(0, turns, turn, 0)
    if rest > 0:
        body(low + size * turns, rest)


def convolved_rows(weights, ref, first, count):
    slab = ref[pl.ds(first - 1, count + 2)]
    return [convolved(weights, slab[place : place + 3]) for place in range(count)]


def row_flag(index, halo, rows, up, down):
    return jnp.where(index < halo, up, jnp.where(index >= halo + rows, down, 1.0))


def first_body(
    c_ref, pair_ref, cross_ref, side_ref, w_ref, *refs, channels, rows, depth, sender
):
    outs = refs[:-3]
    active = (lax.axis_index("layer") == 0) == sender

    @pl.when(jnp.logical_not(active))
    def nothing():
        for out_ref in outs:
            out_ref[...] = jnp.zeros(out_ref.shape, out_ref.dtype)

    @pl.when(active)
    def run():
        first_pass(
            c_ref, pair_ref, cross_ref, side_ref, w_ref, outs, *refs[-3:],
            channels, rows, depth,
        )


def first_pass(
    c_ref, pair_ref, cross_ref, side_ref, w_ref, outs, x_ref, a_ref, a2_ref,
    channels, rows, depth,
):
    cols = c_ref.shape[1]
    up, down, left, right = flags()
    mask = lane_mask(cols, left, right)
    halo = depth

    def put(index, own, beyond):
        x_ref[index, :, :cols] = own
        x_ref[index, :, cols:] = beyond
        a_ref[index, :, :cols] = own.astype(bf16)
        a_ref[index, :, cols:] = beyond.astype(bf16)

    (edge, low), _ = layout(rows, depth)
    own_side = side_ref[...].astype(f32)
    for row in range(rows):
        own = row_of(c_ref, row, channels, rows)
        put(halo + row, own, side_lanes(own_side, edge, low, row))
    beside = Beside(pair_ref, cross_ref)
    above_side, below_side = strips_of(beside.above, depth), strips_of(beside.below, depth)
    for row in range(depth):
        place = rows - depth + row
        put(row, beside.above(row), side_lanes(above_side, edge, low, place))
        put(halo + rows + row, beside.below(row), side_lanes(below_side, edge, low, row))

    total = rows + 2 * halo
    for layer in range(depth):
        now, later = (a_ref, a2_ref) if layer % 2 == 0 else (a2_ref, a_ref)

        def step(first, count, layer=layer, now=now, later=later):
            states = x_ref[pl.ds(first, count)]
            done = []
            for place, z in enumerate(convolved_rows(w_ref[layer], now, first, count)):
                gain = mask * (step_size * row_flag(first + place, halo, rows, up, down))
                done.append(states[place] + gain * jnp.tanh(z))
            for place, x in enumerate(done):
                x_ref[first + place] = x
                if layer < depth - 1:
                    later[first + place] = x.astype(bf16)

        row_blocks(layer + 1, total - layer - 1, step)
    image = [x_ref[halo + row, :, cols:] for row in range(rows)]
    values = [x_ref[halo + row, :, :cols] for row in range(rows)]
    values.append(fold_edges(image, 2 * depth, 0, jnp.zeros((channels, cols), f32)))
    for row, value in enumerate(values):
        out_ref, place = piece_of(outs, row, rows)
        out_ref[place] = value.astype(out_ref.dtype)


def hop_body(s_ref, c_ref, *refs, start, channels, rows):
    f_ref, m_ref, out_ref = refs[-3:]
    work = [
        (row, row_of(c_ref, row, channels, rows)) for row in range(start, start + rows // 2)
    ]
    work += [(rows, ref[...]) for ref in refs[:-3]]
    for place, (row, base) in enumerate(work):
        e = s_ref[place].astype(f32) - base
        high = e.astype(bf16)
        low = (e - high.astype(f32)).astype(bf16)
        stacked = jnp.concatenate([high, high, low], 0)
        moved = jnp.dot(m_ref[...], stacked, preferred_element_type=f32)
        out_ref[place] = (f_ref[row] + e + moved).astype(bf16)


def arrived_row(refs, row, rows):
    value = 0.0
    for pieces in zip(refs[::2], refs[1::2]):
        ref, place = piece_of(pieces, row, rows)
        value = value + ref[place].astype(f32)
    return value


def settle_body(c_ref, strip_ref, *refs, channels, rows):
    arrived, s_ref = refs[:-1], refs[-1]
    first = lax.axis_index("layer") == 0
    base = [row_of(c_ref, row, channels, rows) for row in range(rows)] + [strip_ref[...]]
    for row in range(rows + 1):
        value = arrived_row(arrived, row, rows)
        s_ref[row] = jnp.where(first, base[row], value).astype(bf16)


def second_body(
    c_ref, q_ref, s_ref, s_pair_ref, s_cross_ref, pair_ref, cross_ref, side_ref, w_ref, wt_ref,
    state_ref, g_ref, g_upper_ref, g_lower_ref, kept_ref, sent_ref,
    x_ref, a_ref, a2_ref, slope_ref, adj_ref, src_ref,
    *, channels, rows, depth,
):
    cols = c_ref.shape[1]
    up, down, left, right = flags()
    mask = lane_mask(cols, left, right)
    halo = 2 * depth
    total = rows + 2 * halo
    first = lax.axis_index("layer") == 0

    def put(index, own, beyond):
        x_ref[index, :, :cols] = own
        x_ref[index, :, cols:] = beyond
        a_ref[index, :, :cols] = own.astype(bf16)
        a_ref[index, :, cols:] = beyond.astype(bf16)

    edge = 2 * depth

    beside = Beside(s_pair_ref, s_cross_ref)
    own_side = s_ref[rows].astype(f32)
    above_side, below_side = beside.above(rows), beside.below(rows)
    for row in range(rows):
        own = jnp.where(first, row_of(c_ref, row, channels, rows), s_ref[row].astype(f32))
        state_ref[pl.ds(row, channels, stride=rows), :] = own
        put(halo + row, own, side_lanes(own_side, edge, 0, row))
    for row in range(halo):
        place = rows - halo + row
        put(
            row,
            beside.above(place),
            side_lanes(above_side, edge, 0, place),
        )
        put(
            halo + rows + row,
            beside.below(row),
            side_lanes(below_side, edge, 0, row),
        )

    def put_adj(index, own, beyond):
        adj_ref[index, :, :cols] = own
        adj_ref[index, :, cols:] = beyond

    _, (edge, low) = layout(rows, depth)
    own_side = side_ref[...].astype(f32)
    beside = Beside(pair_ref, cross_ref)
    above_side, below_side = strips_of(beside.above, depth), strips_of(beside.below, depth)
    for row in range(rows):
        put_adj(
            halo + row, row_of(q_ref, row, channels, rows), side_lanes(own_side, edge, low, row)
        )
    for row in range(depth):
        place = rows - depth + row
        put_adj(
            halo - depth + row,
            beside.above(depth + row),
            side_lanes(above_side, edge, low, place),
        )
        put_adj(
            halo + rows + row,
            beside.below(depth + row),
            side_lanes(below_side, edge, low, row),
        )

    for layer in range(depth):
        now, later = (a_ref, a2_ref) if layer % 2 == 0 else (a2_ref, a_ref)
        kept_ref[layer] = now[pl.ds(halo, rows)]

        def step(first, count, layer=layer, now=now, later=later):
            states = x_ref[pl.ds(first, count)]
            done = []
            for place, z in enumerate(convolved_rows(w_ref[layer], now, first, count)):
                gain = mask * (step_size * row_flag(first + place, halo, rows, up, down))
                t = jnp.tanh(z)
                moved = gain * t
                done.append((gain - moved * t, states[place] + moved))
            for place, (slope, x) in enumerate(done):
                slope_ref[layer, first + place] = slope
                if layer < depth - 1:
                    x_ref[first + place] = x
                    later[first + place] = x.astype(bf16)

        row_blocks(layer + 1, total - layer - 1, step)

    for layer in reversed(range(depth)):
        reach = layer + 1

        def source(first, count, layer=layer):
            part = pl.ds(first, count)
            src_ref[part] = (adj_ref[part] * slope_ref[layer, part]).astype(bf16)

        row_blocks(halo - reach, halo + rows + reach, source)

        def back(first, count, layer=layer):
            adjoints = adj_ref[pl.ds(first, count)]
            moved = convolved_rows(wt_ref[layer], src_ref, first, count)
            for place in range(count):
                adj_ref[first + place] = adjoints[place] + moved[place]

        row_blocks(halo - layer, halo + rows + layer, back)
        sent_ref[layer] = src_ref[pl.ds(halo - 1, rows + 2), :, :cols]
    for row in range(rows):
        value = adj_ref[halo + row, :, :cols]
        g_ref[row] = value
        ref, place = piece_of((g_upper_ref, g_lower_ref), row, rows)
        ref[place] = value.astype(bf16)


def grad_body(kept_ref, sent_ref, grad_ref, *, channels, rows, depth):
    lanes = kept_ref.shape[3]
    cols = lanes // 2
    for layer in range(depth):
        columns = []
        for row in range(rows):
            a = kept_ref[layer, row].astype(f32)
            columns.append(
                jnp.concatenate(
                    [
                        pltpu.roll(a, 1, 1)[:, :cols],
                        a[:, :cols],
                        pltpu.roll(a, lanes - 1, 1)[:, :cols],
                    ],
                    0,
                ).astype(bf16)
            )
        sources = [
            sent_ref[layer, pl.ds(row, 3)].reshape(3 * channels, cols) for row in range(rows)
        ]
        grad = lax.dot_general(
            jnp.concatenate(sources, 1),
            jnp.concatenate(columns, 1),
            (((1,), (1,)), ((), ())),
            preferred_element_type=f32,
        )
        for tap in range(3):
            grad_ref[layer, :, pl.ds(tap * 3 * channels, 3 * channels)] = grad[
                (2 - tap) * channels : (3 - tap) * channels
            ]


def last_body(q_ref, half_ref, other_ref, *refs, channels, rows):
    arrived, out_ref, grad_ref = refs[:-2], refs[-2], refs[-1]
    half = half_ref.shape[0]
    odd = jnp.logical_not(even_row()).astype(jnp.int32)
    grad_ref[pl.ds(odd * half, half)] = half_ref[...]
    grad_ref[pl.ds((1 - odd) * half, half)] = other_ref[...]
    last = lax.axis_index("layer") == lax.axis_size("layer") - 1
    for row in range(rows):
        value = arrived_row(arrived, row, rows)
        value = jnp.where(last, row_of(q_ref, row, channels, rows), value)
        out_ref[pl.ds(row, channels, stride=rows), :] = value


def shifted(array, axis, by):
    count = lax.axis_size(axis)
    pairs = [(i, i + by) for i in range(count) if 0 <= i + by < count]
    return lax.ppermute(array, axis, pairs)


def exchanged(to_pair, to_cross):
    rows = lax.axis_size("row")
    pairs = [(r, r ^ 1) for r in range(rows)]
    crossing = [(r, r + 1 if r % 2 else r - 1) for r in range(1, rows - 1)]
    return lax.ppermute(to_pair, "row", pairs), lax.ppermute(to_cross, "row", crossing)


def from_sides(array):
    if lax.axis_size("col") == 2:
        other = lax.ppermute(array, "col", [(0, 1), (1, 0)])
        return other, other
    return shifted(array, "col", 1), shifted(array, "col", -1)


def total_over_tiles(grads):
    rows, cols = lax.axis_size("row"), lax.axis_size("col")
    depth = grads.shape[0]
    half = depth // 2
    odd = lax.axis_index("row") % 2 == 1
    sent = jnp.where(odd, grads[:half], grads[half:])
    own = jnp.where(odd, grads[half:], grads[:half])
    pair = [(r, r ^ 1) for r in range(rows)]
    value = own + lax.ppermute(sent, "row", pair)

    flips = [(1 << bit, 0) for bit in range(1, rows.bit_length() - 1)]
    flips += [(0, 1 << bit) for bit in range(cols.bit_length() - 1)]
    for even, uneven in zip(flips, flips[::-1]):
        pairs = []
        for r in range(rows):
            row_by, col_by = uneven if r % 2 else even
            pairs += [
                (r * cols + c, (r ^ row_by) * cols + (c ^ col_by)) for c in range(cols)
            ]
        rounded = value.astype(bf16)
        arrived = lax.ppermute(rounded, ("row", "col"), pairs)
        value = rounded.astype(f32) + arrived.astype(f32)
    return value, lax.ppermute(value, "row", pair)


def local(c_states, c_adjoints, weights):
    groups = lax.axis_size("layer")
    channels, rows, cols = c_states.shape[1:]
    depth = weights.shape[0]
    flat = (channels * rows, cols)
    c_flat, q_flat = c_states.reshape(flat), c_adjoints.reshape(flat)
    sizes = dict(channels=channels, rows=rows)
    tile_f = jax.ShapeDtypeStruct((rows, channels, cols), f32)

    strip_f = jax.ShapeDtypeStruct((channels, cols), f32)
    wide_b = jax.ShapeDtypeStruct((channels, 2 * cols), bf16)
    half = rows // 2
    more_f, more_b, upper_b, lower_b, message_b = (
        jax.ShapeDtypeStruct((count, channels, cols), kind)
        for count, kind in (
            (rows + 1, f32), (rows + 1, bf16), (half + 1, bf16), (half, bf16),
            (2 * depth + 2, bf16),
        )
    )
    flat_f = jax.ShapeDtypeStruct(flat, f32)
    edges = call(
        functools.partial(strip_body, depth=depth, **sizes), wide_b, vmem=STRIP_VMEM_BYTES
    )(c_flat, q_flat)
    left, right = from_sides(edges)
    to_pair, to_cross, side, strip = call(
        functools.partial(message_body, depth=depth, **sizes),
        (message_b, message_b, wide_b, strip_f),
    )(c_flat, q_flat, left, right)
    pair, cross = exchanged(to_pair, to_cross)

    taps = weights.reshape(depth, channels, 3, 3, channels)
    w_fwd = jnp.transpose(taps, (0, 3, 1, 2, 4)).reshape(depth, 3 * channels, 3 * channels)
    later_taps, _ = lax.optimization_barrier((taps, to_pair))
    w_back = jnp.transpose(later_taps[:, :, ::-1, ::-1, :], (0, 3, 4, 2, 1)).reshape(
        depth, 3 * channels, 3 * channels
    )
    w_fwd, w_back = lax.optimization_barrier((w_fwd, w_back))
    coarse = step_size * jnp.sum(weights[0].astype(f32).reshape(channels, 9, channels), axis=1)
    high = coarse.astype(bf16)
    low = (coarse - high.astype(f32)).astype(bf16)
    m_fwd = jnp.concatenate([high, low, high], 1)
    m_back = jnp.concatenate([high.T, low.T, high.T], 1)

    lanes = 2 * cols
    mac = 2 * 9 * channels * channels * lanes
    total = rows + 2 * depth

    def first(kind, sender, *inputs):
        return call(
            functools.partial(first_body, depth=depth, sender=sender, **sizes),
            kind,
            [
                pltpu.VMEM((total, channels, lanes), f32),
                pltpu.VMEM((total, channels, lanes), bf16),
                pltpu.VMEM((total, channels, lanes), bf16),
            ],
            flops=mac * 44,
        )(*inputs)

    def chain(pieces, target, matrix, order):
        sendings = [piece[0] for piece in pieces]
        arrivals = []
        for turn, step in enumerate(order):
            arrived = [lax.ppermute(sending, "layer", [step]) for sending in sendings]
            arrivals += arrived
            if turn < len(order) - 1:
                sendings = [
                    call(
                        functools.partial(hop_body, start=start, **sizes),
                        jax.ShapeDtypeStruct(value.shape, bf16),
                        flops=10**10,
                    )(value, *base, target, matrix)
                    for value, (_, start, base) in zip(arrived, pieces)
                ]
        return arrivals

    inputs = (c_flat, pair, cross, side, w_fwd)
    upper, lower = first((upper_b, lower_b), True, *inputs)
    inputs = lax.optimization_barrier((inputs, upper))[0]
    (f,) = first((more_f,), False, *inputs)
    arrivals = chain(
        ((upper, 0, (c_flat, strip)), (lower, half, (c_flat,))),
        f,
        m_fwd,
        [(k, k + 1) for k in range(groups - 1)],
    )
    s = call(functools.partial(settle_body, **sizes), more_b)(c_flat, strip, *arrivals)
    s_pair, s_cross = exchanged(s, s)

    total = rows + 4 * depth
    state, g, upper, lower, kept, sources = call(
        functools.partial(second_body, depth=depth, **sizes),
        (
            flat_f,
            tile_f,
            lower_b,
            lower_b,
            jax.ShapeDtypeStruct((depth, rows, channels, lanes), bf16),
            jax.ShapeDtypeStruct((depth, rows + 2, channels, cols), bf16),
        ),
        [
            pltpu.VMEM((total, channels, lanes), f32),
            pltpu.VMEM((total, channels, lanes), bf16),
            pltpu.VMEM((total, channels, lanes), bf16),
            pltpu.VMEM((depth, total, channels, lanes), f32),
            pltpu.VMEM((total, channels, lanes), f32),
            pltpu.VMEM((total, channels, lanes), bf16),
        ],
        flops=mac * 120,
    )(c_flat, q_flat, s, s_pair, s_cross, pair, cross, side, w_fwd, w_back)
    returned = chain(
        ((upper, 0, (q_flat,)), (lower, half, (q_flat,))),
        g,
        m_back,
        [(k, k - 1) for k in range(groups - 1, 0, -1)],
    )
    grads = call(
        functools.partial(grad_body, depth=depth, **sizes),
        jax.ShapeDtypeStruct((depth, channels, 9 * channels), f32),
        flops=10**9,
    )(kept, sources)
    own_half, other_half = total_over_tiles(grads)
    adjoint, weight_grads = call(
        functools.partial(last_body, **sizes),
        (flat_f, jax.ShapeDtypeStruct((depth, channels, 9 * channels), f32)),
        flops=10**10,
    )(q_flat, own_half, other_half, *returned)
    return state.reshape(c_states.shape), adjoint.reshape(c_states.shape), weight_grads


def solution(mesh):
    placed = (
        P("layer", None, "row", "col"),
        P("layer", None, "row", "col"),
        P("layer", None, None),
    )
    return jax.shard_map(
        local, mesh=mesh, in_specs=placed, out_specs=placed, check_vma=False
    )
```

```python
import functools

import jax
import jax.numpy as jnp
from jax import lax
from jax.experimental import pallas as pl
from jax.experimental.pallas import tpu as pltpu
from jax.sharding import PartitionSpec as P

step_size = 0.2
VMEM_BYTES = 40 * 1024 * 1024
STRIP_VMEM_BYTES = 63 * 1024 * 1024
PARTS = 4
f32 = jnp.float32
bf16 = jnp.bfloat16
HERE = pl.BlockSpec(memory_space=pltpu.VMEM)
AWAY = pl.BlockSpec(memory_space=pltpu.HBM)


def call(body, out_shape, scratch=(), flops=0, vmem=VMEM_BYTES, **more):
    return pl.pallas_call(
        body,
        out_shape=out_shape,
        scratch_shapes=list(scratch),
        cost_estimate=pl.CostEstimate(
            flops=int(flops), bytes_accessed=0, transcendentals=0
        ),
        compiler_params=pltpu.CompilerParams(vmem_limit_bytes=vmem),
        **more,
    )


def in_parts(source, target, arrived, first):
    size = source.shape[0] // PARTS
    return [
        pltpu.make_async_copy(
            source.at[pl.ds(part * size, size)],
            target.at[pl.ds(part * size, size)],
            arrived.at[first + part],
        )
        for part in range(PARTS)
    ]


def piece_of(parts, row, rows):
    half = rows // 2
    if len(parts) == 1 or row < half:
        return parts[0], row
    return (parts[1], row - half) if row < rows else (parts[0], half)


def row_of(ref, row, channels, rows):
    return ref[pl.ds(row, channels, stride=rows), :]


def lanes_of(shape):
    return lax.broadcasted_iota(jnp.int32, shape, 1)


def slots(shape, low, width, count):
    return (lanes_of(shape) - low + width * count) // width - count


def fold_edges(rows_list, edge, low, total):
    doubled = total.shape[1] > rows_list[0].shape[1]
    cols = rows_list[0].shape[1]
    slot = slots(total.shape, low, 2 * edge, len(rows_list))
    for place, row in enumerate(rows_list):
        wide = jnp.concatenate([row, row], 1) if doubled else row
        turned = pltpu.roll(wide, (low + 2 * edge * place + edge - cols) % wide.shape[1], 1)
        total = jnp.where(slot == place, turned, total)
    return total


def join_edges(from_left, from_right, left, right, edges):
    lanes = lanes_of(from_left.shape)
    far = jnp.zeros(lanes.shape, jnp.bool_)
    for edge, low, high in edges:
        inside = (lanes >= low) & (lanes < high)
        far = far | (inside & ((lanes - low) % (2 * edge) >= edge))
    return jnp.where(far, from_right.astype(f32) * right, from_left.astype(f32) * left)


def side_lanes(joined, edge, low, place):
    lanes = joined.shape[1]
    turned = pltpu.roll(joined, (2 * lanes - (low + 2 * edge * place + edge)) % lanes, 1)
    if lanes == 128:
        return turned
    front, back = turned[:, :128], turned[:, lanes - 128 :]
    return jnp.where(lanes_of(front.shape) < 64, front, back)


def convolved(weights, slab):
    channels = slab.shape[1]
    lanes = slab.shape[2]
    product = jnp.dot(
        weights, slab.reshape(3 * channels, lanes), preferred_element_type=f32
    )
    return (
        pltpu.roll(product[:channels], 1, 1)
        + product[channels : 2 * channels]
        + pltpu.roll(product[2 * channels :], lanes - 1, 1)
    )


def flags():
    row, col = lax.axis_index("row"), lax.axis_index("col")
    up = (row > 0).astype(f32)
    down = (row < lax.axis_size("row") - 1).astype(f32)
    left = (col > 0).astype(f32)
    right = (col < lax.axis_size("col") - 1).astype(f32)
    return up, down, left, right


def even_row():
    return lax.axis_index("row") % 2 == 0


def lane_mask(cols, left, right):
    lanes = lax.broadcasted_iota(jnp.int32, (1, 2 * cols), 1)
    return jnp.where(lanes < cols, 1.0, jnp.where(lanes < cols + cols // 2, right, left))


def layout(rows, depth):
    state_edge, adjoint_edge = 3 * depth, depth
    return (state_edge, 0), (adjoint_edge, 2 * state_edge * rows)


def strip_body(c_hbm, q_hbm, edge_ref, c_ref, q_ref, arrived, *, channels, rows, depth):
    copies = in_parts(c_hbm, c_ref, arrived, 0) + in_parts(q_hbm, q_ref, arrived, PARTS)
    for copy in copies:
        copy.start()
    for copy in copies:
        copy.wait()
    total = jnp.zeros(edge_ref.shape, f32)
    for ref, (edge, low) in zip((c_ref, q_ref), layout(rows, depth)):
        image = [row_of(ref, row, channels, rows) for row in range(rows)]
        total = fold_edges(image, edge, low, total)
    edge_ref[...] = total.astype(bf16)


def message_body(
    c_ref, q_ref, left_ref, right_ref, pair_ref, cross_ref, side_ref, strip_ref,
    *, channels, rows, depth,
):
    cols = c_ref.shape[1]
    _, _, left, right = flags()
    (c_edge, _), (q_edge, middle) = layout(rows, depth)
    edges = ((c_edge, 0, middle), (q_edge, middle, 2 * cols))
    side = join_edges(left_ref[...], right_ref[...], left, right, edges).astype(bf16)
    side_ref[...] = side
    wide = side.astype(f32)
    image = [side_lanes(wide, c_edge, 0, row) for row in range(rows)]
    strip_ref[...] = fold_edges(image, 2 * depth, 0, jnp.zeros(strip_ref.shape, f32))
    even = even_row()
    for which, ref in enumerate((c_ref, q_ref)):
        for row in range(depth):
            place = which * depth + row
            top = row_of(ref, row, channels, rows)
            bottom = row_of(ref, rows - depth + row, channels, rows)
            pair_ref[place] = jnp.where(even, bottom, top).astype(bf16)
            cross_ref[place] = jnp.where(even, top, bottom).astype(bf16)
    for half in range(2):
        part = side[:, half * cols : (half + 1) * cols]
        pair_ref[2 * depth + half] = part
        cross_ref[2 * depth + half] = part


class Beside:
    def __init__(self, pair_ref, cross_ref):
        self.pair, self.cross, self.even = pair_ref, cross_ref, even_row()

    def above(self, place):
        return jnp.where(
            self.even, self.cross[place].astype(f32), self.pair[place].astype(f32)
        )

    def below(self, place):
        return jnp.where(
            self.even, self.pair[place].astype(f32), self.cross[place].astype(f32)
        )


def strips_of(get, depth):
    return jnp.concatenate([get(2 * depth), get(2 * depth + 1)], 1)


def row_blocks(low, high, body):
    turns = 1 if high - low <= 10 else 2
    size, rest = divmod(high - low, turns)

    def turn(number, carry):
        body(low + size * number, size)
        return carry

    if size > 0:
        lax.fori_loop(0, turns, turn, 0)
    if rest > 0:
        body(low + size * turns, rest)


def convolved_rows(weights, ref, first, count):
    slab = ref[pl.ds(first - 1, count + 2)]
    return [convolved(weights, slab[place : place + 3]) for place in range(count)]


def row_flag(index, halo, rows, up, down):
    return jnp.where(index < halo, up, jnp.where(index >= halo + rows, down, 1.0))


def first_body(
    c_ref, pair_ref, cross_ref, side_ref, w_ref, *refs, channels, rows, depth, sender
):
    outs = refs[:-3]
    active = (lax.axis_index("layer") == 0) == sender

    @pl.when(jnp.logical_not(active))
    def nothing():
        for out_ref in outs:
            out_ref[...] = jnp.zeros(out_ref.shape, out_ref.dtype)

    @pl.when(active)
    def run():
        first_pass(
            c_ref, pair_ref, cross_ref, side_ref, w_ref, outs, *refs[-3:],
            channels, rows, depth,
        )


def first_pass(
    c_ref, pair_ref, cross_ref, side_ref, w_ref, outs, x_ref, a_ref, a2_ref,
    channels, rows, depth,
):
    cols = c_ref.shape[1]
    up, down, left, right = flags()
    mask = lane_mask(cols, left, right)
    halo = depth

    def put(index, own, beyond):
        x_ref[index, :, :cols] = own
        x_ref[index, :, cols:] = beyond
        a_ref[index, :, :cols] = own.astype(bf16)
        a_ref[index, :, cols:] = beyond.astype(bf16)

    (edge, low), _ = layout(rows, depth)
    own_side = side_ref[...].astype(f32)
    for row in range(rows):
        own = row_of(c_ref, row, channels, rows)
        put(halo + row, own, side_lanes(own_side, edge, low, row))
    beside = Beside(pair_ref, cross_ref)
    above_side, below_side = strips_of(beside.above, depth), strips_of(beside.below, depth)
    for row in range(depth):
        place = rows - depth + row
        put(row, beside.above(row), side_lanes(above_side, edge, low, place))
        put(halo + rows + row, beside.below(row), side_lanes(below_side, edge, low, row))

    total = rows + 2 * halo
    for layer in range(depth):
        now, later = (a_ref, a2_ref) if layer % 2 == 0 else (a2_ref, a_ref)

        def step(first, count, layer=layer, now=now, later=later):
            states = x_ref[pl.ds(first, count)]
            done = []
            for place, z in enumerate(convolved_rows(w_ref[layer], now, first, count)):
                gain = mask * (step_size * row_flag(first + place, halo, rows, up, down))
                done.append(states[place] + gain * jnp.tanh(z))
            for place, x in enumerate(done):
                x_ref[first + place] = x
                if layer < depth - 1:
                    later[first + place] = x.astype(bf16)

        row_blocks(layer + 1, total - layer - 1, step)
    image = [x_ref[halo + row, :, cols:] for row in range(rows)]
    values = [x_ref[halo + row, :, :cols] for row in range(rows)]
    values.append(fold_edges(image, 2 * depth, 0, jnp.zeros((channels, cols), f32)))
    for row, value in enumerate(values):
        out_ref, place = piece_of(outs, row, rows)
        out_ref[place] = value.astype(out_ref.dtype)


def hop_body(s_ref, c_ref, *refs, start, channels, rows):
    f_ref, m_ref, out_ref = refs[-3:]
    work = [
        (row, row_of(c_ref, row, channels, rows)) for row in range(start, start + rows // 2)
    ]
    work += [(rows, ref[...]) for ref in refs[:-3]]
    for place, (row, base) in enumerate(work):
        e = s_ref[place].astype(f32) - base
        high = e.astype(bf16)
        low = (e - high.astype(f32)).astype(bf16)
        stacked = jnp.concatenate([high, high, low], 0)
        moved = jnp.dot(m_ref[...], stacked, preferred_element_type=f32)
        out_ref[place] = (f_ref[row] + e + moved).astype(bf16)


def arrived_row(refs, row, rows):
    value = 0.0
    for pieces in zip(refs[::2], refs[1::2]):
        ref, place = piece_of(pieces, row, rows)
        value = value + ref[place].astype(f32)
    return value


def settle_body(c_ref, strip_ref, *refs, channels, rows):
    arrived, s_ref = refs[:-1], refs[-1]
    first = lax.axis_index("layer") == 0
    base = [row_of(c_ref, row, channels, rows) for row in range(rows)] + [strip_ref[...]]
    for row in range(rows + 1):
        value = arrived_row(arrived, row, rows)
        s_ref[row] = jnp.where(first, base[row], value).astype(bf16)


def second_body(
    c_ref, q_ref, s_ref, s_pair_ref, s_cross_ref, pair_ref, cross_ref, side_ref, w_ref, wt_ref,
    state_hbm, g_ref, g_upper_ref, g_lower_ref, kept_ref, sent_ref,
    x_ref, a_ref, a2_ref, slope_ref, adj_ref, src_ref, state_ref, left_here,
    *, channels, rows, depth,
):
    cols = c_ref.shape[1]
    up, down, left, right = flags()
    mask = lane_mask(cols, left, right)
    halo = 2 * depth
    total = rows + 2 * halo
    first = lax.axis_index("layer") == 0

    def put(index, own, beyond):
        x_ref[index, :, :cols] = own
        x_ref[index, :, cols:] = beyond
        a_ref[index, :, :cols] = own.astype(bf16)
        a_ref[index, :, cols:] = beyond.astype(bf16)

    edge = 2 * depth

    beside = Beside(s_pair_ref, s_cross_ref)
    own_side = s_ref[rows].astype(f32)
    above_side, below_side = beside.above(rows), beside.below(rows)
    for row in range(rows):
        own = jnp.where(first, row_of(c_ref, row, channels, rows), s_ref[row].astype(f32))
        state_ref[pl.ds(row, channels, stride=rows), :] = own
        put(halo + row, own, side_lanes(own_side, edge, 0, row))
    leaving = in_parts(state_ref, state_hbm, left_here, 0)
    for copy in leaving:
        copy.start()
    for row in range(halo):
        place = rows - halo + row
        put(
            row,
            beside.above(place),
            side_lanes(above_side, edge, 0, place),
        )
        put(
            halo + rows + row,
            beside.below(row),
            side_lanes(below_side, edge, 0, row),
        )

    def put_adj(index, own, beyond):
        adj_ref[index, :, :cols] = own
        adj_ref[index, :, cols:] = beyond

    _, (edge, low) = layout(rows, depth)
    own_side = side_ref[...].astype(f32)
    beside = Beside(pair_ref, cross_ref)
    above_side, below_side = strips_of(beside.above, depth), strips_of(beside.below, depth)
    for row in range(rows):
        put_adj(
            halo + row, row_of(q_ref, row, channels, rows), side_lanes(own_side, edge, low, row)
        )
    for row in range(depth):
        place = rows - depth + row
        put_adj(
            halo - depth + row,
            beside.above(depth + row),
            side_lanes(above_side, edge, low, place),
        )
        put_adj(
            halo + rows + row,
            beside.below(depth + row),
            side_lanes(below_side, edge, low, row),
        )

    for layer in range(depth):
        now, later = (a_ref, a2_ref) if layer % 2 == 0 else (a2_ref, a_ref)
        kept_ref[layer] = now[pl.ds(halo, rows)]

        def step(first, count, layer=layer, now=now, later=later):
            states = x_ref[pl.ds(first, count)]
            done = []
            for place, z in enumerate(convolved_rows(w_ref[layer], now, first, count)):
                gain = mask * (step_size * row_flag(first + place, halo, rows, up, down))
                t = jnp.tanh(z)
                moved = gain * t
                done.append((gain - moved * t, states[place] + moved))
            for place, (slope, x) in enumerate(done):
                slope_ref[layer, first + place] = slope
                if layer < depth - 1:
                    x_ref[first + place] = x
                    later[first + place] = x.astype(bf16)

        row_blocks(layer + 1, total - layer - 1, step)

    for layer in reversed(range(depth)):
        reach = layer + 1

        def source(first, count, layer=layer):
            part = pl.ds(first, count)
            src_ref[part] = (adj_ref[part] * slope_ref[layer, part]).astype(bf16)

        row_blocks(halo - reach, halo + rows + reach, source)

        def back(first, count, layer=layer):
            adjoints = adj_ref[pl.ds(first, count)]
            moved = convolved_rows(wt_ref[layer], src_ref, first, count)
            for place in range(count):
                adj_ref[first + place] = adjoints[place] + moved[place]

        row_blocks(halo - layer, halo + rows + layer, back)
        sent_ref[layer] = src_ref[pl.ds(halo - 1, rows + 2), :, :cols]
    for row in range(rows):
        value = adj_ref[halo + row, :, :cols]
        g_ref[row] = value
        ref, place = piece_of((g_upper_ref, g_lower_ref), row, rows)
        ref[place] = value.astype(bf16)
    for copy in leaving:
        copy.wait()


def grad_body(kept_ref, sent_ref, grad_ref, *, channels, rows, depth):
    lanes = kept_ref.shape[3]
    cols = lanes // 2
    for layer in range(depth):
        columns = []
        for row in range(rows):
            a = kept_ref[layer, row].astype(f32)
            columns.append(
                jnp.concatenate(
                    [
                        pltpu.roll(a, 1, 1)[:, :cols],
                        a[:, :cols],
                        pltpu.roll(a, lanes - 1, 1)[:, :cols],
                    ],
                    0,
                ).astype(bf16)
            )
        sources = [
            sent_ref[layer, pl.ds(row, 3)].reshape(3 * channels, cols) for row in range(rows)
        ]
        grad = lax.dot_general(
            jnp.concatenate(sources, 1),
            jnp.concatenate(columns, 1),
            (((1,), (1,)), ((), ())),
            preferred_element_type=f32,
        )
        for tap in range(3):
            grad_ref[layer, :, pl.ds(tap * 3 * channels, 3 * channels)] = grad[
                (2 - tap) * channels : (3 - tap) * channels
            ]


def last_body(q_ref, half_ref, other_ref, *refs, channels, rows):
    arrived, (out_hbm, grad_hbm, out_ref, left_here) = refs[:-4], refs[-4:]
    half = half_ref.shape[0]
    odd = jnp.logical_not(even_row()).astype(jnp.int32)
    leaving = []
    for which, ref in enumerate((half_ref, other_ref)):
        low = half * (odd if which == 0 else 1 - odd)
        for layer in range(half):
            leaving.append(
                pltpu.make_async_copy(
                    ref.at[layer], grad_hbm.at[low + layer], left_here.at[len(leaving)]
                )
            )
    for copy in leaving:
        copy.start()
    last = lax.axis_index("layer") == lax.axis_size("layer") - 1
    for row in range(rows):
        value = arrived_row(arrived, row, rows)
        value = jnp.where(last, row_of(q_ref, row, channels, rows), value)
        out_ref[pl.ds(row, channels, stride=rows), :] = value
    parts = in_parts(out_ref, out_hbm, left_here, 2 * half)
    for copy in parts:
        copy.start()
    for copy in leaving + parts:
        copy.wait()


def shifted(array, axis, by):
    count = lax.axis_size(axis)
    pairs = [(i, i + by) for i in range(count) if 0 <= i + by < count]
    return lax.ppermute(array, axis, pairs)


def exchanged(to_pair, to_cross):
    rows = lax.axis_size("row")
    pairs = [(r, r ^ 1) for r in range(rows)]
    crossing = [(r, r + 1 if r % 2 else r - 1) for r in range(1, rows - 1)]
    return lax.ppermute(to_pair, "row", pairs), lax.ppermute(to_cross, "row", crossing)


def from_sides(array):
    if lax.axis_size("col") == 2:
        other = lax.ppermute(array, "col", [(0, 1), (1, 0)])
        return other, other
    return shifted(array, "col", 1), shifted(array, "col", -1)


def total_over_tiles(grads):
    rows, cols = lax.axis_size("row"), lax.axis_size("col")
    depth = grads.shape[0]
    half = depth // 2
    odd = lax.axis_index("row") % 2 == 1
    sent = jnp.where(odd, grads[:half], grads[half:])
    own = jnp.where(odd, grads[half:], grads[:half])
    pair = [(r, r ^ 1) for r in range(rows)]
    value = own + lax.ppermute(sent, "row", pair)

    flips = [(1 << bit, 0) for bit in range(1, rows.bit_length() - 1)]
    flips += [(0, 1 << bit) for bit in range(cols.bit_length() - 1)]
    for even, uneven in zip(flips, flips[::-1]):
        pairs = []
        for r in range(rows):
            row_by, col_by = uneven if r % 2 else even
            pairs += [
                (r * cols + c, (r ^ row_by) * cols + (c ^ col_by)) for c in range(cols)
            ]
        rounded = value.astype(bf16)
        arrived = lax.ppermute(rounded, ("row", "col"), pairs)
        value = rounded.astype(f32) + arrived.astype(f32)
    return value, lax.ppermute(value, "row", pair)


def local(c_states, c_adjoints, weights):
    groups = lax.axis_size("layer")
    channels, rows, cols = c_states.shape[1:]
    depth = weights.shape[0]
    flat = (channels * rows, cols)
    c_flat, q_flat = c_states.reshape(flat), c_adjoints.reshape(flat)
    sizes = dict(channels=channels, rows=rows)
    tile_f = jax.ShapeDtypeStruct((rows, channels, cols), f32)

    strip_f = jax.ShapeDtypeStruct((channels, cols), f32)
    wide_b = jax.ShapeDtypeStruct((channels, 2 * cols), bf16)
    half = rows // 2
    more_f, more_b, upper_b, lower_b, message_b = (
        jax.ShapeDtypeStruct((count, channels, cols), kind)
        for count, kind in (
            (rows + 1, f32), (rows + 1, bf16), (half + 1, bf16), (half, bf16),
            (2 * depth + 2, bf16),
        )
    )
    flat_f = jax.ShapeDtypeStruct(flat, f32)
    edges = call(
        functools.partial(strip_body, depth=depth, **sizes),
        wide_b,
        [
            pltpu.VMEM(flat, f32),
            pltpu.VMEM(flat, f32),
            pltpu.SemaphoreType.DMA((2 * PARTS,)),
        ],
        vmem=STRIP_VMEM_BYTES,
        in_specs=[AWAY, AWAY],
        out_specs=HERE,
    )(c_flat, q_flat)
    left, right = from_sides(edges)
    to_pair, to_cross, side, strip = call(
        functools.partial(message_body, depth=depth, **sizes),
        (message_b, message_b, wide_b, strip_f),
    )(c_flat, q_flat, left, right)
    pair, cross = exchanged(to_pair, to_cross)

    taps = weights.reshape(depth, channels, 3, 3, channels)
    w_fwd = jnp.transpose(taps, (0, 3, 1, 2, 4)).reshape(depth, 3 * channels, 3 * channels)
    later_taps, _ = lax.optimization_barrier((taps, to_pair))
    w_back = jnp.transpose(later_taps[:, :, ::-1, ::-1, :], (0, 3, 4, 2, 1)).reshape(
        depth, 3 * channels, 3 * channels
    )
    w_fwd, w_back = lax.optimization_barrier((w_fwd, w_back))
    coarse = step_size * jnp.sum(weights[0].astype(f32).reshape(channels, 9, channels), axis=1)
    high = coarse.astype(bf16)
    low = (coarse - high.astype(f32)).astype(bf16)
    m_fwd = jnp.concatenate([high, low, high], 1)
    m_back = jnp.concatenate([high.T, low.T, high.T], 1)

    lanes = 2 * cols
    mac = 2 * 9 * channels * channels * lanes
    total = rows + 2 * depth

    def first(kind, sender, *inputs):
        return call(
            functools.partial(first_body, depth=depth, sender=sender, **sizes),
            kind,
            [
                pltpu.VMEM((total, channels, lanes), f32),
                pltpu.VMEM((total, channels, lanes), bf16),
                pltpu.VMEM((total, channels, lanes), bf16),
            ],
            flops=mac * 44,
        )(*inputs)

    def chain(pieces, target, matrix, order):
        sendings = [piece[0] for piece in pieces]
        arrivals = []
        for turn, step in enumerate(order):
            arrived = [lax.ppermute(sending, "layer", [step]) for sending in sendings]
            arrivals += arrived
            if turn < len(order) - 1:
                sendings = [
                    call(
                        functools.partial(hop_body, start=start, **sizes),
                        jax.ShapeDtypeStruct(value.shape, bf16),
                        flops=10**10,
                    )(value, *base, target, matrix)
                    for value, (_, start, base) in zip(arrived, pieces)
                ]
        return arrivals

    inputs = (c_flat, pair, cross, side, w_fwd)
    upper, lower = first((upper_b, lower_b), True, *inputs)
    inputs = lax.optimization_barrier((inputs, upper))[0]
    (f,) = first((more_f,), False, *inputs)
    arrivals = chain(
        ((upper, 0, (c_flat, strip)), (lower, half, (c_flat,))),
        f,
        m_fwd,
        [(k, k + 1) for k in range(groups - 1)],
    )
    s = call(functools.partial(settle_body, **sizes), more_b)(c_flat, strip, *arrivals)
    s_pair, s_cross = exchanged(s, s)

    total = rows + 4 * depth
    state, g, upper, lower, kept, sources = call(
        functools.partial(second_body, depth=depth, **sizes),
        (
            flat_f,
            tile_f,
            lower_b,
            lower_b,
            jax.ShapeDtypeStruct((depth, rows, channels, lanes), bf16),
            jax.ShapeDtypeStruct((depth, rows + 2, channels, cols), bf16),
        ),
        [
            pltpu.VMEM((total, channels, lanes), f32),
            pltpu.VMEM((total, channels, lanes), bf16),
            pltpu.VMEM((total, channels, lanes), bf16),
            pltpu.VMEM((depth, total, channels, lanes), f32),
            pltpu.VMEM((total, channels, lanes), f32),
            pltpu.VMEM((total, channels, lanes), bf16),
            pltpu.VMEM(flat, f32),
            pltpu.SemaphoreType.DMA((PARTS,)),
        ],
        flops=mac * 120,
        out_specs=(AWAY, HERE, HERE, HERE, HERE, HERE),
    )(c_flat, q_flat, s, s_pair, s_cross, pair, cross, side, w_fwd, w_back)
    returned = chain(
        ((upper, 0, (q_flat,)), (lower, half, (q_flat,))),
        g,
        m_back,
        [(k, k - 1) for k in range(groups - 1, 0, -1)],
    )
    grads = call(
        functools.partial(grad_body, depth=depth, **sizes),
        jax.ShapeDtypeStruct((depth, channels, 9 * channels), f32),
        flops=10**9,
    )(kept, sources)
    own_half, other_half = total_over_tiles(grads)
    adjoint, weight_grads = call(
        functools.partial(last_body, **sizes),
        (flat_f, jax.ShapeDtypeStruct((depth, channels, 9 * channels), f32)),
        [pltpu.VMEM(flat, f32), pltpu.SemaphoreType.DMA((depth + PARTS,))],
        flops=10**10,
        out_specs=(AWAY, AWAY),
    )(q_flat, own_half, other_half, *returned)
    return state.reshape(c_states.shape), adjoint.reshape(c_states.shape), weight_grads


def solution(mesh):
    placed = (
        P("layer", None, "row", "col"),
        P("layer", None, "row", "col"),
        P("layer", None, None),
    )
    return jax.shard_map(
        local, mesh=mesh, in_specs=placed, out_specs=placed, check_vma=False
    )
```

```python
import functools

import jax
import jax.numpy as jnp
from jax import lax
from jax.experimental import pallas as pl
from jax.experimental.pallas import tpu as pltpu
from jax.sharding import PartitionSpec as P

step_size = 0.2
VMEM_BYTES = 40 * 1024 * 1024
STRIP_VMEM_BYTES = 63 * 1024 * 1024
PARTS = 4
f32 = jnp.float32
bf16 = jnp.bfloat16
HERE = pl.BlockSpec(memory_space=pltpu.VMEM)
AWAY = pl.BlockSpec(memory_space=pltpu.HBM)


def call(body, out_shape, scratch=(), flops=0, vmem=VMEM_BYTES, **more):
    return pl.pallas_call(
        body,
        out_shape=out_shape,
        scratch_shapes=list(scratch),
        cost_estimate=pl.CostEstimate(
            flops=int(flops), bytes_accessed=0, transcendentals=0
        ),
        compiler_params=pltpu.CompilerParams(vmem_limit_bytes=vmem),
        **more,
    )


def in_parts(source, target, arrived, first):
    size = source.shape[0] // PARTS
    return [
        pltpu.make_async_copy(
            source.at[pl.ds(part * size, size)],
            target.at[pl.ds(part * size, size)],
            arrived.at[first + part],
        )
        for part in range(PARTS)
    ]


def piece_of(parts, row, rows):
    half = rows // 2
    if len(parts) == 1 or row < half:
        return parts[0], row
    return (parts[1], row - half) if row < rows else (parts[0], half)


def row_of(ref, row, channels, rows):
    return ref[pl.ds(row, channels, stride=rows), :]


def lanes_of(shape):
    return lax.broadcasted_iota(jnp.int32, shape, 1)


def slots(shape, low, width, count):
    return (lanes_of(shape) - low + width * count) // width - count


def fold_edges(rows_list, edge, low, total):
    doubled = total.shape[1] > rows_list[0].shape[1]
    cols = rows_list[0].shape[1]
    slot = slots(total.shape, low, 2 * edge, len(rows_list))
    for place, row in enumerate(rows_list):
        wide = jnp.concatenate([row, row], 1) if doubled else row
        turned = pltpu.roll(wide, (low + 2 * edge * place + edge - cols) % wide.shape[1], 1)
        total = jnp.where(slot == place, turned, total)
    return total


def join_edges(from_left, from_right, left, right, edges):
    lanes = lanes_of(from_left.shape)
    far = jnp.zeros(lanes.shape, jnp.bool_)
    for edge, low, high in edges:
        inside = (lanes >= low) & (lanes < high)
        far = far | (inside & ((lanes - low) % (2 * edge) >= edge))
    return jnp.where(far, from_right.astype(f32) * right, from_left.astype(f32) * left)


def side_lanes(joined, edge, low, place):
    lanes = joined.shape[1]
    turned = pltpu.roll(joined, (2 * lanes - (low + 2 * edge * place + edge)) % lanes, 1)
    if lanes == 128:
        return turned
    front, back = turned[:, :128], turned[:, lanes - 128 :]
    return jnp.where(lanes_of(front.shape) < 64, front, back)


def convolved(weights, slab):
    channels = slab.shape[1]
    lanes = slab.shape[2]
    product = jnp.dot(
        weights, slab.reshape(3 * channels, lanes), preferred_element_type=f32
    )
    return (
        pltpu.roll(product[:channels], 1, 1)
        + product[channels : 2 * channels]
        + pltpu.roll(product[2 * channels :], lanes - 1, 1)
    )


def flags():
    row, col = lax.axis_index("row"), lax.axis_index("col")
    up = (row > 0).astype(f32)
    down = (row < lax.axis_size("row") - 1).astype(f32)
    left = (col > 0).astype(f32)
    right = (col < lax.axis_size("col") - 1).astype(f32)
    return up, down, left, right


def even_row():
    return lax.axis_index("row") % 2 == 0


def lane_mask(cols, left, right):
    lanes = lax.broadcasted_iota(jnp.int32, (1, 2 * cols), 1)
    return jnp.where(lanes < cols, 1.0, jnp.where(lanes < cols + cols // 2, right, left))


def layout(rows, depth):
    state_edge, adjoint_edge = 3 * depth, depth
    return (state_edge, 0), (adjoint_edge, 2 * state_edge * rows)


def strip_body(c_hbm, q_hbm, edge_ref, c_ref, q_ref, arrived, *, channels, rows, depth):
    copies = in_parts(c_hbm, c_ref, arrived, 0) + in_parts(q_hbm, q_ref, arrived, PARTS)
    for copy in copies:
        copy.start()
    for copy in copies:
        copy.wait()
    total = jnp.zeros(edge_ref.shape, f32)
    for ref, (edge, low) in zip((c_ref, q_ref), layout(rows, depth)):
        image = [row_of(ref, row, channels, rows) for row in range(rows)]
        total = fold_edges(image, edge, low, total)
    edge_ref[...] = total.astype(bf16)


def message_body(
    c_ref, q_ref, left_ref, right_ref, pair_ref, cross_ref, side_ref, strip_ref,
    *, channels, rows, depth,
):
    cols = c_ref.shape[1]
    _, _, left, right = flags()
    (c_edge, _), (q_edge, middle) = layout(rows, depth)
    edges = ((c_edge, 0, middle), (q_edge, middle, 2 * cols))
    side = join_edges(left_ref[...], right_ref[...], left, right, edges).astype(bf16)
    side_ref[...] = side
    wide = side.astype(f32)
    image = [side_lanes(wide, c_edge, 0, row) for row in range(rows)]
    strip_ref[...] = fold_edges(image, 2 * depth, 0, jnp.zeros(strip_ref.shape, f32))
    even = even_row()
    for which, ref in enumerate((c_ref, q_ref)):
        for row in range(depth):
            place = which * depth + row
            top = row_of(ref, row, channels, rows)
            bottom = row_of(ref, rows - depth + row, channels, rows)
            pair_ref[place] = jnp.where(even, bottom, top).astype(bf16)
            cross_ref[place] = jnp.where(even, top, bottom).astype(bf16)
    for half in range(2):
        part = side[:, half * cols : (half + 1) * cols]
        pair_ref[2 * depth + half] = part
        cross_ref[2 * depth + half] = part


class Beside:
    def __init__(self, pair_ref, cross_ref):
        self.pair, self.cross, self.even = pair_ref, cross_ref, even_row()

    def above(self, place):
        return jnp.where(
            self.even, self.cross[place].astype(f32), self.pair[place].astype(f32)
        )

    def below(self, place):
        return jnp.where(
            self.even, self.pair[place].astype(f32), self.cross[place].astype(f32)
        )


def strips_of(get, depth):
    return jnp.concatenate([get(2 * depth), get(2 * depth + 1)], 1)


def row_blocks(low, high, body):
    turns = 1 if high - low <= 32 else 2
    size, rest = divmod(high - low, turns)

    def turn(number, carry):
        body(low + size * number, size)
        return carry

    if size > 0:
        lax.fori_loop(0, turns, turn, 0)
    if rest > 0:
        body(low + size * turns, rest)


def convolved_rows(weights, ref, first, count):
    slab = ref[pl.ds(first - 1, count + 2)]
    return [convolved(weights, slab[place : place + 3]) for place in range(count)]


def row_flag(index, halo, rows, up, down):
    return jnp.where(index < halo, up, jnp.where(index >= halo + rows, down, 1.0))


def first_body(
    c_ref, pair_ref, cross_ref, side_ref, w_ref, *refs, channels, rows, depth, sender
):
    outs = refs[:-3]
    active = (lax.axis_index("layer") == 0) == sender

    @pl.when(jnp.logical_not(active))
    def nothing():
        for out_ref in outs:
            out_ref[...] = jnp.zeros(out_ref.shape, out_ref.dtype)

    @pl.when(active)
    def run():
        first_pass(
            c_ref, pair_ref, cross_ref, side_ref, w_ref, outs, *refs[-3:],
            channels, rows, depth,
        )


def first_pass(
    c_ref, pair_ref, cross_ref, side_ref, w_ref, outs, x_ref, a_ref, a2_ref,
    channels, rows, depth,
):
    cols = c_ref.shape[1]
    up, down, left, right = flags()
    mask = lane_mask(cols, left, right)
    halo = depth

    def put(index, own, beyond):
        x_ref[index, :, :cols] = own
        x_ref[index, :, cols:] = beyond
        a_ref[index, :, :cols] = own.astype(bf16)
        a_ref[index, :, cols:] = beyond.astype(bf16)

    (edge, low), _ = layout(rows, depth)
    own_side = side_ref[...].astype(f32)
    for row in range(rows):
        own = row_of(c_ref, row, channels, rows)
        put(halo + row, own, side_lanes(own_side, edge, low, row))
    beside = Beside(pair_ref, cross_ref)
    above_side, below_side = strips_of(beside.above, depth), strips_of(beside.below, depth)
    for row in range(depth):
        place = rows - depth + row
        put(row, beside.above(row), side_lanes(above_side, edge, low, place))
        put(halo + rows + row, beside.below(row), side_lanes(below_side, edge, low, row))

    total = rows + 2 * halo
    for layer in range(depth):
        now, later = (a_ref, a2_ref) if layer % 2 == 0 else (a2_ref, a_ref)

        def step(first, count, layer=layer, now=now, later=later):
            states = x_ref[pl.ds(first, count)]
            done = []
            for place, z in enumerate(convolved_rows(w_ref[layer], now, first, count)):
                gain = mask * (step_size * row_flag(first + place, halo, rows, up, down))
                done.append(states[place] + gain * jnp.tanh(z))
            for place, x in enumerate(done):
                x_ref[first + place] = x
                if layer < depth - 1:
                    later[first + place] = x.astype(bf16)

        row_blocks(layer + 1, total - layer - 1, step)
    image = [x_ref[halo + row, :, cols:] for row in range(rows)]
    values = [x_ref[halo + row, :, :cols] for row in range(rows)]
    values.append(fold_edges(image, 2 * depth, 0, jnp.zeros((channels, cols), f32)))
    for row, value in enumerate(values):
        out_ref, place = piece_of(outs, row, rows)
        out_ref[place] = value.astype(out_ref.dtype)


def hop_body(s_ref, c_ref, *refs, start, channels, rows):
    f_ref, m_ref, out_ref = refs[-3:]
    work = [
        (row, row_of(c_ref, row, channels, rows)) for row in range(start, start + rows // 2)
    ]
    work += [(rows, ref[...]) for ref in refs[:-3]]
    for place, (row, base) in enumerate(work):
        e = s_ref[place].astype(f32) - base
        high = e.astype(bf16)
        low = (e - high.astype(f32)).astype(bf16)
        stacked = jnp.concatenate([high, high, low], 0)
        moved = jnp.dot(m_ref[...], stacked, preferred_element_type=f32)
        out_ref[place] = (f_ref[row] + e + moved).astype(bf16)


def arrived_row(refs, row, rows):
    value = 0.0
    for pieces in zip(refs[::2], refs[1::2]):
        ref, place = piece_of(pieces, row, rows)
        value = value + ref[place].astype(f32)
    return value


def settle_body(c_ref, strip_ref, *refs, channels, rows):
    arrived, s_ref = refs[:-1], refs[-1]
    first = lax.axis_index("layer") == 0
    base = [row_of(c_ref, row, channels, rows) for row in range(rows)] + [strip_ref[...]]
    for row in range(rows + 1):
        value = arrived_row(arrived, row, rows)
        s_ref[row] = jnp.where(first, base[row], value).astype(bf16)


def second_body(
    c_ref, q_ref, s_ref, s_pair_ref, s_cross_ref, pair_ref, cross_ref, side_ref, w_ref, wt_ref,
    state_hbm, g_ref, g_upper_ref, g_lower_ref, kept_ref, sent_ref,
    x_ref, a_ref, a2_ref, slope_ref, adj_ref, src_ref, state_ref, left_here,
    *, channels, rows, depth,
):
    cols = c_ref.shape[1]
    up, down, left, right = flags()
    mask = lane_mask(cols, left, right)
    halo = 2 * depth
    total = rows + 2 * halo
    first = lax.axis_index("layer") == 0

    def put(index, own, beyond):
        x_ref[index, :, :cols] = own
        x_ref[index, :, cols:] = beyond
        a_ref[index, :, :cols] = own.astype(bf16)
        a_ref[index, :, cols:] = beyond.astype(bf16)

    edge = 2 * depth

    beside = Beside(s_pair_ref, s_cross_ref)
    own_side = s_ref[rows].astype(f32)
    above_side, below_side = beside.above(rows), beside.below(rows)
    for row in range(rows):
        own = jnp.where(first, row_of(c_ref, row, channels, rows), s_ref[row].astype(f32))
        state_ref[pl.ds(row, channels, stride=rows), :] = own
        put(halo + row, own, side_lanes(own_side, edge, 0, row))
    leaving = in_parts(state_ref, state_hbm, left_here, 0)
    for copy in leaving:
        copy.start()
    for row in range(halo):
        place = rows - halo + row
        put(
            row,
            beside.above(place),
            side_lanes(above_side, edge, 0, place),
        )
        put(
            halo + rows + row,
            beside.below(row),
            side_lanes(below_side, edge, 0, row),
        )

    def put_adj(index, own, beyond):
        adj_ref[index, :, :cols] = own
        adj_ref[index, :, cols:] = beyond

    _, (edge, low) = layout(rows, depth)
    own_side = side_ref[...].astype(f32)
    beside = Beside(pair_ref, cross_ref)
    above_side, below_side = strips_of(beside.above, depth), strips_of(beside.below, depth)
    for row in range(rows):
        put_adj(
            halo + row, row_of(q_ref, row, channels, rows), side_lanes(own_side, edge, low, row)
        )
    for row in range(depth):
        place = rows - depth + row
        put_adj(
            halo - depth + row,
            beside.above(depth + row),
            side_lanes(above_side, edge, low, place),
        )
        put_adj(
            halo + rows + row,
            beside.below(depth + row),
            side_lanes(below_side, edge, low, row),
        )

    for layer in range(depth):
        now, later = (a_ref, a2_ref) if layer % 2 == 0 else (a2_ref, a_ref)
        kept_ref[layer] = now[pl.ds(halo, rows)]

        def step(first, count, layer=layer, now=now, later=later):
            states = x_ref[pl.ds(first, count)]
            done = []
            for place, z in enumerate(convolved_rows(w_ref[layer], now, first, count)):
                gain = mask * (step_size * row_flag(first + place, halo, rows, up, down))
                t = jnp.tanh(z)
                moved = gain * t
                done.append((gain - moved * t, states[place] + moved))
            for place, (slope, x) in enumerate(done):
                slope_ref[layer, first + place] = slope
                if layer < depth - 1:
                    x_ref[first + place] = x
                    later[first + place] = x.astype(bf16)

        row_blocks(layer + 1, total - layer - 1, step)

    for layer in reversed(range(depth)):
        reach = layer + 1

        def source(first, count, layer=layer):
            part = pl.ds(first, count)
            src_ref[part] = (adj_ref[part] * slope_ref[layer, part]).astype(bf16)

        row_blocks(halo - reach, halo + rows + reach, source)

        def back(first, count, layer=layer):
            adjoints = adj_ref[pl.ds(first, count)]
            moved = convolved_rows(wt_ref[layer], src_ref, first, count)
            for place in range(count):
                adj_ref[first + place] = adjoints[place] + moved[place]

        row_blocks(halo - layer, halo + rows + layer, back)
        sent_ref[layer] = src_ref[pl.ds(halo - 1, rows + 2), :, :cols]
    for row in range(rows):
        value = adj_ref[halo + row, :, :cols]
        g_ref[row] = value
        ref, place = piece_of((g_upper_ref, g_lower_ref), row, rows)
        ref[place] = value.astype(bf16)
    for copy in leaving:
        copy.wait()


def grad_body(kept_ref, sent_ref, grad_ref, *, channels, rows, depth):
    lanes = kept_ref.shape[3]
    cols = lanes // 2
    for layer in range(depth):
        columns = []
        for row in range(rows):
            a = kept_ref[layer, row].astype(f32)
            columns.append(
                jnp.concatenate(
                    [
                        pltpu.roll(a, 1, 1)[:, :cols],
                        a[:, :cols],
                        pltpu.roll(a, lanes - 1, 1)[:, :cols],
                    ],
                    0,
                ).astype(bf16)
            )
        sources = [
            sent_ref[layer, pl.ds(row, 3)].reshape(3 * channels, cols) for row in range(rows)
        ]
        grad = lax.dot_general(
            jnp.concatenate(sources, 1),
            jnp.concatenate(columns, 1),
            (((1,), (1,)), ((), ())),
            preferred_element_type=f32,
        )
        for tap in range(3):
            grad_ref[layer, :, pl.ds(tap * 3 * channels, 3 * channels)] = grad[
                (2 - tap) * channels : (3 - tap) * channels
            ]


def last_body(q_ref, half_ref, other_ref, *refs, channels, rows):
    arrived, (out_hbm, grad_hbm, out_ref, left_here) = refs[:-4], refs[-4:]
    half = half_ref.shape[0]
    odd = jnp.logical_not(even_row()).astype(jnp.int32)
    leaving = []
    for which, ref in enumerate((half_ref, other_ref)):
        low = half * (odd if which == 0 else 1 - odd)
        for layer in range(half):
            leaving.append(
                pltpu.make_async_copy(
                    ref.at[layer], grad_hbm.at[low + layer], left_here.at[len(leaving)]
                )
            )
    for copy in leaving:
        copy.start()
    last = lax.axis_index("layer") == lax.axis_size("layer") - 1
    for row in range(rows):
        value = arrived_row(arrived, row, rows)
        value = jnp.where(last, row_of(q_ref, row, channels, rows), value)
        out_ref[pl.ds(row, channels, stride=rows), :] = value
    parts = in_parts(out_ref, out_hbm, left_here, 2 * half)
    for copy in parts:
        copy.start()
    for copy in leaving + parts:
        copy.wait()


def shifted(array, axis, by):
    count = lax.axis_size(axis)
    pairs = [(i, i + by) for i in range(count) if 0 <= i + by < count]
    return lax.ppermute(array, axis, pairs)


def exchanged(to_pair, to_cross):
    rows = lax.axis_size("row")
    pairs = [(r, r ^ 1) for r in range(rows)]
    crossing = [(r, r + 1 if r % 2 else r - 1) for r in range(1, rows - 1)]
    return lax.ppermute(to_pair, "row", pairs), lax.ppermute(to_cross, "row", crossing)


def from_sides(array):
    if lax.axis_size("col") == 2:
        other = lax.ppermute(array, "col", [(0, 1), (1, 0)])
        return other, other
    return shifted(array, "col", 1), shifted(array, "col", -1)


def total_over_tiles(grads):
    rows, cols = lax.axis_size("row"), lax.axis_size("col")
    depth = grads.shape[0]
    half = depth // 2
    odd = lax.axis_index("row") % 2 == 1
    sent = jnp.where(odd, grads[:half], grads[half:])
    own = jnp.where(odd, grads[half:], grads[:half])
    pair = [(r, r ^ 1) for r in range(rows)]
    value = own + lax.ppermute(sent, "row", pair)

    flips = [(1 << bit, 0) for bit in range(1, rows.bit_length() - 1)]
    flips += [(0, 1 << bit) for bit in range(cols.bit_length() - 1)]
    for even, uneven in zip(flips, flips[::-1]):
        pairs = []
        for r in range(rows):
            row_by, col_by = uneven if r % 2 else even
            pairs += [
                (r * cols + c, (r ^ row_by) * cols + (c ^ col_by)) for c in range(cols)
            ]
        rounded = value.astype(bf16)
        arrived = lax.ppermute(rounded, ("row", "col"), pairs)
        value = rounded.astype(f32) + arrived.astype(f32)
    return value, lax.ppermute(value, "row", pair)


def local(c_states, c_adjoints, weights):
    groups = lax.axis_size("layer")
    channels, rows, cols = c_states.shape[1:]
    depth = weights.shape[0]
    flat = (channels * rows, cols)
    c_flat, q_flat = c_states.reshape(flat), c_adjoints.reshape(flat)
    sizes = dict(channels=channels, rows=rows)
    tile_f = jax.ShapeDtypeStruct((rows, channels, cols), f32)

    strip_f = jax.ShapeDtypeStruct((channels, cols), f32)
    wide_b = jax.ShapeDtypeStruct((channels, 2 * cols), bf16)
    half = rows // 2
    more_f, more_b, upper_b, lower_b, message_b = (
        jax.ShapeDtypeStruct((count, channels, cols), kind)
        for count, kind in (
            (rows + 1, f32), (rows + 1, bf16), (half + 1, bf16), (half, bf16),
            (2 * depth + 2, bf16),
        )
    )
    flat_f = jax.ShapeDtypeStruct(flat, f32)
    edges = call(
        functools.partial(strip_body, depth=depth, **sizes),
        wide_b,
        [
            pltpu.VMEM(flat, f32),
            pltpu.VMEM(flat, f32),
            pltpu.SemaphoreType.DMA((2 * PARTS,)),
        ],
        vmem=STRIP_VMEM_BYTES,
        in_specs=[AWAY, AWAY],
        out_specs=HERE,
    )(c_flat, q_flat)
    left, right = from_sides(edges)
    to_pair, to_cross, side, strip = call(
        functools.partial(message_body, depth=depth, **sizes),
        (message_b, message_b, wide_b, strip_f),
    )(c_flat, q_flat, left, right)
    pair, cross = exchanged(to_pair, to_cross)

    taps = weights.reshape(depth, channels, 3, 3, channels)
    w_fwd = jnp.transpose(taps, (0, 3, 1, 2, 4)).reshape(depth, 3 * channels, 3 * channels)
    later_taps, _ = lax.optimization_barrier((taps, to_pair))
    w_back = jnp.transpose(later_taps[:, :, ::-1, ::-1, :], (0, 3, 4, 2, 1)).reshape(
        depth, 3 * channels, 3 * channels
    )
    w_fwd, w_back = lax.optimization_barrier((w_fwd, w_back))
    coarse = step_size * jnp.sum(weights[0].astype(f32).reshape(channels, 9, channels), axis=1)
    high = coarse.astype(bf16)
    low = (coarse - high.astype(f32)).astype(bf16)
    m_fwd = jnp.concatenate([high, low, high], 1)
    m_back = jnp.concatenate([high.T, low.T, high.T], 1)

    lanes = 2 * cols
    mac = 2 * 9 * channels * channels * lanes
    total = rows + 2 * depth

    def first(kind, sender, *inputs):
        return call(
            functools.partial(first_body, depth=depth, sender=sender, **sizes),
            kind,
            [
                pltpu.VMEM((total, channels, lanes), f32),
                pltpu.VMEM((total, channels, lanes), bf16),
                pltpu.VMEM((total, channels, lanes), bf16),
            ],
            flops=mac * 44,
        )(*inputs)

    def chain(pieces, target, matrix, order):
        sendings = [piece[0] for piece in pieces]
        arrivals = []
        for turn, step in enumerate(order):
            arrived = [lax.ppermute(sending, "layer", [step]) for sending in sendings]
            arrivals += arrived
            if turn < len(order) - 1:
                sendings = [
                    call(
                        functools.partial(hop_body, start=start, **sizes),
                        jax.ShapeDtypeStruct(value.shape, bf16),
                        flops=10**10,
                    )(value, *base, target, matrix)
                    for value, (_, start, base) in zip(arrived, pieces)
                ]
        return arrivals

    inputs = (c_flat, pair, cross, side, w_fwd)
    upper, lower = first((upper_b, lower_b), True, *inputs)
    inputs = lax.optimization_barrier((inputs, upper))[0]
    (f,) = first((more_f,), False, *inputs)
    arrivals = chain(
        ((upper, 0, (c_flat, strip)), (lower, half, (c_flat,))),
        f,
        m_fwd,
        [(k, k + 1) for k in range(groups - 1)],
    )
    s = call(functools.partial(settle_body, **sizes), more_b)(c_flat, strip, *arrivals)
    s_pair, s_cross = exchanged(s, s)

    total = rows + 4 * depth
    state, g, upper, lower, kept, sources = call(
        functools.partial(second_body, depth=depth, **sizes),
        (
            flat_f,
            tile_f,
            lower_b,
            lower_b,
            jax.ShapeDtypeStruct((depth, rows, channels, lanes), bf16),
            jax.ShapeDtypeStruct((depth, rows + 2, channels, cols), bf16),
        ),
        [
            pltpu.VMEM((total, channels, lanes), f32),
            pltpu.VMEM((total, channels, lanes), bf16),
            pltpu.VMEM((total, channels, lanes), bf16),
            pltpu.VMEM((depth, total, channels, lanes), f32),
            pltpu.VMEM((total, channels, lanes), f32),
            pltpu.VMEM((total, channels, lanes), bf16),
            pltpu.VMEM(flat, f32),
            pltpu.SemaphoreType.DMA((PARTS,)),
        ],
        flops=mac * 120,
        out_specs=(AWAY, HERE, HERE, HERE, HERE, HERE),
    )(c_flat, q_flat, s, s_pair, s_cross, pair, cross, side, w_fwd, w_back)
    returned = chain(
        ((upper, 0, (q_flat,)), (lower, half, (q_flat,))),
        g,
        m_back,
        [(k, k - 1) for k in range(groups - 1, 0, -1)],
    )
    grads = call(
        functools.partial(grad_body, depth=depth, **sizes),
        jax.ShapeDtypeStruct((depth, channels, 9 * channels), f32),
        flops=10**9,
    )(kept, sources)
    own_half, other_half = total_over_tiles(grads)
    adjoint, weight_grads = call(
        functools.partial(last_body, **sizes),
        (flat_f, jax.ShapeDtypeStruct((depth, channels, 9 * channels), f32)),
        [pltpu.VMEM(flat, f32), pltpu.SemaphoreType.DMA((depth + PARTS,))],
        flops=10**10,
        out_specs=(AWAY, AWAY),
    )(q_flat, own_half, other_half, *returned)
    return state.reshape(c_states.shape), adjoint.reshape(c_states.shape), weight_grads


def solution(mesh):
    placed = (
        P("layer", None, "row", "col"),
        P("layer", None, "row", "col"),
        P("layer", None, None),
    )
    return jax.shard_map(
        local, mesh=mesh, in_specs=placed, out_specs=placed, check_vma=False
    )
```

```python
import functools

import jax
import jax.numpy as jnp
from jax import lax
from jax.experimental import pallas as pl
from jax.experimental.pallas import tpu as pltpu
from jax.sharding import PartitionSpec as P

step_size = 0.2
VMEM_BYTES = 40 * 1024 * 1024
STRIP_VMEM_BYTES = 63 * 1024 * 1024
PARTS = 4
f32 = jnp.float32
bf16 = jnp.bfloat16
HERE = pl.BlockSpec(memory_space=pltpu.VMEM)
AWAY = pl.BlockSpec(memory_space=pltpu.HBM)


def call(body, out_shape, scratch=(), flops=0, vmem=VMEM_BYTES, **more):
    return pl.pallas_call(
        body,
        out_shape=out_shape,
        scratch_shapes=list(scratch),
        cost_estimate=pl.CostEstimate(
            flops=int(flops), bytes_accessed=0, transcendentals=0
        ),
        compiler_params=pltpu.CompilerParams(vmem_limit_bytes=vmem),
        **more,
    )


def in_parts(source, target, arrived, first):
    size = source.shape[0] // PARTS
    return [
        pltpu.make_async_copy(
            source.at[pl.ds(part * size, size)],
            target.at[pl.ds(part * size, size)],
            arrived.at[first + part],
        )
        for part in range(PARTS)
    ]


def piece_of(parts, row, rows):
    half = rows // 2
    if len(parts) == 1 or row < half:
        return parts[0], row
    return (parts[1], row - half) if row < rows else (parts[0], half)


def row_of(ref, row, channels, rows):
    return ref[pl.ds(row, channels, stride=rows), :]


def lanes_of(shape):
    return lax.broadcasted_iota(jnp.int32, shape, 1)


def slots(shape, low, width, count):
    return (lanes_of(shape) - low + width * count) // width - count


def fold_edges(rows_list, edge, low, total):
    doubled = total.shape[1] > rows_list[0].shape[1]
    cols = rows_list[0].shape[1]
    slot = slots(total.shape, low, 2 * edge, len(rows_list))
    for place, row in enumerate(rows_list):
        wide = jnp.concatenate([row, row], 1) if doubled else row
        turned = pltpu.roll(wide, (low + 2 * edge * place + edge - cols) % wide.shape[1], 1)
        total = jnp.where(slot == place, turned, total)
    return total


def join_edges(from_left, from_right, left, right, edges):
    lanes = lanes_of(from_left.shape)
    far = jnp.zeros(lanes.shape, jnp.bool_)
    for edge, low, high in edges:
        inside = (lanes >= low) & (lanes < high)
        far = far | (inside & ((lanes - low) % (2 * edge) >= edge))
    return jnp.where(far, from_right.astype(f32) * right, from_left.astype(f32) * left)


def side_lanes(joined, edge, low, place):
    lanes = joined.shape[1]
    turned = pltpu.roll(joined, (2 * lanes - (low + 2 * edge * place + edge)) % lanes, 1)
    if lanes == 128:
        return turned
    front, back = turned[:, :128], turned[:, lanes - 128 :]
    return jnp.where(lanes_of(front.shape) < 64, front, back)


def convolved(weights, slab):
    channels = slab.shape[1]
    lanes = slab.shape[2]
    product = jnp.dot(
        weights, slab.reshape(3 * channels, lanes), preferred_element_type=f32
    )
    return (
        pltpu.roll(product[:channels], 1, 1)
        + product[channels : 2 * channels]
        + pltpu.roll(product[2 * channels :], lanes - 1, 1)
    )


def flags():
    row, col = lax.axis_index("row"), lax.axis_index("col")
    up = (row > 0).astype(f32)
    down = (row < lax.axis_size("row") - 1).astype(f32)
    left = (col > 0).astype(f32)
    right = (col < lax.axis_size("col") - 1).astype(f32)
    return up, down, left, right


def even_row():
    return lax.axis_index("row") % 2 == 0


def lane_mask(cols, left, right):
    lanes = lax.broadcasted_iota(jnp.int32, (1, 2 * cols), 1)
    return jnp.where(lanes < cols, 1.0, jnp.where(lanes < cols + cols // 2, right, left))


def layout(rows, depth):
    state_edge, adjoint_edge = 3 * depth, depth
    return (state_edge, 0), (adjoint_edge, 2 * state_edge * rows)


def strip_body(c_hbm, q_hbm, edge_ref, c_ref, q_ref, arrived, *, channels, rows, depth):
    copies = in_parts(c_hbm, c_ref, arrived, 0) + in_parts(q_hbm, q_ref, arrived, PARTS)
    for copy in copies:
        copy.start()
    for copy in copies:
        copy.wait()
    total = jnp.zeros(edge_ref.shape, f32)
    for ref, (edge, low) in zip((c_ref, q_ref), layout(rows, depth)):
        image = [row_of(ref, row, channels, rows) for row in range(rows)]
        total = fold_edges(image, edge, low, total)
    edge_ref[...] = total.astype(bf16)


def message_body(
    c_ref, q_ref, left_ref, right_ref, pair_ref, cross_ref, side_ref, strip_ref,
    *, channels, rows, depth,
):
    cols = c_ref.shape[1]
    _, _, left, right = flags()
    (c_edge, _), (q_edge, middle) = layout(rows, depth)
    edges = ((c_edge, 0, middle), (q_edge, middle, 2 * cols))
    side = join_edges(left_ref[...], right_ref[...], left, right, edges).astype(bf16)
    side_ref[...] = side
    wide = side.astype(f32)
    image = [side_lanes(wide, c_edge, 0, row) for row in range(rows)]
    strip_ref[...] = fold_edges(image, 2 * depth, 0, jnp.zeros(strip_ref.shape, f32))
    even = even_row()
    for which, ref in enumerate((c_ref, q_ref)):
        for row in range(depth):
            place = which * depth + row
            top = row_of(ref, row, channels, rows)
            bottom = row_of(ref, rows - depth + row, channels, rows)
            pair_ref[place] = jnp.where(even, bottom, top).astype(bf16)
            cross_ref[place] = jnp.where(even, top, bottom).astype(bf16)
    for half in range(2):
        part = side[:, half * cols : (half + 1) * cols]
        pair_ref[2 * depth + half] = part
        cross_ref[2 * depth + half] = part


class Beside:
    def __init__(self, pair_ref, cross_ref):
        self.pair, self.cross, self.even = pair_ref, cross_ref, even_row()

    def above(self, place):
        return jnp.where(
            self.even, self.cross[place].astype(f32), self.pair[place].astype(f32)
        )

    def below(self, place):
        return jnp.where(
            self.even, self.pair[place].astype(f32), self.cross[place].astype(f32)
        )


def strips_of(get, depth):
    return jnp.concatenate([get(2 * depth), get(2 * depth + 1)], 1)


def row_blocks(low, high, body):
    body(low, high - low)


def convolved_rows(weights, ref, first, count):
    slab = ref[pl.ds(first - 1, count + 2)]
    return [convolved(weights, slab[place : place + 3]) for place in range(count)]


def row_flag(index, halo, rows, up, down):
    if index < halo:
        return up
    return down if index >= halo + rows else 1.0


def first_body(
    c_ref, pair_ref, cross_ref, side_ref, w_ref, *refs, channels, rows, depth, sender
):
    outs = refs[:-3]
    active = (lax.axis_index("layer") == 0) == sender

    @pl.when(jnp.logical_not(active))
    def nothing():
        for out_ref in outs:
            out_ref[...] = jnp.zeros(out_ref.shape, out_ref.dtype)

    @pl.when(active)
    def run():
        first_pass(
            c_ref, pair_ref, cross_ref, side_ref, w_ref, outs, *refs[-3:],
            channels, rows, depth,
        )


def first_pass(
    c_ref, pair_ref, cross_ref, side_ref, w_ref, outs, x_ref, a_ref, a2_ref,
    channels, rows, depth,
):
    cols = c_ref.shape[1]
    up, down, left, right = flags()
    mask = lane_mask(cols, left, right)
    halo = depth

    def put(index, own, beyond):
        x_ref[index, :, :cols] = own
        x_ref[index, :, cols:] = beyond
        a_ref[index, :, :cols] = own.astype(bf16)
        a_ref[index, :, cols:] = beyond.astype(bf16)

    (edge, low), _ = layout(rows, depth)
    own_side = side_ref[...].astype(f32)
    for row in range(rows):
        own = row_of(c_ref, row, channels, rows)
        put(halo + row, own, side_lanes(own_side, edge, low, row))
    beside = Beside(pair_ref, cross_ref)
    above_side, below_side = strips_of(beside.above, depth), strips_of(beside.below, depth)
    for row in range(depth):
        place = rows - depth + row
        put(row, beside.above(row), side_lanes(above_side, edge, low, place))
        put(halo + rows + row, beside.below(row), side_lanes(below_side, edge, low, row))

    total = rows + 2 * halo
    for layer in range(depth):
        now, later = (a_ref, a2_ref) if layer % 2 == 0 else (a2_ref, a_ref)

        def step(first, count, layer=layer, now=now, later=later):
            states = x_ref[pl.ds(first, count)]
            done = []
            for place, z in enumerate(convolved_rows(w_ref[layer], now, first, count)):
                gain = mask * (step_size * row_flag(first + place, halo, rows, up, down))
                done.append(states[place] + gain * jnp.tanh(z))
            for place, x in enumerate(done):
                x_ref[first + place] = x
                if layer < depth - 1:
                    later[first + place] = x.astype(bf16)

        row_blocks(layer + 1, total - layer - 1, step)
    image = [x_ref[halo + row, :, cols:] for row in range(rows)]
    values = [x_ref[halo + row, :, :cols] for row in range(rows)]
    values.append(fold_edges(image, 2 * depth, 0, jnp.zeros((channels, cols), f32)))
    for row, value in enumerate(values):
        out_ref, place = piece_of(outs, row, rows)
        out_ref[place] = value.astype(out_ref.dtype)


def hop_body(s_ref, c_ref, *refs, start, channels, rows):
    f_ref, m_ref, out_ref = refs[-3:]
    work = [
        (row, row_of(c_ref, row, channels, rows)) for row in range(start, start + rows // 2)
    ]
    work += [(rows, ref[...]) for ref in refs[:-3]]
    for place, (row, base) in enumerate(work):
        e = s_ref[place].astype(f32) - base
        high = e.astype(bf16)
        low = (e - high.astype(f32)).astype(bf16)
        stacked = jnp.concatenate([high, high, low], 0)
        moved = jnp.dot(m_ref[...], stacked, preferred_element_type=f32)
        out_ref[place] = (f_ref[row] + e + moved).astype(bf16)


def arrived_row(refs, row, rows):
    value = 0.0
    for pieces in zip(refs[::2], refs[1::2]):
        ref, place = piece_of(pieces, row, rows)
        value = value + ref[place].astype(f32)
    return value


def settle_body(c_ref, strip_ref, *refs, channels, rows):
    arrived, s_ref = refs[:-1], refs[-1]
    first = lax.axis_index("layer") == 0
    base = [row_of(c_ref, row, channels, rows) for row in range(rows)] + [strip_ref[...]]
    for row in range(rows + 1):
        value = arrived_row(arrived, row, rows)
        s_ref[row] = jnp.where(first, base[row], value).astype(bf16)


def second_body(
    c_ref, q_ref, s_ref, s_pair_ref, s_cross_ref, pair_ref, cross_ref, side_ref, w_ref, wt_ref,
    state_hbm, g_ref, g_upper_ref, g_lower_ref, kept_ref, sent_ref,
    x_ref, a_ref, a2_ref, slope_ref, adj_ref, src_ref, state_ref, left_here,
    *, channels, rows, depth,
):
    cols = c_ref.shape[1]
    up, down, left, right = flags()
    mask = lane_mask(cols, left, right)
    halo = 2 * depth
    total = rows + 2 * halo
    first = lax.axis_index("layer") == 0

    def put(index, own, beyond):
        x_ref[index, :, :cols] = own
        x_ref[index, :, cols:] = beyond
        a_ref[index, :, :cols] = own.astype(bf16)
        a_ref[index, :, cols:] = beyond.astype(bf16)

    edge = 2 * depth

    beside = Beside(s_pair_ref, s_cross_ref)
    own_side = s_ref[rows].astype(f32)
    above_side, below_side = beside.above(rows), beside.below(rows)
    for row in range(rows):
        own = jnp.where(first, row_of(c_ref, row, channels, rows), s_ref[row].astype(f32))
        state_ref[pl.ds(row, channels, stride=rows), :] = own
        put(halo + row, own, side_lanes(own_side, edge, 0, row))
    leaving = in_parts(state_ref, state_hbm, left_here, 0)
    for copy in leaving:
        copy.start()
    for row in range(halo):
        place = rows - halo + row
        put(
            row,
            beside.above(place),
            side_lanes(above_side, edge, 0, place),
        )
        put(
            halo + rows + row,
            beside.below(row),
            side_lanes(below_side, edge, 0, row),
        )

    def put_adj(index, own, beyond):
        adj_ref[index, :, :cols] = own
        adj_ref[index, :, cols:] = beyond

    _, (edge, low) = layout(rows, depth)
    own_side = side_ref[...].astype(f32)
    beside = Beside(pair_ref, cross_ref)
    above_side, below_side = strips_of(beside.above, depth), strips_of(beside.below, depth)
    for row in range(rows):
        put_adj(
            halo + row, row_of(q_ref, row, channels, rows), side_lanes(own_side, edge, low, row)
        )
    for row in range(depth):
        place = rows - depth + row
        put_adj(
            halo - depth + row,
            beside.above(depth + row),
            side_lanes(above_side, edge, low, place),
        )
        put_adj(
            halo + rows + row,
            beside.below(depth + row),
            side_lanes(below_side, edge, low, row),
        )

    for layer in range(depth):
        now, later = (a_ref, a2_ref) if layer % 2 == 0 else (a2_ref, a_ref)
        kept_ref[layer] = now[pl.ds(halo, rows)]

        def step(first, count, layer=layer, now=now, later=later):
            states = x_ref[pl.ds(first, count)]
            done = []
            for place, z in enumerate(convolved_rows(w_ref[layer], now, first, count)):
                gain = mask * (step_size * row_flag(first + place, halo, rows, up, down))
                t = jnp.tanh(z)
                moved = gain * t
                done.append((gain - moved * t, states[place] + moved))
            for place, (slope, x) in enumerate(done):
                slope_ref[layer, first + place] = slope
                if layer < depth - 1:
                    x_ref[first + place] = x
                    later[first + place] = x.astype(bf16)

        row_blocks(layer + 1, total - layer - 1, step)

    for layer in reversed(range(depth)):
        reach = layer + 1

        def source(first, count, layer=layer):
            part = pl.ds(first, count)
            src_ref[part] = (adj_ref[part] * slope_ref[layer, part]).astype(bf16)

        row_blocks(halo - reach, halo + rows + reach, source)

        def back(first, count, layer=layer):
            adjoints = adj_ref[pl.ds(first, count)]
            moved = convolved_rows(wt_ref[layer], src_ref, first, count)
            for place in range(count):
                adj_ref[first + place] = adjoints[place] + moved[place]

        row_blocks(halo - layer, halo + rows + layer, back)
        sent_ref[layer] = src_ref[pl.ds(halo - 1, rows + 2), :, :cols]
    for row in range(rows):
        value = adj_ref[halo + row, :, :cols]
        g_ref[row] = value
        ref, place = piece_of((g_upper_ref, g_lower_ref), row, rows)
        ref[place] = value.astype(bf16)
    for copy in leaving:
        copy.wait()


def grad_body(kept_ref, sent_ref, grad_ref, *, channels, rows, depth):
    lanes = kept_ref.shape[3]
    cols = lanes // 2
    for layer in range(depth):
        columns = []
        for row in range(rows):
            a = kept_ref[layer, row].astype(f32)
            columns.append(
                jnp.concatenate(
                    [
                        pltpu.roll(a, 1, 1)[:, :cols],
                        a[:, :cols],
                        pltpu.roll(a, lanes - 1, 1)[:, :cols],
                    ],
                    0,
                ).astype(bf16)
            )
        sources = [
            sent_ref[layer, pl.ds(row, 3)].reshape(3 * channels, cols) for row in range(rows)
        ]
        grad = lax.dot_general(
            jnp.concatenate(sources, 1),
            jnp.concatenate(columns, 1),
            (((1,), (1,)), ((), ())),
            preferred_element_type=f32,
        )
        for tap in range(3):
            grad_ref[layer, :, pl.ds(tap * 3 * channels, 3 * channels)] = grad[
                (2 - tap) * channels : (3 - tap) * channels
            ]


def last_body(q_ref, half_ref, other_ref, *refs, channels, rows):
    arrived, (out_hbm, grad_hbm, out_ref, left_here) = refs[:-4], refs[-4:]
    half = half_ref.shape[0]
    odd = jnp.logical_not(even_row()).astype(jnp.int32)
    leaving = []
    for which, ref in enumerate((half_ref, other_ref)):
        low = half * (odd if which == 0 else 1 - odd)
        for layer in range(half):
            leaving.append(
                pltpu.make_async_copy(
                    ref.at[layer], grad_hbm.at[low + layer], left_here.at[len(leaving)]
                )
            )
    for copy in leaving:
        copy.start()
    last = lax.axis_index("layer") == lax.axis_size("layer") - 1
    for row in range(rows):
        value = arrived_row(arrived, row, rows)
        value = jnp.where(last, row_of(q_ref, row, channels, rows), value)
        out_ref[pl.ds(row, channels, stride=rows), :] = value
    parts = in_parts(out_ref, out_hbm, left_here, 2 * half)
    for copy in parts:
        copy.start()
    for copy in leaving + parts:
        copy.wait()


def shifted(array, axis, by):
    count = lax.axis_size(axis)
    pairs = [(i, i + by) for i in range(count) if 0 <= i + by < count]
    return lax.ppermute(array, axis, pairs)


def exchanged(to_pair, to_cross):
    rows = lax.axis_size("row")
    pairs = [(r, r ^ 1) for r in range(rows)]
    crossing = [(r, r + 1 if r % 2 else r - 1) for r in range(1, rows - 1)]
    return lax.ppermute(to_pair, "row", pairs), lax.ppermute(to_cross, "row", crossing)


def from_sides(array):
    if lax.axis_size("col") == 2:
        other = lax.ppermute(array, "col", [(0, 1), (1, 0)])
        return other, other
    return shifted(array, "col", 1), shifted(array, "col", -1)


def total_over_tiles(grads):
    rows, cols = lax.axis_size("row"), lax.axis_size("col")
    depth = grads.shape[0]
    half = depth // 2
    odd = lax.axis_index("row") % 2 == 1
    sent = jnp.where(odd, grads[:half], grads[half:])
    own = jnp.where(odd, grads[half:], grads[:half])
    pair = [(r, r ^ 1) for r in range(rows)]
    value = own + lax.ppermute(sent, "row", pair)

    flips = [(1 << bit, 0) for bit in range(1, rows.bit_length() - 1)]
    flips += [(0, 1 << bit) for bit in range(cols.bit_length() - 1)]
    for even, uneven in zip(flips, flips[::-1]):
        pairs = []
        for r in range(rows):
            row_by, col_by = uneven if r % 2 else even
            pairs += [
                (r * cols + c, (r ^ row_by) * cols + (c ^ col_by)) for c in range(cols)
            ]
        rounded = value.astype(bf16)
        arrived = lax.ppermute(rounded, ("row", "col"), pairs)
        value = rounded.astype(f32) + arrived.astype(f32)
    return value, lax.ppermute(value, "row", pair)


def local(c_states, c_adjoints, weights):
    groups = lax.axis_size("layer")
    channels, rows, cols = c_states.shape[1:]
    depth = weights.shape[0]
    flat = (channels * rows, cols)
    c_flat, q_flat = c_states.reshape(flat), c_adjoints.reshape(flat)
    sizes = dict(channels=channels, rows=rows)
    tile_f = jax.ShapeDtypeStruct((rows, channels, cols), f32)

    strip_f = jax.ShapeDtypeStruct((channels, cols), f32)
    wide_b = jax.ShapeDtypeStruct((channels, 2 * cols), bf16)
    half = rows // 2
    more_f, more_b, upper_b, lower_b, message_b = (
        jax.ShapeDtypeStruct((count, channels, cols), kind)
        for count, kind in (
            (rows + 1, f32), (rows + 1, bf16), (half + 1, bf16), (half, bf16),
            (2 * depth + 2, bf16),
        )
    )
    flat_f = jax.ShapeDtypeStruct(flat, f32)
    edges = call(
        functools.partial(strip_body, depth=depth, **sizes),
        wide_b,
        [
            pltpu.VMEM(flat, f32),
            pltpu.VMEM(flat, f32),
            pltpu.SemaphoreType.DMA((2 * PARTS,)),
        ],
        vmem=STRIP_VMEM_BYTES,
        in_specs=[AWAY, AWAY],
        out_specs=HERE,
    )(c_flat, q_flat)
    left, right = from_sides(edges)
    to_pair, to_cross, side, strip = call(
        functools.partial(message_body, depth=depth, **sizes),
        (message_b, message_b, wide_b, strip_f),
    )(c_flat, q_flat, left, right)
    pair, cross = exchanged(to_pair, to_cross)

    taps = weights.reshape(depth, channels, 3, 3, channels)
    w_fwd = jnp.transpose(taps, (0, 3, 1, 2, 4)).reshape(depth, 3 * channels, 3 * channels)
    later_taps, _ = lax.optimization_barrier((taps, to_pair))
    w_back = jnp.transpose(later_taps[:, :, ::-1, ::-1, :], (0, 3, 4, 2, 1)).reshape(
        depth, 3 * channels, 3 * channels
    )
    w_fwd, w_back = lax.optimization_barrier((w_fwd, w_back))
    coarse = step_size * jnp.sum(weights[0].astype(f32).reshape(channels, 9, channels), axis=1)
    high = coarse.astype(bf16)
    low = (coarse - high.astype(f32)).astype(bf16)
    m_fwd = jnp.concatenate([high, low, high], 1)
    m_back = jnp.concatenate([high.T, low.T, high.T], 1)

    lanes = 2 * cols
    mac = 2 * 9 * channels * channels * lanes
    total = rows + 2 * depth

    def first(kind, sender, *inputs):
        return call(
            functools.partial(first_body, depth=depth, sender=sender, **sizes),
            kind,
            [
                pltpu.VMEM((total, channels, lanes), f32),
                pltpu.VMEM((total, channels, lanes), bf16),
                pltpu.VMEM((total, channels, lanes), bf16),
            ],
            flops=mac * 44,
        )(*inputs)

    def chain(pieces, target, matrix, order):
        sendings = [piece[0] for piece in pieces]
        arrivals = []
        for turn, step in enumerate(order):
            arrived = [lax.ppermute(sending, "layer", [step]) for sending in sendings]
            arrivals += arrived
            if turn < len(order) - 1:
                sendings = [
                    call(
                        functools.partial(hop_body, start=start, **sizes),
                        jax.ShapeDtypeStruct(value.shape, bf16),
                        flops=10**10,
                    )(value, *base, target, matrix)
                    for value, (_, start, base) in zip(arrived, pieces)
                ]
        return arrivals

    inputs = (c_flat, pair, cross, side, w_fwd)
    upper, lower = first((upper_b, lower_b), True, *inputs)
    inputs = lax.optimization_barrier((inputs, upper))[0]
    (f,) = first((more_f,), False, *inputs)
    arrivals = chain(
        ((upper, 0, (c_flat, strip)), (lower, half, (c_flat,))),
        f,
        m_fwd,
        [(k, k + 1) for k in range(groups - 1)],
    )
    s = call(functools.partial(settle_body, **sizes), more_b)(c_flat, strip, *arrivals)
    s_pair, s_cross = exchanged(s, s)

    total = rows + 4 * depth
    state, g, upper, lower, kept, sources = call(
        functools.partial(second_body, depth=depth, **sizes),
        (
            flat_f,
            tile_f,
            lower_b,
            lower_b,
            jax.ShapeDtypeStruct((depth, rows, channels, lanes), bf16),
            jax.ShapeDtypeStruct((depth, rows + 2, channels, cols), bf16),
        ),
        [
            pltpu.VMEM((total, channels, lanes), f32),
            pltpu.VMEM((total, channels, lanes), bf16),
            pltpu.VMEM((total, channels, lanes), bf16),
            pltpu.VMEM((depth, total, channels, lanes), f32),
            pltpu.VMEM((total, channels, lanes), f32),
            pltpu.VMEM((total, channels, lanes), bf16),
            pltpu.VMEM(flat, f32),
            pltpu.SemaphoreType.DMA((PARTS,)),
        ],
        flops=mac * 120,
        out_specs=(AWAY, HERE, HERE, HERE, HERE, HERE),
    )(c_flat, q_flat, s, s_pair, s_cross, pair, cross, side, w_fwd, w_back)
    returned = chain(
        ((upper, 0, (q_flat,)), (lower, half, (q_flat,))),
        g,
        m_back,
        [(k, k - 1) for k in range(groups - 1, 0, -1)],
    )
    grads = call(
        functools.partial(grad_body, depth=depth, **sizes),
        jax.ShapeDtypeStruct((depth, channels, 9 * channels), f32),
        flops=10**9,
    )(kept, sources)
    own_half, other_half = total_over_tiles(grads)
    adjoint, weight_grads = call(
        functools.partial(last_body, **sizes),
        (flat_f, jax.ShapeDtypeStruct((depth, channels, 9 * channels), f32)),
        [pltpu.VMEM(flat, f32), pltpu.SemaphoreType.DMA((depth + PARTS,))],
        flops=10**10,
        out_specs=(AWAY, AWAY),
    )(q_flat, own_half, other_half, *returned)
    return state.reshape(c_states.shape), adjoint.reshape(c_states.shape), weight_grads


def solution(mesh):
    placed = (
        P("layer", None, "row", "col"),
        P("layer", None, "row", "col"),
        P("layer", None, None),
    )
    return jax.shard_map(
        local, mesh=mesh, in_specs=placed, out_specs=placed, check_vma=False
    )
```

```python
import functools

import jax
import jax.numpy as jnp
from jax import lax
from jax.experimental import pallas as pl
from jax.experimental.pallas import tpu as pltpu
from jax.sharding import PartitionSpec as P

step_size = 0.2
VMEM_BYTES = 40 * 1024 * 1024
STRIP_VMEM_BYTES = 63 * 1024 * 1024
PARTS = 4
f32 = jnp.float32
bf16 = jnp.bfloat16
HERE = pl.BlockSpec(memory_space=pltpu.VMEM)
AWAY = pl.BlockSpec(memory_space=pltpu.HBM)


def call(body, out_shape, scratch=(), flops=0, vmem=VMEM_BYTES, **more):
    return pl.pallas_call(
        body,
        out_shape=out_shape,
        scratch_shapes=list(scratch),
        cost_estimate=pl.CostEstimate(
            flops=int(flops), bytes_accessed=0, transcendentals=0
        ),
        compiler_params=pltpu.CompilerParams(vmem_limit_bytes=vmem),
        **more,
    )


def in_parts(source, target, arrived, first):
    size = source.shape[0] // PARTS
    return [
        pltpu.make_async_copy(
            source.at[pl.ds(part * size, size)],
            target.at[pl.ds(part * size, size)],
            arrived.at[first + part],
        )
        for part in range(PARTS)
    ]


def piece_of(parts, row, rows):
    half = rows // 2
    if len(parts) == 1 or row < half:
        return parts[0], row
    return (parts[1], row - half) if row < rows else (parts[0], half)


def row_of(ref, row, channels, rows):
    return ref[pl.ds(row, channels, stride=rows), :]


def lanes_of(shape):
    return lax.broadcasted_iota(jnp.int32, shape, 1)


def slots(shape, low, width, count):
    return (lanes_of(shape) - low + width * count) // width - count


def fold_edges(rows_list, edge, low, total):
    doubled = total.shape[1] > rows_list[0].shape[1]
    cols = rows_list[0].shape[1]
    slot = slots(total.shape, low, 2 * edge, len(rows_list))
    for place, row in enumerate(rows_list):
        wide = jnp.concatenate([row, row], 1) if doubled else row
        turned = pltpu.roll(wide, (low + 2 * edge * place + edge - cols) % wide.shape[1], 1)
        total = jnp.where(slot == place, turned, total)
    return total


def join_edges(from_left, from_right, left, right, edges):
    lanes = lanes_of(from_left.shape)
    far = jnp.zeros(lanes.shape, jnp.bool_)
    for edge, low, high in edges:
        inside = (lanes >= low) & (lanes < high)
        far = far | (inside & ((lanes - low) % (2 * edge) >= edge))
    return jnp.where(far, from_right.astype(f32) * right, from_left.astype(f32) * left)


def side_lanes(joined, edge, low, place):
    lanes = joined.shape[1]
    turned = pltpu.roll(joined, (2 * lanes - (low + 2 * edge * place + edge)) % lanes, 1)
    if lanes == 128:
        return turned
    front, back = turned[:, :128], turned[:, lanes - 128 :]
    return jnp.where(lanes_of(front.shape) < 64, front, back)


def convolved(weights, slab):
    channels = slab.shape[1]
    lanes = slab.shape[2]
    product = jnp.dot(
        weights, slab.reshape(3 * channels, lanes), preferred_element_type=f32
    )
    return (
        pltpu.roll(product[:channels], 1, 1)
        + product[channels : 2 * channels]
        + pltpu.roll(product[2 * channels :], lanes - 1, 1)
    )


def flags():
    row, col = lax.axis_index("row"), lax.axis_index("col")
    up = (row > 0).astype(f32)
    down = (row < lax.axis_size("row") - 1).astype(f32)
    left = (col > 0).astype(f32)
    right = (col < lax.axis_size("col") - 1).astype(f32)
    return up, down, left, right


def even_row():
    return lax.axis_index("row") % 2 == 0


def lane_mask(cols, left, right):
    lanes = lax.broadcasted_iota(jnp.int32, (1, 2 * cols), 1)
    return jnp.where(lanes < cols, 1.0, jnp.where(lanes < cols + cols // 2, right, left))


def layout(rows, depth):
    state_edge, adjoint_edge = 3 * depth, depth
    return (state_edge, 0), (adjoint_edge, 2 * state_edge * rows)


def strip_body(c_hbm, q_hbm, edge_ref, c_ref, q_ref, arrived, *, channels, rows, depth):
    copies = in_parts(c_hbm, c_ref, arrived, 0) + in_parts(q_hbm, q_ref, arrived, PARTS)
    for copy in copies:
        copy.start()
    for copy in copies:
        copy.wait()
    total = jnp.zeros(edge_ref.shape, f32)
    for ref, (edge, low) in zip((c_ref, q_ref), layout(rows, depth)):
        image = [row_of(ref, row, channels, rows) for row in range(rows)]
        total = fold_edges(image, edge, low, total)
    edge_ref[...] = total.astype(bf16)


def message_body(
    c_ref, q_ref, left_ref, right_ref, pair_ref, cross_ref, side_ref, strip_ref,
    *, channels, rows, depth,
):
    cols = c_ref.shape[1]
    _, _, left, right = flags()
    (c_edge, _), (q_edge, middle) = layout(rows, depth)
    edges = ((c_edge, 0, middle), (q_edge, middle, 2 * cols))
    side = join_edges(left_ref[...], right_ref[...], left, right, edges).astype(bf16)
    side_ref[...] = side
    wide = side.astype(f32)
    image = [side_lanes(wide, c_edge, 0, row) for row in range(rows)]
    strip_ref[...] = fold_edges(image, 2 * depth, 0, jnp.zeros(strip_ref.shape, f32))
    even = even_row()
    for which, ref in enumerate((c_ref, q_ref)):
        for row in range(depth):
            place = which * depth + row
            top = row_of(ref, row, channels, rows)
            bottom = row_of(ref, rows - depth + row, channels, rows)
            pair_ref[place] = jnp.where(even, bottom, top).astype(bf16)
            cross_ref[place] = jnp.where(even, top, bottom).astype(bf16)
    for half in range(2):
        part = side[:, half * cols : (half + 1) * cols]
        pair_ref[2 * depth + half] = part
        cross_ref[2 * depth + half] = part


class Beside:
    def __init__(self, pair_ref, cross_ref):
        self.pair, self.cross, self.even = pair_ref, cross_ref, even_row()

    def above(self, place):
        return jnp.where(
            self.even, self.cross[place].astype(f32), self.pair[place].astype(f32)
        )

    def below(self, place):
        return jnp.where(
            self.even, self.pair[place].astype(f32), self.cross[place].astype(f32)
        )


def strips_of(get, depth):
    return jnp.concatenate([get(2 * depth), get(2 * depth + 1)], 1)


def row_blocks(low, high, body):
    body(low, high - low)


def convolved_rows(weights, ref, first, count):
    slab = ref[pl.ds(first - 1, count + 2)]
    return [convolved(weights, slab[place : place + 3]) for place in range(count)]


def row_flag(index, halo, rows, up, down):
    if index < halo:
        return up
    return down if index >= halo + rows else 1.0


def first_body(
    c_ref, pair_ref, cross_ref, side_ref, w_ref, *refs, channels, rows, depth, sender
):
    outs = refs[:-3]
    active = (lax.axis_index("layer") == 0) == sender

    @pl.when(jnp.logical_not(active))
    def nothing():
        for out_ref in outs:
            out_ref[...] = jnp.zeros(out_ref.shape, out_ref.dtype)

    @pl.when(active)
    def run():
        first_pass(
            c_ref, pair_ref, cross_ref, side_ref, w_ref, outs, *refs[-3:],
            channels, rows, depth,
        )


def first_pass(
    c_ref, pair_ref, cross_ref, side_ref, w_ref, outs, x_ref, a_ref, a2_ref,
    channels, rows, depth,
):
    cols = c_ref.shape[1]
    up, down, left, right = flags()
    mask = lane_mask(cols, left, right)
    halo = depth

    def put(index, own, beyond):
        x_ref[index, :, :cols] = own
        x_ref[index, :, cols:] = beyond
        a_ref[index, :, :cols] = own.astype(bf16)
        a_ref[index, :, cols:] = beyond.astype(bf16)

    (edge, low), _ = layout(rows, depth)
    own_side = side_ref[...].astype(f32)
    for row in range(rows):
        own = row_of(c_ref, row, channels, rows)
        put(halo + row, own, side_lanes(own_side, edge, low, row))
    beside = Beside(pair_ref, cross_ref)
    above_side, below_side = strips_of(beside.above, depth), strips_of(beside.below, depth)
    for row in range(depth):
        place = rows - depth + row
        put(row, beside.above(row), side_lanes(above_side, edge, low, place))
        put(halo + rows + row, beside.below(row), side_lanes(below_side, edge, low, row))

    total = rows + 2 * halo
    for layer in range(depth):
        now, later = (a_ref, a2_ref) if layer % 2 == 0 else (a2_ref, a_ref)

        def step(first, count, layer=layer, now=now, later=later):
            states = x_ref[pl.ds(first, count)]
            done = []
            for place, z in enumerate(convolved_rows(w_ref[layer], now, first, count)):
                gain = mask * (step_size * row_flag(first + place, halo, rows, up, down))
                done.append(states[place] + gain * jnp.tanh(z))
            for place, x in enumerate(done):
                x_ref[first + place] = x
                if layer < depth - 1:
                    later[first + place] = x.astype(bf16)

        row_blocks(layer + 1, total - layer - 1, step)
    image = [x_ref[halo + row, :, cols:] for row in range(rows)]
    values = [x_ref[halo + row, :, :cols] for row in range(rows)]
    values.append(fold_edges(image, 2 * depth, 0, jnp.zeros((channels, cols), f32)))
    for row, value in enumerate(values):
        out_ref, place = piece_of(outs, row, rows)
        out_ref[place] = value.astype(out_ref.dtype)


def hop_body(s_ref, c_ref, *refs, start, channels, rows):
    f_ref, m_ref, out_ref = refs[-3:]
    work = [
        (row, row_of(c_ref, row, channels, rows)) for row in range(start, start + rows // 2)
    ]
    work += [(rows, ref[...]) for ref in refs[:-3]]
    for place, (row, base) in enumerate(work):
        e = s_ref[place].astype(f32) - base
        high = e.astype(bf16)
        low = (e - high.astype(f32)).astype(bf16)
        stacked = jnp.concatenate([high, high, low], 0)
        moved = jnp.dot(m_ref[...], stacked, preferred_element_type=f32)
        out_ref[place] = (f_ref[row] + e + moved).astype(bf16)


def arrived_row(refs, row, rows):
    value = 0.0
    for pieces in zip(refs[::2], refs[1::2]):
        ref, place = piece_of(pieces, row, rows)
        value = value + ref[place].astype(f32)
    return value


def settle_body(c_ref, strip_ref, *refs, channels, rows):
    arrived, s_ref = refs[:-1], refs[-1]
    first = lax.axis_index("layer") == 0
    base = [row_of(c_ref, row, channels, rows) for row in range(rows)] + [strip_ref[...]]
    for row in range(rows + 1):
        value = arrived_row(arrived, row, rows)
        s_ref[row] = jnp.where(first, base[row], value).astype(bf16)


def second_body(
    c_ref, q_ref, s_ref, s_pair_ref, s_cross_ref, pair_ref, cross_ref, side_ref, w_ref, wt_ref,
    state_hbm, g_ref, g_upper_ref, g_lower_ref, kept_ref, sent_ref,
    x_ref, a_ref, a2_ref, slope_ref, adj_ref, src_ref, state_ref, left_here,
    *, channels, rows, depth,
):
    cols = c_ref.shape[1]
    up, down, left, right = flags()
    mask = lane_mask(cols, left, right)
    halo = 2 * depth
    total = rows + 2 * halo
    first = lax.axis_index("layer") == 0

    def put(index, own, beyond):
        x_ref[index, :, :cols] = own
        x_ref[index, :, cols:] = beyond
        a_ref[index, :, :cols] = own.astype(bf16)
        a_ref[index, :, cols:] = beyond.astype(bf16)

    edge = 2 * depth

    beside = Beside(s_pair_ref, s_cross_ref)
    own_side = s_ref[rows].astype(f32)
    above_side, below_side = beside.above(rows), beside.below(rows)
    for row in range(rows):
        own = jnp.where(first, row_of(c_ref, row, channels, rows), s_ref[row].astype(f32))
        state_ref[pl.ds(row, channels, stride=rows), :] = own
        put(halo + row, own, side_lanes(own_side, edge, 0, row))
    leaving = in_parts(state_ref, state_hbm, left_here, 0)
    for copy in leaving:
        copy.start()
    for row in range(halo):
        place = rows - halo + row
        put(
            row,
            beside.above(place),
            side_lanes(above_side, edge, 0, place),
        )
        put(
            halo + rows + row,
            beside.below(row),
            side_lanes(below_side, edge, 0, row),
        )

    def put_adj(index, own, beyond):
        adj_ref[index, :, :cols] = own
        adj_ref[index, :, cols:] = beyond

    _, (edge, low) = layout(rows, depth)
    own_side = side_ref[...].astype(f32)
    beside = Beside(pair_ref, cross_ref)
    above_side, below_side = strips_of(beside.above, depth), strips_of(beside.below, depth)
    for row in range(rows):
        put_adj(
            halo + row, row_of(q_ref, row, channels, rows), side_lanes(own_side, edge, low, row)
        )
    for row in range(depth):
        place = rows - depth + row
        put_adj(
            halo - depth + row,
            beside.above(depth + row),
            side_lanes(above_side, edge, low, place),
        )
        put_adj(
            halo + rows + row,
            beside.below(depth + row),
            side_lanes(below_side, edge, low, row),
        )

    for layer in range(depth):
        now, later = (a_ref, a2_ref) if layer % 2 == 0 else (a2_ref, a_ref)
        kept_ref[layer] = now[pl.ds(halo, rows)]

        def step(first, count, layer=layer, now=now, later=later):
            states = x_ref[pl.ds(first, count)]
            done = []
            for place, z in enumerate(convolved_rows(w_ref[layer], now, first, count)):
                gain = mask * (step_size * row_flag(first + place, halo, rows, up, down))
                t = jnp.tanh(z)
                moved = gain * t
                done.append((gain - moved * t, states[place] + moved))
            for place, (slope, x) in enumerate(done):
                slope_ref[layer, first + place] = slope
                if layer < depth - 1:
                    x_ref[first + place] = x
                    later[first + place] = x.astype(bf16)

        row_blocks(layer + 1, total - layer - 1, step)

    for layer in reversed(range(depth)):
        reach = layer + 1

        def source(first, count, layer=layer):
            part = pl.ds(first, count)
            src_ref[part] = (adj_ref[part] * slope_ref[layer, part]).astype(bf16)

        row_blocks(halo - reach, halo + rows + reach, source)

        def back(first, count, layer=layer):
            adjoints = adj_ref[pl.ds(first, count)]
            moved = convolved_rows(wt_ref[layer], src_ref, first, count)
            for place in range(count):
                adj_ref[first + place] = adjoints[place] + moved[place]

        row_blocks(halo - layer, halo + rows + layer, back)
        sent_ref[layer] = src_ref[pl.ds(halo - 1, rows + 2), :, :cols]
    for row in range(rows):
        value = adj_ref[halo + row, :, :cols]
        g_ref[row] = value
        ref, place = piece_of((g_upper_ref, g_lower_ref), row, rows)
        ref[place] = value.astype(bf16)
    for copy in leaving:
        copy.wait()


def grad_body(kept_ref, sent_ref, grad_ref, *, channels, rows, depth):
    lanes = kept_ref.shape[3]
    cols = lanes // 2
    for layer in range(depth):
        columns = []
        for row in range(rows):
            a = kept_ref[layer, row].astype(f32)
            columns.append(
                jnp.concatenate(
                    [
                        pltpu.roll(a, 1, 1)[:, :cols],
                        a[:, :cols],
                        pltpu.roll(a, lanes - 1, 1)[:, :cols],
                    ],
                    0,
                ).astype(bf16)
            )
        sources = [
            sent_ref[layer, pl.ds(row, 3)].reshape(3 * channels, cols) for row in range(rows)
        ]
        grad = lax.dot_general(
            jnp.concatenate(sources, 1),
            jnp.concatenate(columns, 1),
            (((1,), (1,)), ((), ())),
            preferred_element_type=f32,
        )
        for tap in range(3):
            grad_ref[layer, :, pl.ds(tap * 3 * channels, 3 * channels)] = grad[
                (2 - tap) * channels : (3 - tap) * channels
            ]


def last_body(q_ref, half_ref, other_ref, *refs, channels, rows):
    arrived, (out_hbm, grad_hbm, out_ref, left_here) = refs[:-4], refs[-4:]
    half = half_ref.shape[0]
    odd = jnp.logical_not(even_row()).astype(jnp.int32)
    leaving = []
    for which, ref in enumerate((half_ref, other_ref)):
        low = half * (odd if which == 0 else 1 - odd)
        for layer in range(half):
            leaving.append(
                pltpu.make_async_copy(
                    ref.at[layer], grad_hbm.at[low + layer], left_here.at[len(leaving)]
                )
            )
    for copy in leaving:
        copy.start()
    last = lax.axis_index("layer") == lax.axis_size("layer") - 1
    for row in range(rows):
        value = arrived_row(arrived, row, rows)
        value = jnp.where(last, row_of(q_ref, row, channels, rows), value)
        out_ref[pl.ds(row, channels, stride=rows), :] = value
    parts = in_parts(out_ref, out_hbm, left_here, 2 * half)
    for copy in parts:
        copy.start()
    for copy in leaving + parts:
        copy.wait()


def shifted(array, axis, by):
    count = lax.axis_size(axis)
    pairs = [(i, i + by) for i in range(count) if 0 <= i + by < count]
    return lax.ppermute(array, axis, pairs)


def exchanged(to_pair, to_cross):
    rows = lax.axis_size("row")
    pairs = [(r, r ^ 1) for r in range(rows)]
    crossing = [(r, r + 1 if r % 2 else r - 1) for r in range(1, rows - 1)]
    return lax.ppermute(to_pair, "row", pairs), lax.ppermute(to_cross, "row", crossing)


def from_sides(array):
    if lax.axis_size("col") == 2:
        other = lax.ppermute(array, "col", [(0, 1), (1, 0)])
        return other, other
    return shifted(array, "col", 1), shifted(array, "col", -1)


def total_over_tiles(grads):
    rows, cols = lax.axis_size("row"), lax.axis_size("col")
    depth = grads.shape[0]
    half = depth // 2
    odd = lax.axis_index("row") % 2 == 1
    sent = jnp.where(odd, grads[:half], grads[half:])
    own = jnp.where(odd, grads[half:], grads[:half])
    pair = [(r, r ^ 1) for r in range(rows)]
    value = own + lax.ppermute(sent, "row", pair)

    flips = [(1 << bit, 0) for bit in range(1, rows.bit_length() - 1)]
    flips += [(0, 1 << bit) for bit in range(cols.bit_length() - 1)]
    for even, uneven in zip(flips[::-1], flips):
        pairs = []
        for r in range(rows):
            row_by, col_by = uneven if r % 2 else even
            pairs += [
                (r * cols + c, (r ^ row_by) * cols + (c ^ col_by)) for c in range(cols)
            ]
        rounded = value.astype(bf16)
        arrived = lax.ppermute(rounded, ("row", "col"), pairs)
        value = rounded.astype(f32) + arrived.astype(f32)
    return value, lax.ppermute(value, "row", pair)


def local(c_states, c_adjoints, weights):
    groups = lax.axis_size("layer")
    channels, rows, cols = c_states.shape[1:]
    depth = weights.shape[0]
    flat = (channels * rows, cols)
    c_flat, q_flat = c_states.reshape(flat), c_adjoints.reshape(flat)
    sizes = dict(channels=channels, rows=rows)
    tile_f = jax.ShapeDtypeStruct((rows, channels, cols), f32)

    strip_f = jax.ShapeDtypeStruct((channels, cols), f32)
    wide_b = jax.ShapeDtypeStruct((channels, 2 * cols), bf16)
    half = rows // 2
    more_f, more_b, upper_b, lower_b, message_b = (
        jax.ShapeDtypeStruct((count, channels, cols), kind)
        for count, kind in (
            (rows + 1, f32), (rows + 1, bf16), (half + 1, bf16), (half, bf16),
            (2 * depth + 2, bf16),
        )
    )
    flat_f = jax.ShapeDtypeStruct(flat, f32)
    edges = call(
        functools.partial(strip_body, depth=depth, **sizes),
        wide_b,
        [
            pltpu.VMEM(flat, f32),
            pltpu.VMEM(flat, f32),
            pltpu.SemaphoreType.DMA((2 * PARTS,)),
        ],
        vmem=STRIP_VMEM_BYTES,
        in_specs=[AWAY, AWAY],
        out_specs=HERE,
    )(c_flat, q_flat)
    left, right = from_sides(edges)
    to_pair, to_cross, side, strip = call(
        functools.partial(message_body, depth=depth, **sizes),
        (message_b, message_b, wide_b, strip_f),
    )(c_flat, q_flat, left, right)
    pair, cross = exchanged(to_pair, to_cross)

    taps = weights.reshape(depth, channels, 3, 3, channels)
    w_fwd = jnp.transpose(taps, (0, 3, 1, 2, 4)).reshape(depth, 3 * channels, 3 * channels)
    later_taps, _ = lax.optimization_barrier((taps, to_pair))
    w_back = jnp.transpose(later_taps[:, :, ::-1, ::-1, :], (0, 3, 4, 2, 1)).reshape(
        depth, 3 * channels, 3 * channels
    )
    w_fwd, w_back = lax.optimization_barrier((w_fwd, w_back))
    coarse = step_size * jnp.sum(weights[0].astype(f32).reshape(channels, 9, channels), axis=1)
    high = coarse.astype(bf16)
    low = (coarse - high.astype(f32)).astype(bf16)
    m_fwd = jnp.concatenate([high, low, high], 1)
    m_back = jnp.concatenate([high.T, low.T, high.T], 1)

    lanes = 2 * cols
    mac = 2 * 9 * channels * channels * lanes
    total = rows + 2 * depth

    def first(kind, sender, *inputs):
        return call(
            functools.partial(first_body, depth=depth, sender=sender, **sizes),
            kind,
            [
                pltpu.VMEM((total, channels, lanes), f32),
                pltpu.VMEM((total, channels, lanes), bf16),
                pltpu.VMEM((total, channels, lanes), bf16),
            ],
            flops=mac * 44,
        )(*inputs)

    def chain(pieces, target, matrix, order):
        sendings = [piece[0] for piece in pieces]
        arrivals = []
        for turn, step in enumerate(order):
            arrived = [lax.ppermute(sending, "layer", [step]) for sending in sendings]
            arrivals += arrived
            if turn < len(order) - 1:
                sendings = [
                    call(
                        functools.partial(hop_body, start=start, **sizes),
                        jax.ShapeDtypeStruct(value.shape, bf16),
                        flops=10**10,
                    )(value, *base, target, matrix)
                    for value, (_, start, base) in zip(arrived, pieces)
                ]
        return arrivals

    inputs = (c_flat, pair, cross, side, w_fwd)
    upper, lower = first((upper_b, lower_b), True, *inputs)
    inputs = lax.optimization_barrier((inputs, upper))[0]
    (f,) = first((more_f,), False, *inputs)
    arrivals = chain(
        ((upper, 0, (c_flat, strip)), (lower, half, (c_flat,))),
        f,
        m_fwd,
        [(k, k + 1) for k in range(groups - 1)],
    )
    s = call(functools.partial(settle_body, **sizes), more_b)(c_flat, strip, *arrivals)
    s_pair, s_cross = exchanged(s, s)

    total = rows + 4 * depth
    state, g, upper, lower, kept, sources = call(
        functools.partial(second_body, depth=depth, **sizes),
        (
            flat_f,
            tile_f,
            lower_b,
            lower_b,
            jax.ShapeDtypeStruct((depth, rows, channels, lanes), bf16),
            jax.ShapeDtypeStruct((depth, rows + 2, channels, cols), bf16),
        ),
        [
            pltpu.VMEM((total, channels, lanes), f32),
            pltpu.VMEM((total, channels, lanes), bf16),
            pltpu.VMEM((total, channels, lanes), bf16),
            pltpu.VMEM((depth, total, channels, lanes), f32),
            pltpu.VMEM((total, channels, lanes), f32),
            pltpu.VMEM((total, channels, lanes), bf16),
            pltpu.VMEM(flat, f32),
            pltpu.SemaphoreType.DMA((PARTS,)),
        ],
        flops=mac * 120,
        out_specs=(AWAY, HERE, HERE, HERE, HERE, HERE),
    )(c_flat, q_flat, s, s_pair, s_cross, pair, cross, side, w_fwd, w_back)
    returned = chain(
        ((upper, 0, (q_flat,)), (lower, half, (q_flat,))),
        g,
        m_back,
        [(k, k - 1) for k in range(groups - 1, 0, -1)],
    )
    grads = call(
        functools.partial(grad_body, depth=depth, **sizes),
        jax.ShapeDtypeStruct((depth, channels, 9 * channels), f32),
        flops=10**9,
    )(kept, sources)
    own_half, other_half = total_over_tiles(grads)
    adjoint, weight_grads = call(
        functools.partial(last_body, **sizes),
        (flat_f, jax.ShapeDtypeStruct((depth, channels, 9 * channels), f32)),
        [pltpu.VMEM(flat, f32), pltpu.SemaphoreType.DMA((depth + PARTS,))],
        flops=10**10,
        out_specs=(AWAY, AWAY),
    )(q_flat, own_half, other_half, *returned)
    return state.reshape(c_states.shape), adjoint.reshape(c_states.shape), weight_grads


def solution(mesh):
    placed = (
        P("layer", None, "row", "col"),
        P("layer", None, "row", "col"),
        P("layer", None, None),
    )
    return jax.shard_map(
        local, mesh=mesh, in_specs=placed, out_specs=placed, check_vma=False
    )
```

```python
import functools

import jax
import jax.numpy as jnp
from jax import lax
from jax.experimental import pallas as pl
from jax.experimental.pallas import tpu as pltpu
from jax.sharding import PartitionSpec as P

step_size = 0.2
VMEM_BYTES = 40 * 1024 * 1024
STRIP_VMEM_BYTES = 63 * 1024 * 1024
PARTS = 4
f32 = jnp.float32
bf16 = jnp.bfloat16
HERE = pl.BlockSpec(memory_space=pltpu.VMEM)
AWAY = pl.BlockSpec(memory_space=pltpu.HBM)


def call(body, out_shape, scratch=(), flops=0, vmem=VMEM_BYTES, **more):
    return pl.pallas_call(
        body,
        out_shape=out_shape,
        scratch_shapes=list(scratch),
        cost_estimate=pl.CostEstimate(
            flops=int(flops), bytes_accessed=0, transcendentals=0
        ),
        compiler_params=pltpu.CompilerParams(vmem_limit_bytes=vmem),
        **more,
    )


def in_parts(source, target, arrived, first):
    size = source.shape[0] // PARTS
    return [
        pltpu.make_async_copy(
            source.at[pl.ds(part * size, size)],
            target.at[pl.ds(part * size, size)],
            arrived.at[first + part],
        )
        for part in range(PARTS)
    ]


def piece_of(parts, row, rows):
    half = rows // 2
    if len(parts) == 1 or row < half:
        return parts[0], row
    return (parts[1], row - half) if row < rows else (parts[0], half)


def row_of(ref, row, channels, rows):
    return ref[pl.ds(row, channels, stride=rows), :]


def lanes_of(shape):
    return lax.broadcasted_iota(jnp.int32, shape, 1)


def slots(shape, low, width, count):
    return (lanes_of(shape) - low + width * count) // width - count


def fold_edges(rows_list, edge, low, total):
    doubled = total.shape[1] > rows_list[0].shape[1]
    cols = rows_list[0].shape[1]
    slot = slots(total.shape, low, 2 * edge, len(rows_list))
    for place, row in enumerate(rows_list):
        wide = jnp.concatenate([row, row], 1) if doubled else row
        turned = pltpu.roll(wide, (low + 2 * edge * place + edge - cols) % wide.shape[1], 1)
        total = jnp.where(slot == place, turned, total)
    return total


def join_edges(from_left, from_right, left, right, edges):
    lanes = lanes_of(from_left.shape)
    far = jnp.zeros(lanes.shape, jnp.bool_)
    for edge, low, high in edges:
        inside = (lanes >= low) & (lanes < high)
        far = far | (inside & ((lanes - low) % (2 * edge) >= edge))
    return jnp.where(far, from_right.astype(f32) * right, from_left.astype(f32) * left)


def side_lanes(joined, edge, low, place):
    lanes = joined.shape[1]
    turned = pltpu.roll(joined, (2 * lanes - (low + 2 * edge * place + edge)) % lanes, 1)
    if lanes == 128:
        return turned
    front, back = turned[:, :128], turned[:, lanes - 128 :]
    return jnp.where(lanes_of(front.shape) < 64, front, back)


def convolved(weights, slab):
    channels = slab.shape[1]
    lanes = slab.shape[2]
    product = jnp.dot(
        weights, slab.reshape(3 * channels, lanes), preferred_element_type=f32
    )
    return (
        pltpu.roll(product[:channels], 1, 1)
        + product[channels : 2 * channels]
        + pltpu.roll(product[2 * channels :], lanes - 1, 1)
    )


def flags():
    row, col = lax.axis_index("row"), lax.axis_index("col")
    up = (row > 0).astype(f32)
    down = (row < lax.axis_size("row") - 1).astype(f32)
    left = (col > 0).astype(f32)
    right = (col < lax.axis_size("col") - 1).astype(f32)
    return up, down, left, right


def even_row():
    return lax.axis_index("row") % 2 == 0


def lane_mask(cols, left, right):
    lanes = lax.broadcasted_iota(jnp.int32, (1, 2 * cols), 1)
    return jnp.where(lanes < cols, 1.0, jnp.where(lanes < cols + cols // 2, right, left))


def layout(rows, depth):
    state_edge, adjoint_edge = 3 * depth, depth
    return (state_edge, 0), (adjoint_edge, 2 * state_edge * rows)


def strip_body(c_hbm, q_hbm, edge_ref, c_ref, q_ref, arrived, *, channels, rows, depth):
    copies = in_parts(c_hbm, c_ref, arrived, 0) + in_parts(q_hbm, q_ref, arrived, PARTS)
    for copy in copies:
        copy.start()
    for copy in copies:
        copy.wait()
    total = jnp.zeros(edge_ref.shape, f32)
    for ref, (edge, low) in zip((c_ref, q_ref), layout(rows, depth)):
        image = [row_of(ref, row, channels, rows) for row in range(rows)]
        total = fold_edges(image, edge, low, total)
    edge_ref[...] = total.astype(bf16)


def message_body(
    c_ref, q_ref, left_ref, right_ref, pair_ref, cross_ref, side_ref, *, channels, rows, depth
):
    cols = c_ref.shape[1]
    _, _, left, right = flags()
    (c_edge, _), (q_edge, middle) = layout(rows, depth)
    edges = ((c_edge, 0, middle), (q_edge, middle, 2 * cols))
    side = join_edges(left_ref[...], right_ref[...], left, right, edges).astype(bf16)
    side_ref[...] = side
    even = even_row()
    for which, ref in enumerate((c_ref, q_ref)):
        for row in range(depth):
            place = which * depth + row
            top = row_of(ref, row, channels, rows)
            bottom = row_of(ref, rows - depth + row, channels, rows)
            pair_ref[place] = jnp.where(even, bottom, top).astype(bf16)
            cross_ref[place] = jnp.where(even, top, bottom).astype(bf16)
    for half in range(2):
        part = side[:, half * cols : (half + 1) * cols]
        pair_ref[2 * depth + half] = part
        cross_ref[2 * depth + half] = part


class Beside:
    def __init__(self, pair_ref, cross_ref):
        self.pair, self.cross, self.even = pair_ref, cross_ref, even_row()

    def above(self, place):
        return jnp.where(
            self.even, self.cross[place].astype(f32), self.pair[place].astype(f32)
        )

    def below(self, place):
        return jnp.where(
            self.even, self.pair[place].astype(f32), self.cross[place].astype(f32)
        )


def halo_strip_body(side_ref, strip_ref, *, rows, depth):
    (edge, low), _ = layout(rows, depth)
    side = side_ref[...].astype(f32)
    image = [side_lanes(side, edge, low, row) for row in range(rows)]
    strip_ref[...] = fold_edges(image, 2 * depth, 0, jnp.zeros(strip_ref.shape, f32))


def strips_of(get, depth):
    return jnp.concatenate([get(2 * depth), get(2 * depth + 1)], 1)


def row_blocks(low, high, body):
    body(low, high - low)


def convolved_rows(weights, ref, first, count):
    slab = ref[pl.ds(first - 1, count + 2)]
    return [convolved(weights, slab[place : place + 3]) for place in range(count)]


def row_flag(index, halo, rows, up, down):
    if index < halo:
        return up
    return down if index >= halo + rows else 1.0


def first_body(
    c_ref, pair_ref, cross_ref, side_ref, w_ref, *refs, channels, rows, depth, sender
):
    outs = refs[:-3]
    active = (lax.axis_index("layer") == 0) == sender

    @pl.when(jnp.logical_not(active))
    def nothing():
        for out_ref in outs:
            out_ref[...] = jnp.zeros(out_ref.shape, out_ref.dtype)

    @pl.when(active)
    def run():
        first_pass(
            c_ref, pair_ref, cross_ref, side_ref, w_ref, outs, *refs[-3:],
            channels, rows, depth,
        )


def first_pass(
    c_ref, pair_ref, cross_ref, side_ref, w_ref, outs, x_ref, a_ref, a2_ref,
    channels, rows, depth,
):
    cols = c_ref.shape[1]
    up, down, left, right = flags()
    mask = lane_mask(cols, left, right)
    halo = depth

    def put(index, own, beyond):
        x_ref[index, :, :cols] = own
        x_ref[index, :, cols:] = beyond
        a_ref[index, :, :cols] = own.astype(bf16)
        a_ref[index, :, cols:] = beyond.astype(bf16)

    (edge, low), _ = layout(rows, depth)
    own_side = side_ref[...].astype(f32)
    for row in range(rows):
        own = row_of(c_ref, row, channels, rows)
        put(halo + row, own, side_lanes(own_side, edge, low, row))
    beside = Beside(pair_ref, cross_ref)
    above_side, below_side = strips_of(beside.above, depth), strips_of(beside.below, depth)
    for row in range(depth):
        place = rows - depth + row
        put(row, beside.above(row), side_lanes(above_side, edge, low, place))
        put(halo + rows + row, beside.below(row), side_lanes(below_side, edge, low, row))

    total = rows + 2 * halo
    for layer in range(depth):
        now, later = (a_ref, a2_ref) if layer % 2 == 0 else (a2_ref, a_ref)

        def step(first, count, layer=layer, now=now, later=later):
            states = x_ref[pl.ds(first, count)]
            done = []
            for place, z in enumerate(convolved_rows(w_ref[layer], now, first, count)):
                gain = mask * (step_size * row_flag(first + place, halo, rows, up, down))
                done.append(states[place] + gain * jnp.tanh(z))
            for place, x in enumerate(done):
                x_ref[first + place] = x
                if layer < depth - 1:
                    later[first + place] = x.astype(bf16)

        row_blocks(layer + 1, total - layer - 1, step)
    image = [x_ref[halo + row, :, cols:] for row in range(rows)]
    values = [x_ref[halo + row, :, :cols] for row in range(rows)]
    values.append(fold_edges(image, 2 * depth, 0, jnp.zeros((channels, cols), f32)))
    for row, value in enumerate(values):
        out_ref, place = piece_of(outs, row, rows)
        out_ref[place] = value.astype(out_ref.dtype)


def hop_body(s_ref, c_ref, *refs, start, channels, rows):
    f_ref, m_ref, out_ref = refs[-3:]
    work = [
        (row, row_of(c_ref, row, channels, rows)) for row in range(start, start + rows // 2)
    ]
    work += [(rows, ref[...]) for ref in refs[:-3]]
    for place, (row, base) in enumerate(work):
        e = s_ref[place].astype(f32) - base
        high = e.astype(bf16)
        low = (e - high.astype(f32)).astype(bf16)
        stacked = jnp.concatenate([high, high, low], 0)
        moved = jnp.dot(m_ref[...], stacked, preferred_element_type=f32)
        out_ref[place] = (f_ref[row] + e + moved).astype(bf16)


def arrived_row(refs, row, rows):
    value = 0.0
    for pieces in zip(refs[::2], refs[1::2]):
        ref, place = piece_of(pieces, row, rows)
        value = value + ref[place].astype(f32)
    return value


def settle_body(c_ref, strip_ref, *refs, channels, rows):
    arrived, s_ref = refs[:-1], refs[-1]
    first = lax.axis_index("layer") == 0
    base = [row_of(c_ref, row, channels, rows) for row in range(rows)] + [strip_ref[...]]
    for row in range(rows + 1):
        value = arrived_row(arrived, row, rows)
        s_ref[row] = jnp.where(first, base[row], value).astype(bf16)


def prepare_body(
    c_ref, q_ref, s_ref, pair_ref, cross_ref, side_ref, state_hbm, adj_ref,
    state_ref, left_here, *, channels, rows, depth,
):
    cols = c_ref.shape[1]
    first = lax.axis_index("layer") == 0
    for row in range(rows):
        own = jnp.where(first, row_of(c_ref, row, channels, rows), s_ref[row].astype(f32))
        state_ref[pl.ds(row, channels, stride=rows), :] = own
    leaving = in_parts(state_ref, state_hbm, left_here, 0)
    for copy in leaving:
        copy.start()

    def put_adj(index, own, beyond):
        adj_ref[index, :, :cols] = own
        adj_ref[index, :, cols:] = beyond

    _, (edge, low) = layout(rows, depth)
    own_side = side_ref[...].astype(f32)
    beside = Beside(pair_ref, cross_ref)
    above_side, below_side = strips_of(beside.above, depth), strips_of(beside.below, depth)
    for row in range(rows):
        put_adj(
            depth + row, row_of(q_ref, row, channels, rows), side_lanes(own_side, edge, low, row)
        )
    for row in range(depth):
        place = rows - depth + row
        put_adj(
            row,
            beside.above(depth + row),
            side_lanes(above_side, edge, low, place),
        )
        put_adj(
            depth + rows + row,
            beside.below(depth + row),
            side_lanes(below_side, edge, low, row),
        )
    for copy in leaving:
        copy.wait()


def second_body(
    c_ref, s_ref, s_pair_ref, s_cross_ref, ready_ref, w_ref, wt_ref,
    g_ref, g_upper_ref, g_lower_ref, kept_ref, sent_ref,
    x_ref, a_ref, a2_ref, slope_ref, adj_ref, src_ref,
    *, channels, rows, depth,
):
    cols = c_ref.shape[1]
    up, down, left, right = flags()
    mask = lane_mask(cols, left, right)
    halo = 2 * depth
    total = rows + 2 * halo
    first = lax.axis_index("layer") == 0

    def put(index, own, beyond):
        x_ref[index, :, :cols] = own
        x_ref[index, :, cols:] = beyond
        a_ref[index, :, :cols] = own.astype(bf16)
        a_ref[index, :, cols:] = beyond.astype(bf16)

    edge = 2 * depth

    beside = Beside(s_pair_ref, s_cross_ref)
    own_side = s_ref[rows].astype(f32)
    above_side, below_side = beside.above(rows), beside.below(rows)
    for row in range(rows):
        own = jnp.where(first, row_of(c_ref, row, channels, rows), s_ref[row].astype(f32))
        put(halo + row, own, side_lanes(own_side, edge, 0, row))
    for row in range(halo):
        place = rows - halo + row
        put(
            row,
            beside.above(place),
            side_lanes(above_side, edge, 0, place),
        )
        put(
            halo + rows + row,
            beside.below(row),
            side_lanes(below_side, edge, 0, row),
        )

    for layer in range(depth):
        now, later = (a_ref, a2_ref) if layer % 2 == 0 else (a2_ref, a_ref)
        kept_ref[layer] = now[pl.ds(halo, rows)]

        def step(first, count, layer=layer, now=now, later=later):
            states = x_ref[pl.ds(first, count)]
            done = []
            for place, z in enumerate(convolved_rows(w_ref[layer], now, first, count)):
                gain = mask * (step_size * row_flag(first + place, halo, rows, up, down))
                t = jnp.tanh(z)
                moved = gain * t
                done.append((gain - moved * t, states[place] + moved))
            for place, (slope, x) in enumerate(done):
                slope_ref[layer, first + place] = slope
                if layer < depth - 1:
                    x_ref[first + place] = x
                    later[first + place] = x.astype(bf16)

        row_blocks(layer + 1, total - layer - 1, step)

    def before(layer, first, count):
        if layer == depth - 1:
            return ready_ref[pl.ds(first - (halo - depth), count)]
        return adj_ref[pl.ds(first, count)]

    for layer in reversed(range(depth)):
        reach = layer + 1

        def source(first, count, layer=layer):
            part = pl.ds(first, count)
            adjoints = before(layer, first, count)
            src_ref[part] = (adjoints * slope_ref[layer, part]).astype(bf16)

        row_blocks(halo - reach, halo + rows + reach, source)

        def back(first, count, layer=layer):
            adjoints = before(layer, first, count)
            moved = convolved_rows(wt_ref[layer], src_ref, first, count)
            for place in range(count):
                adj_ref[first + place] = adjoints[place] + moved[place]

        row_blocks(halo - layer, halo + rows + layer, back)
        sent_ref[layer] = src_ref[pl.ds(halo - 1, rows + 2), :, :cols]
    for row in range(rows):
        value = adj_ref[halo + row, :, :cols]
        g_ref[row] = value
        ref, place = piece_of((g_upper_ref, g_lower_ref), row, rows)
        ref[place] = value.astype(bf16)


def grad_body(kept_ref, sent_ref, grad_ref, *, channels, rows, depth):
    lanes = kept_ref.shape[3]
    cols = lanes // 2
    for layer in range(depth):
        columns = []
        for row in range(rows):
            a = kept_ref[layer, row].astype(f32)
            columns.append(
                jnp.concatenate(
                    [
                        pltpu.roll(a, 1, 1)[:, :cols],
                        a[:, :cols],
                        pltpu.roll(a, lanes - 1, 1)[:, :cols],
                    ],
                    0,
                ).astype(bf16)
            )
        sources = [
            sent_ref[layer, pl.ds(row, 3)].reshape(3 * channels, cols) for row in range(rows)
        ]
        grad = lax.dot_general(
            jnp.concatenate(sources, 1),
            jnp.concatenate(columns, 1),
            (((1,), (1,)), ((), ())),
            preferred_element_type=f32,
        )
        for tap in range(3):
            grad_ref[layer, :, pl.ds(tap * 3 * channels, 3 * channels)] = grad[
                (2 - tap) * channels : (3 - tap) * channels
            ]


def last_body(q_ref, half_ref, other_ref, *refs, channels, rows):
    arrived, (out_hbm, grad_hbm, out_ref, left_here) = refs[:-4], refs[-4:]
    half = half_ref.shape[0]
    odd = jnp.logical_not(even_row()).astype(jnp.int32)
    leaving = []
    for which, ref in enumerate((half_ref, other_ref)):
        low = half * (odd if which == 0 else 1 - odd)
        for layer in range(half):
            leaving.append(
                pltpu.make_async_copy(
                    ref.at[layer], grad_hbm.at[low + layer], left_here.at[len(leaving)]
                )
            )
    for copy in leaving:
        copy.start()
    last = lax.axis_index("layer") == lax.axis_size("layer") - 1
    for row in range(rows):
        value = arrived_row(arrived, row, rows)
        value = jnp.where(last, row_of(q_ref, row, channels, rows), value)
        out_ref[pl.ds(row, channels, stride=rows), :] = value
    parts = in_parts(out_ref, out_hbm, left_here, 2 * half)
    for copy in parts:
        copy.start()
    for copy in leaving + parts:
        copy.wait()


def shifted(array, axis, by):
    count = lax.axis_size(axis)
    pairs = [(i, i + by) for i in range(count) if 0 <= i + by < count]
    return lax.ppermute(array, axis, pairs)


def exchanged(to_pair, to_cross):
    rows = lax.axis_size("row")
    pairs = [(r, r ^ 1) for r in range(rows)]
    crossing = [(r, r + 1 if r % 2 else r - 1) for r in range(1, rows - 1)]
    return lax.ppermute(to_pair, "row", pairs), lax.ppermute(to_cross, "row", crossing)


def from_sides(array):
    if lax.axis_size("col") == 2:
        other = lax.ppermute(array, "col", [(0, 1), (1, 0)])
        return other, other
    return shifted(array, "col", 1), shifted(array, "col", -1)


def total_over_tiles(grads):
    rows, cols = lax.axis_size("row"), lax.axis_size("col")
    depth = grads.shape[0]
    half = depth // 2
    odd = lax.axis_index("row") % 2 == 1
    sent = jnp.where(odd, grads[:half], grads[half:])
    own = jnp.where(odd, grads[half:], grads[:half])
    pair = [(r, r ^ 1) for r in range(rows)]
    value = own + lax.ppermute(sent, "row", pair)

    flips = [(1 << bit, 0) for bit in range(1, rows.bit_length() - 1)]
    flips += [(0, 1 << bit) for bit in range(cols.bit_length() - 1)]
    for even, uneven in zip(flips[::-1], flips):
        pairs = []
        for r in range(rows):
            row_by, col_by = uneven if r % 2 else even
            pairs += [
                (r * cols + c, (r ^ row_by) * cols + (c ^ col_by)) for c in range(cols)
            ]
        rounded = value.astype(bf16)
        arrived = lax.ppermute(rounded, ("row", "col"), pairs)
        value = rounded.astype(f32) + arrived.astype(f32)
    return value, lax.ppermute(value, "row", pair)


def local(c_states, c_adjoints, weights):
    groups = lax.axis_size("layer")
    channels, rows, cols = c_states.shape[1:]
    depth = weights.shape[0]
    flat = (channels * rows, cols)
    c_flat, q_flat = c_states.reshape(flat), c_adjoints.reshape(flat)
    sizes = dict(channels=channels, rows=rows)
    tile_f = jax.ShapeDtypeStruct((rows, channels, cols), f32)

    strip_f = jax.ShapeDtypeStruct((channels, cols), f32)
    wide_b = jax.ShapeDtypeStruct((channels, 2 * cols), bf16)
    half = rows // 2
    more_f, more_b, upper_b, lower_b, message_b = (
        jax.ShapeDtypeStruct((count, channels, cols), kind)
        for count, kind in (
            (rows + 1, f32), (rows + 1, bf16), (half + 1, bf16), (half, bf16),
            (2 * depth + 2, bf16),
        )
    )
    flat_f = jax.ShapeDtypeStruct(flat, f32)
    edges = call(
        functools.partial(strip_body, depth=depth, **sizes),
        wide_b,
        [
            pltpu.VMEM(flat, f32),
            pltpu.VMEM(flat, f32),
            pltpu.SemaphoreType.DMA((2 * PARTS,)),
        ],
        vmem=STRIP_VMEM_BYTES,
        in_specs=[AWAY, AWAY],
        out_specs=HERE,
    )(c_flat, q_flat)
    left, right = from_sides(edges)
    to_pair, to_cross, side = call(
        functools.partial(message_body, depth=depth, **sizes),
        (message_b, message_b, wide_b),
    )(c_flat, q_flat, left, right)
    pair, cross = exchanged(to_pair, to_cross)
    strip = call(
        functools.partial(halo_strip_body, rows=rows, depth=depth), strip_f, flops=10**9
    )(side)

    taps = weights.reshape(depth, channels, 3, 3, channels)
    w_fwd = jnp.transpose(taps, (0, 3, 1, 2, 4)).reshape(depth, 3 * channels, 3 * channels)
    later_taps, _ = lax.optimization_barrier((taps, to_pair))
    w_back = jnp.transpose(later_taps[:, :, ::-1, ::-1, :], (0, 3, 4, 2, 1)).reshape(
        depth, 3 * channels, 3 * channels
    )
    w_fwd, w_back = lax.optimization_barrier((w_fwd, w_back))
    coarse = step_size * jnp.sum(weights[0].astype(f32).reshape(channels, 9, channels), axis=1)
    high = coarse.astype(bf16)
    low = (coarse - high.astype(f32)).astype(bf16)
    m_fwd = jnp.concatenate([high, low, high], 1)
    m_back = jnp.concatenate([high.T, low.T, high.T], 1)

    lanes = 2 * cols
    mac = 2 * 9 * channels * channels * lanes
    total = rows + 2 * depth

    def first(kind, sender, *inputs):
        return call(
            functools.partial(first_body, depth=depth, sender=sender, **sizes),
            kind,
            [
                pltpu.VMEM((total, channels, lanes), f32),
                pltpu.VMEM((total, channels, lanes), bf16),
                pltpu.VMEM((total, channels, lanes), bf16),
            ],
            flops=mac * 44,
        )(*inputs)

    def chain(pieces, target, matrix, order):
        sendings = [piece[0] for piece in pieces]
        arrivals = []
        for turn, step in enumerate(order):
            arrived = [lax.ppermute(sending, "layer", [step]) for sending in sendings]
            arrivals += arrived
            if turn < len(order) - 1:
                sendings = [
                    call(
                        functools.partial(hop_body, start=start, **sizes),
                        jax.ShapeDtypeStruct(value.shape, bf16),
                        flops=10**10,
                    )(value, *base, target, matrix)
                    for value, (_, start, base) in zip(arrived, pieces)
                ]
        return arrivals

    inputs = (c_flat, pair, cross, side, w_fwd)
    upper, lower = first((upper_b, lower_b), True, *inputs)
    inputs = lax.optimization_barrier((inputs, upper))[0]
    (f,) = first((more_f,), False, *inputs)
    arrivals = chain(
        ((upper, 0, (c_flat, strip)), (lower, half, (c_flat,))),
        f,
        m_fwd,
        [(k, k + 1) for k in range(groups - 1)],
    )
    s = call(functools.partial(settle_body, **sizes), more_b)(c_flat, strip, *arrivals)
    s_pair, s_cross = exchanged(s, s)

    total = rows + 4 * depth
    held, _ = lax.optimization_barrier(((c_flat, q_flat), s))
    state, ready = call(
        functools.partial(prepare_body, depth=depth, **sizes),
        (flat_f, jax.ShapeDtypeStruct((rows + 2 * depth, channels, lanes), f32)),
        [pltpu.VMEM(flat, f32), pltpu.SemaphoreType.DMA((PARTS,))],
        flops=2 * 10**9,
        out_specs=(AWAY, HERE),
    )(*held, s, pair, cross, side)
    g, upper, lower, kept, sources = call(
        functools.partial(second_body, depth=depth, **sizes),
        (
            tile_f,
            lower_b,
            lower_b,
            jax.ShapeDtypeStruct((depth, rows, channels, lanes), bf16),
            jax.ShapeDtypeStruct((depth, rows + 2, channels, cols), bf16),
        ),
        [
            pltpu.VMEM((total, channels, lanes), f32),
            pltpu.VMEM((total, channels, lanes), bf16),
            pltpu.VMEM((total, channels, lanes), bf16),
            pltpu.VMEM((depth, total, channels, lanes), f32),
            pltpu.VMEM((total, channels, lanes), f32),
            pltpu.VMEM((total, channels, lanes), bf16),
        ],
        flops=mac * 120,
    )(c_flat, s, s_pair, s_cross, ready, w_fwd, w_back)
    returned = chain(
        ((upper, 0, (q_flat,)), (lower, half, (q_flat,))),
        g,
        m_back,
        [(k, k - 1) for k in range(groups - 1, 0, -1)],
    )
    grads = call(
        functools.partial(grad_body, depth=depth, **sizes),
        jax.ShapeDtypeStruct((depth, channels, 9 * channels), f32),
        flops=10**9,
    )(kept, sources)
    own_half, other_half = total_over_tiles(grads)
    adjoint, weight_grads = call(
        functools.partial(last_body, **sizes),
        (flat_f, jax.ShapeDtypeStruct((depth, channels, 9 * channels), f32)),
        [pltpu.VMEM(flat, f32), pltpu.SemaphoreType.DMA((depth + PARTS,))],
        flops=10**10,
        out_specs=(AWAY, AWAY),
    )(q_flat, own_half, other_half, *returned)
    return state.reshape(c_states.shape), adjoint.reshape(c_states.shape), weight_grads


def solution(mesh):
    placed = (
        P("layer", None, "row", "col"),
        P("layer", None, "row", "col"),
        P("layer", None, None),
    )
    return jax.shard_map(
        local, mesh=mesh, in_specs=placed, out_specs=placed, check_vma=False
    )
```

```python
import functools

import jax
import jax.numpy as jnp
from jax import lax
from jax.experimental import pallas as pl
from jax.experimental.pallas import tpu as pltpu
from jax.sharding import PartitionSpec as P

step_size = 0.2
VMEM_BYTES = 40 * 1024 * 1024
STRIP_VMEM_BYTES = 63 * 1024 * 1024
PARTS = 4
f32 = jnp.float32
bf16 = jnp.bfloat16
HERE = pl.BlockSpec(memory_space=pltpu.VMEM)
AWAY = pl.BlockSpec(memory_space=pltpu.HBM)


def call(body, out_shape, scratch=(), flops=0, vmem=VMEM_BYTES, **more):
    return pl.pallas_call(
        body,
        out_shape=out_shape,
        scratch_shapes=list(scratch),
        cost_estimate=pl.CostEstimate(
            flops=int(flops), bytes_accessed=0, transcendentals=0
        ),
        compiler_params=pltpu.CompilerParams(vmem_limit_bytes=vmem),
        **more,
    )


def in_parts(source, target, arrived, first):
    size = source.shape[0] // PARTS
    return [
        pltpu.make_async_copy(
            source.at[pl.ds(part * size, size)],
            target.at[pl.ds(part * size, size)],
            arrived.at[first + part],
        )
        for part in range(PARTS)
    ]


def piece_of(parts, row, rows):
    half = rows // 2
    if len(parts) == 1 or row < half:
        return parts[0], row
    return (parts[1], row - half) if row < rows else (parts[0], half)


def row_of(ref, row, channels, rows):
    return ref[pl.ds(row, channels, stride=rows), :]


def lanes_of(shape):
    return lax.broadcasted_iota(jnp.int32, shape, 1)


def slots(shape, low, width, count):
    return (lanes_of(shape) - low + width * count) // width - count


def fold_edges(rows_list, edge, low, total):
    doubled = total.shape[1] > rows_list[0].shape[1]
    cols = rows_list[0].shape[1]
    slot = slots(total.shape, low, 2 * edge, len(rows_list))
    for place, row in enumerate(rows_list):
        wide = jnp.concatenate([row, row], 1) if doubled else row
        turned = pltpu.roll(wide, (low + 2 * edge * place + edge - cols) % wide.shape[1], 1)
        total = jnp.where(slot == place, turned, total)
    return total


def join_edges(from_left, from_right, left, right, edges):
    lanes = lanes_of(from_left.shape)
    far = jnp.zeros(lanes.shape, jnp.bool_)
    for edge, low, high in edges:
        inside = (lanes >= low) & (lanes < high)
        far = far | (inside & ((lanes - low) % (2 * edge) >= edge))
    return jnp.where(far, from_right.astype(f32) * right, from_left.astype(f32) * left)


def side_lanes(joined, edge, low, place):
    lanes = joined.shape[1]
    turned = pltpu.roll(joined, (2 * lanes - (low + 2 * edge * place + edge)) % lanes, 1)
    if lanes == 128:
        return turned
    front, back = turned[:, :128], turned[:, lanes - 128 :]
    return jnp.where(lanes_of(front.shape) < 64, front, back)


def convolved(weights, slab):
    channels = slab.shape[1]
    lanes = slab.shape[2]
    product = jnp.dot(
        weights, slab.reshape(3 * channels, lanes), preferred_element_type=f32
    )
    return (
        pltpu.roll(product[:channels], 1, 1)
        + product[channels : 2 * channels]
        + pltpu.roll(product[2 * channels :], lanes - 1, 1)
    )


def flags():
    row, col = lax.axis_index("row"), lax.axis_index("col")
    up = (row > 0).astype(f32)
    down = (row < lax.axis_size("row") - 1).astype(f32)
    left = (col > 0).astype(f32)
    right = (col < lax.axis_size("col") - 1).astype(f32)
    return up, down, left, right


def even_row():
    return lax.axis_index("row") % 2 == 0


def lane_mask(cols, left, right):
    lanes = lax.broadcasted_iota(jnp.int32, (1, 2 * cols), 1)
    return jnp.where(lanes < cols, 1.0, jnp.where(lanes < cols + cols // 2, right, left))


def layout(rows, depth):
    state_edge, adjoint_edge = 3 * depth, depth
    return (state_edge, 0), (adjoint_edge, 2 * state_edge * rows)


def strip_body(c_hbm, q_hbm, edge_ref, c_ref, q_ref, arrived, *, channels, rows, depth):
    copies = in_parts(c_hbm, c_ref, arrived, 0) + in_parts(q_hbm, q_ref, arrived, PARTS)
    for copy in copies:
        copy.start()
    for copy in copies:
        copy.wait()
    total = jnp.zeros(edge_ref.shape, f32)
    for ref, (edge, low) in zip((c_ref, q_ref), layout(rows, depth)):
        image = [row_of(ref, row, channels, rows) for row in range(rows)]
        total = fold_edges(image, edge, low, total)
    edge_ref[...] = total.astype(bf16)


def message_body(
    c_ref, q_ref, left_ref, right_ref, pair_ref, cross_ref, side_ref, strip_ref,
    *, channels, rows, depth,
):
    cols = c_ref.shape[1]
    _, _, left, right = flags()
    (c_edge, _), (q_edge, middle) = layout(rows, depth)
    edges = ((c_edge, 0, middle), (q_edge, middle, 2 * cols))
    side = join_edges(left_ref[...], right_ref[...], left, right, edges).astype(bf16)
    side_ref[...] = side
    wide = side.astype(f32)
    image = [side_lanes(wide, c_edge, 0, row) for row in range(rows)]
    strip_ref[...] = fold_edges(image, 2 * depth, 0, jnp.zeros(strip_ref.shape, f32))
    even = even_row()
    for which, ref in enumerate((c_ref, q_ref)):
        for row in range(depth):
            place = which * depth + row
            top = row_of(ref, row, channels, rows)
            bottom = row_of(ref, rows - depth + row, channels, rows)
            pair_ref[place] = jnp.where(even, bottom, top).astype(bf16)
            cross_ref[place] = jnp.where(even, top, bottom).astype(bf16)
    for half in range(2):
        part = side[:, half * cols : (half + 1) * cols]
        pair_ref[2 * depth + half] = part
        cross_ref[2 * depth + half] = part


class Beside:
    def __init__(self, pair_ref, cross_ref):
        self.pair, self.cross, self.even = pair_ref, cross_ref, even_row()

    def above(self, place):
        return jnp.where(
            self.even, self.cross[place].astype(f32), self.pair[place].astype(f32)
        )

    def below(self, place):
        return jnp.where(
            self.even, self.pair[place].astype(f32), self.cross[place].astype(f32)
        )


def strips_of(get, depth):
    return jnp.concatenate([get(2 * depth), get(2 * depth + 1)], 1)


def row_blocks(low, high, body):
    body(low, high - low)


def convolved_rows(weights, ref, first, count):
    slab = ref[pl.ds(first - 1, count + 2)]
    return [convolved(weights, slab[place : place + 3]) for place in range(count)]


def row_flag(index, halo, rows, up, down):
    if index < halo:
        return up
    return down if index >= halo + rows else 1.0


def first_body(
    c_ref, pair_ref, cross_ref, side_ref, w_ref, *refs, channels, rows, depth, sender
):
    outs = refs[:-3]
    active = (lax.axis_index("layer") == 0) == sender

    @pl.when(jnp.logical_not(active))
    def nothing():
        for out_ref in outs:
            out_ref[...] = jnp.zeros(out_ref.shape, out_ref.dtype)

    @pl.when(active)
    def run():
        first_pass(
            c_ref, pair_ref, cross_ref, side_ref, w_ref, outs, *refs[-3:],
            channels, rows, depth,
        )


def first_pass(
    c_ref, pair_ref, cross_ref, side_ref, w_ref, outs, x_ref, a_ref, a2_ref,
    channels, rows, depth,
):
    cols = c_ref.shape[1]
    up, down, left, right = flags()
    mask = lane_mask(cols, left, right)
    halo = depth

    def put(index, own, beyond):
        x_ref[index, :, :cols] = own
        x_ref[index, :, cols:] = beyond
        a_ref[index, :, :cols] = own.astype(bf16)
        a_ref[index, :, cols:] = beyond.astype(bf16)

    (edge, low), _ = layout(rows, depth)
    own_side = side_ref[...].astype(f32)
    for row in range(rows):
        own = row_of(c_ref, row, channels, rows)
        put(halo + row, own, side_lanes(own_side, edge, low, row))
    beside = Beside(pair_ref, cross_ref)
    above_side, below_side = strips_of(beside.above, depth), strips_of(beside.below, depth)
    for row in range(depth):
        place = rows - depth + row
        put(row, beside.above(row), side_lanes(above_side, edge, low, place))
        put(halo + rows + row, beside.below(row), side_lanes(below_side, edge, low, row))

    total = rows + 2 * halo
    for layer in range(depth):
        now, later = (a_ref, a2_ref) if layer % 2 == 0 else (a2_ref, a_ref)

        def step(first, count, layer=layer, now=now, later=later):
            states = x_ref[pl.ds(first, count)]
            done = []
            for place, z in enumerate(convolved_rows(w_ref[layer], now, first, count)):
                gain = mask * (step_size * row_flag(first + place, halo, rows, up, down))
                done.append(states[place] + gain * jnp.tanh(z))
            for place, x in enumerate(done):
                x_ref[first + place] = x
                if layer < depth - 1:
                    later[first + place] = x.astype(bf16)

        row_blocks(layer + 1, total - layer - 1, step)
    image = [x_ref[halo + row, :, cols:] for row in range(rows)]
    values = [x_ref[halo + row, :, :cols] for row in range(rows)]
    values.append(fold_edges(image, 2 * depth, 0, jnp.zeros((channels, cols), f32)))
    for row, value in enumerate(values):
        out_ref, place = piece_of(outs, row, rows)
        out_ref[place] = value.astype(out_ref.dtype)


def hop_body(s_ref, c_ref, *refs, start, channels, rows):
    f_ref, m_ref, out_ref = refs[-3:]
    work = [
        (row, row_of(c_ref, row, channels, rows)) for row in range(start, start + rows // 2)
    ]
    work += [(rows, ref[...]) for ref in refs[:-3]]
    for place, (row, base) in enumerate(work):
        e = s_ref[place].astype(f32) - base
        high = e.astype(bf16)
        low = (e - high.astype(f32)).astype(bf16)
        stacked = jnp.concatenate([high, high, low], 0)
        moved = jnp.dot(m_ref[...], stacked, preferred_element_type=f32)
        out_ref[place] = (f_ref[row] + e + moved).astype(bf16)


def arrived_row(refs, row, rows):
    value = 0.0
    for pieces in zip(refs[::2], refs[1::2]):
        ref, place = piece_of(pieces, row, rows)
        value = value + ref[place].astype(f32)
    return value


def settle_body(c_ref, strip_ref, *refs, channels, rows):
    arrived, s_ref = refs[:-1], refs[-1]
    first = lax.axis_index("layer") == 0
    base = [row_of(c_ref, row, channels, rows) for row in range(rows)] + [strip_ref[...]]
    for row in range(rows + 1):
        value = arrived_row(arrived, row, rows)
        s_ref[row] = jnp.where(first, base[row], value).astype(bf16)


def prepare_body(
    c_ref, q_ref, s_ref, pair_ref, cross_ref, side_ref, state_hbm, adj_ref,
    state_ref, left_here, *, channels, rows, depth,
):
    cols = c_ref.shape[1]
    first = lax.axis_index("layer") == 0
    for row in range(rows):
        own = jnp.where(first, row_of(c_ref, row, channels, rows), s_ref[row].astype(f32))
        state_ref[pl.ds(row, channels, stride=rows), :] = own
    leaving = in_parts(state_ref, state_hbm, left_here, 0)
    for copy in leaving:
        copy.start()

    def put_adj(index, own, beyond):
        adj_ref[index, :, :cols] = own
        adj_ref[index, :, cols:] = beyond

    _, (edge, low) = layout(rows, depth)
    own_side = side_ref[...].astype(f32)
    beside = Beside(pair_ref, cross_ref)
    above_side, below_side = strips_of(beside.above, depth), strips_of(beside.below, depth)
    for row in range(rows):
        put_adj(
            depth + row, row_of(q_ref, row, channels, rows), side_lanes(own_side, edge, low, row)
        )
    for row in range(depth):
        place = rows - depth + row
        put_adj(
            row,
            beside.above(depth + row),
            side_lanes(above_side, edge, low, place),
        )
        put_adj(
            depth + rows + row,
            beside.below(depth + row),
            side_lanes(below_side, edge, low, row),
        )
    for copy in leaving:
        copy.wait()


def second_body(
    c_ref, s_ref, s_pair_ref, s_cross_ref, ready_ref, w_ref, wt_ref,
    g_ref, g_upper_ref, g_lower_ref, kept_ref, sent_ref,
    x_ref, a_ref, a2_ref, slope_ref, adj_ref, src_ref,
    *, channels, rows, depth,
):
    cols = c_ref.shape[1]
    up, down, left, right = flags()
    mask = lane_mask(cols, left, right)
    halo = 2 * depth
    total = rows + 2 * halo
    first = lax.axis_index("layer") == 0

    def put(index, own, beyond):
        x_ref[index, :, :cols] = own
        x_ref[index, :, cols:] = beyond
        a_ref[index, :, :cols] = own.astype(bf16)
        a_ref[index, :, cols:] = beyond.astype(bf16)

    edge = 2 * depth

    beside = Beside(s_pair_ref, s_cross_ref)
    own_side = s_ref[rows].astype(f32)
    above_side, below_side = beside.above(rows), beside.below(rows)
    for row in range(rows):
        own = jnp.where(first, row_of(c_ref, row, channels, rows), s_ref[row].astype(f32))
        put(halo + row, own, side_lanes(own_side, edge, 0, row))
    for row in range(halo):
        place = rows - halo + row
        put(
            row,
            beside.above(place),
            side_lanes(above_side, edge, 0, place),
        )
        put(
            halo + rows + row,
            beside.below(row),
            side_lanes(below_side, edge, 0, row),
        )

    for layer in range(depth):
        now, later = (a_ref, a2_ref) if layer % 2 == 0 else (a2_ref, a_ref)
        kept_ref[layer] = now[pl.ds(halo, rows)]

        def step(first, count, layer=layer, now=now, later=later):
            states = x_ref[pl.ds(first, count)]
            done = []
            for place, z in enumerate(convolved_rows(w_ref[layer], now, first, count)):
                gain = mask * (step_size * row_flag(first + place, halo, rows, up, down))
                t = jnp.tanh(z)
                moved = gain * t
                done.append((gain - moved * t, states[place] + moved))
            for place, (slope, x) in enumerate(done):
                slope_ref[layer, first + place] = slope
                if layer < depth - 1:
                    x_ref[first + place] = x
                    later[first + place] = x.astype(bf16)

        row_blocks(layer + 1, total - layer - 1, step)

    def before(layer, first, count):
        if layer == depth - 1:
            return ready_ref[pl.ds(first - (halo - depth), count)]
        return adj_ref[pl.ds(first, count)]

    for layer in reversed(range(depth)):
        reach = layer + 1

        def source(first, count, layer=layer):
            part = pl.ds(first, count)
            adjoints = before(layer, first, count)
            src_ref[part] = (adjoints * slope_ref[layer, part]).astype(bf16)

        row_blocks(halo - reach, halo + rows + reach, source)

        def back(first, count, layer=layer):
            adjoints = before(layer, first, count)
            moved = convolved_rows(wt_ref[layer], src_ref, first, count)
            for place in range(count):
                adj_ref[first + place] = adjoints[place] + moved[place]

        row_blocks(halo - layer, halo + rows + layer, back)
        sent_ref[layer] = src_ref[pl.ds(halo - 1, rows + 2), :, :cols]
    for row in range(rows):
        value = adj_ref[halo + row, :, :cols]
        g_ref[row] = value
        ref, place = piece_of((g_upper_ref, g_lower_ref), row, rows)
        ref[place] = value.astype(bf16)


def grad_body(kept_ref, sent_ref, grad_ref, *, channels, rows, depth):
    lanes = kept_ref.shape[3]
    cols = lanes // 2
    for layer in range(depth):
        columns = []
        for row in range(rows):
            a = kept_ref[layer, row].astype(f32)
            columns.append(
                jnp.concatenate(
                    [
                        pltpu.roll(a, 1, 1)[:, :cols],
                        a[:, :cols],
                        pltpu.roll(a, lanes - 1, 1)[:, :cols],
                    ],
                    0,
                ).astype(bf16)
            )
        sources = [
            sent_ref[layer, pl.ds(row, 3)].reshape(3 * channels, cols) for row in range(rows)
        ]
        grad = lax.dot_general(
            jnp.concatenate(sources, 1),
            jnp.concatenate(columns, 1),
            (((1,), (1,)), ((), ())),
            preferred_element_type=f32,
        )
        for tap in range(3):
            grad_ref[layer, :, pl.ds(tap * 3 * channels, 3 * channels)] = grad[
                (2 - tap) * channels : (3 - tap) * channels
            ]


def last_body(q_ref, half_ref, other_ref, *refs, channels, rows):
    arrived, (out_hbm, grad_hbm, out_ref, left_here) = refs[:-4], refs[-4:]
    half = half_ref.shape[0]
    odd = jnp.logical_not(even_row()).astype(jnp.int32)
    leaving = []
    for which, ref in enumerate((half_ref, other_ref)):
        low = half * (odd if which == 0 else 1 - odd)
        for layer in range(half):
            leaving.append(
                pltpu.make_async_copy(
                    ref.at[layer], grad_hbm.at[low + layer], left_here.at[len(leaving)]
                )
            )
    for copy in leaving:
        copy.start()
    last = lax.axis_index("layer") == lax.axis_size("layer") - 1
    for row in range(rows):
        value = arrived_row(arrived, row, rows)
        value = jnp.where(last, row_of(q_ref, row, channels, rows), value)
        out_ref[pl.ds(row, channels, stride=rows), :] = value
    parts = in_parts(out_ref, out_hbm, left_here, 2 * half)
    for copy in parts:
        copy.start()
    for copy in leaving + parts:
        copy.wait()


def shifted(array, axis, by):
    count = lax.axis_size(axis)
    pairs = [(i, i + by) for i in range(count) if 0 <= i + by < count]
    return lax.ppermute(array, axis, pairs)


def exchanged(to_pair, to_cross):
    rows = lax.axis_size("row")
    pairs = [(r, r ^ 1) for r in range(rows)]
    crossing = [(r, r + 1 if r % 2 else r - 1) for r in range(1, rows - 1)]
    return lax.ppermute(to_pair, "row", pairs), lax.ppermute(to_cross, "row", crossing)


def from_sides(array):
    if lax.axis_size("col") == 2:
        other = lax.ppermute(array, "col", [(0, 1), (1, 0)])
        return other, other
    return shifted(array, "col", 1), shifted(array, "col", -1)


def total_over_tiles(grads):
    rows, cols = lax.axis_size("row"), lax.axis_size("col")
    depth = grads.shape[0]
    half = depth // 2
    odd = lax.axis_index("row") % 2 == 1
    sent = jnp.where(odd, grads[:half], grads[half:])
    own = jnp.where(odd, grads[half:], grads[:half])
    pair = [(r, r ^ 1) for r in range(rows)]
    value = own + lax.ppermute(sent, "row", pair)

    flips = [(1 << bit, 0) for bit in range(1, rows.bit_length() - 1)]
    flips += [(0, 1 << bit) for bit in range(cols.bit_length() - 1)]
    for even, uneven in zip(flips[::-1], flips):
        pairs = []
        for r in range(rows):
            row_by, col_by = uneven if r % 2 else even
            pairs += [
                (r * cols + c, (r ^ row_by) * cols + (c ^ col_by)) for c in range(cols)
            ]
        rounded = value.astype(bf16)
        arrived = lax.ppermute(rounded, ("row", "col"), pairs)
        value = rounded.astype(f32) + arrived.astype(f32)
    return value, lax.ppermute(value, "row", pair)


def local(c_states, c_adjoints, weights):
    groups = lax.axis_size("layer")
    channels, rows, cols = c_states.shape[1:]
    depth = weights.shape[0]
    flat = (channels * rows, cols)
    c_flat, q_flat = c_states.reshape(flat), c_adjoints.reshape(flat)
    sizes = dict(channels=channels, rows=rows)
    tile_f = jax.ShapeDtypeStruct((rows, channels, cols), f32)

    strip_f = jax.ShapeDtypeStruct((channels, cols), f32)
    wide_b = jax.ShapeDtypeStruct((channels, 2 * cols), bf16)
    half = rows // 2
    more_f, more_b, upper_b, lower_b, message_b = (
        jax.ShapeDtypeStruct((count, channels, cols), kind)
        for count, kind in (
            (rows + 1, f32), (rows + 1, bf16), (half + 1, bf16), (half, bf16),
            (2 * depth + 2, bf16),
        )
    )
    flat_f = jax.ShapeDtypeStruct(flat, f32)
    edges = call(
        functools.partial(strip_body, depth=depth, **sizes),
        wide_b,
        [
            pltpu.VMEM(flat, f32),
            pltpu.VMEM(flat, f32),
            pltpu.SemaphoreType.DMA((2 * PARTS,)),
        ],
        vmem=STRIP_VMEM_BYTES,
        in_specs=[AWAY, AWAY],
        out_specs=HERE,
    )(c_flat, q_flat)
    left, right = from_sides(edges)
    to_pair, to_cross, side, strip = call(
        functools.partial(message_body, depth=depth, **sizes),
        (message_b, message_b, wide_b, strip_f),
    )(c_flat, q_flat, left, right)
    pair, cross = exchanged(to_pair, to_cross)

    taps = weights.reshape(depth, channels, 3, 3, channels)
    w_fwd = jnp.transpose(taps, (0, 3, 1, 2, 4)).reshape(depth, 3 * channels, 3 * channels)
    later_taps, _ = lax.optimization_barrier((taps, to_pair))
    w_back = jnp.transpose(later_taps[:, :, ::-1, ::-1, :], (0, 3, 4, 2, 1)).reshape(
        depth, 3 * channels, 3 * channels
    )
    w_fwd, w_back = lax.optimization_barrier((w_fwd, w_back))
    coarse = step_size * jnp.sum(weights[0].astype(f32).reshape(channels, 9, channels), axis=1)
    high = coarse.astype(bf16)
    low = (coarse - high.astype(f32)).astype(bf16)
    m_fwd = jnp.concatenate([high, low, high], 1)
    m_back = jnp.concatenate([high.T, low.T, high.T], 1)

    lanes = 2 * cols
    mac = 2 * 9 * channels * channels * lanes
    total = rows + 2 * depth

    def first(kind, sender, *inputs):
        return call(
            functools.partial(first_body, depth=depth, sender=sender, **sizes),
            kind,
            [
                pltpu.VMEM((total, channels, lanes), f32),
                pltpu.VMEM((total, channels, lanes), bf16),
                pltpu.VMEM((total, channels, lanes), bf16),
            ],
            flops=mac * 44,
        )(*inputs)

    def chain(pieces, target, matrix, order, in_turn):
        sendings = [piece[0] for piece in pieces]
        arrivals = []
        for turn, step in enumerate(order):
            arrived = [lax.ppermute(sending, "layer", [step]) for sending in sendings]
            arrivals += arrived
            if turn < len(order) - 1:
                sendings = []
                for value, (_, start, base) in zip(arrived, pieces):
                    if in_turn and sendings:
                        value = lax.optimization_barrier((value, sendings[0]))[0]
                    size = len(base) - 1 + half
                    sendings.append(
                        call(
                            functools.partial(hop_body, start=start, **sizes),
                            jax.ShapeDtypeStruct((size, channels, cols), bf16),
                            flops=10**10,
                        )(value, *base, target, matrix)
                    )
        return arrivals

    inputs = (c_flat, pair, cross, side, w_fwd)
    upper, lower = first((upper_b, lower_b), True, *inputs)
    inputs = lax.optimization_barrier((inputs, upper))[0]
    (f,) = first((more_f,), False, *inputs)
    arrivals = chain(
        ((upper, 0, (c_flat, strip)), (lower, half, (c_flat,))),
        f,
        m_fwd,
        [(k, k + 1) for k in range(groups - 1)],
        True,
    )
    s = call(functools.partial(settle_body, **sizes), more_b)(c_flat, strip, *arrivals)
    s_pair, s_cross = exchanged(s, s)

    total = rows + 4 * depth
    held, _ = lax.optimization_barrier(((c_flat, q_flat), s))
    state, ready = call(
        functools.partial(prepare_body, depth=depth, **sizes),
        (flat_f, jax.ShapeDtypeStruct((rows + 2 * depth, channels, lanes), f32)),
        [pltpu.VMEM(flat, f32), pltpu.SemaphoreType.DMA((PARTS,))],
        flops=2 * 10**9,
        out_specs=(AWAY, HERE),
    )(*held, s, pair, cross, side)
    g, upper, lower, kept, sources = call(
        functools.partial(second_body, depth=depth, **sizes),
        (
            tile_f,
            lower_b,
            lower_b,
            jax.ShapeDtypeStruct((depth, rows, channels, lanes), bf16),
            jax.ShapeDtypeStruct((depth, rows + 2, channels, cols), bf16),
        ),
        [
            pltpu.VMEM((total, channels, lanes), f32),
            pltpu.VMEM((total, channels, lanes), bf16),
            pltpu.VMEM((total, channels, lanes), bf16),
            pltpu.VMEM((depth, total, channels, lanes), f32),
            pltpu.VMEM((total, channels, lanes), f32),
            pltpu.VMEM((total, channels, lanes), bf16),
        ],
        flops=mac * 120,
    )(c_flat, s, s_pair, s_cross, ready, w_fwd, w_back)
    returned = chain(
        ((upper, 0, (q_flat,)), (lower, half, (q_flat,))),
        g,
        m_back,
        [(k, k - 1) for k in range(groups - 1, 0, -1)],
        False,
    )
    grads = call(
        functools.partial(grad_body, depth=depth, **sizes),
        jax.ShapeDtypeStruct((depth, channels, 9 * channels), f32),
        flops=10**9,
    )(kept, sources)
    own_half, other_half = total_over_tiles(grads)
    adjoint, weight_grads = call(
        functools.partial(last_body, **sizes),
        (flat_f, jax.ShapeDtypeStruct((depth, channels, 9 * channels), f32)),
        [pltpu.VMEM(flat, f32), pltpu.SemaphoreType.DMA((depth + PARTS,))],
        flops=10**10,
        out_specs=(AWAY, AWAY),
    )(q_flat, own_half, other_half, *returned)
    return state.reshape(c_states.shape), adjoint.reshape(c_states.shape), weight_grads


def solution(mesh):
    placed = (
        P("layer", None, "row", "col"),
        P("layer", None, "row", "col"),
        P("layer", None, None),
    )
    return jax.shard_map(
        local, mesh=mesh, in_specs=placed, out_specs=placed, check_vma=False
    )
```
